128 devices in a mesh: fsdp: 16 (over z, x), head: 8 (over y, core).
Axes of the slice: x: 4, y: 4, z: 4, core: 2. Of those that a mesh axis runs over, the one named last changes fastest.
Arguments:
- grad_parts: bfloat16 [8, 2048, 8192], P('head', 'fsdp'), may hold values from -6 to 6
- params: float32 [2048, 8192], P('fsdp', 'head'), may hold values from -1 to 1
- moment_one: float32 [2048, 8192], P('fsdp', 'head'), may hold values from -3 to 3
- moment_two: float32 [2048, 8192], P('fsdp', 'head'), may hold values from 0.0001 to 0.01
- query_latent: bfloat16 [8, 128, 1536], P(None, 'fsdp'), may hold values from -6 to 6
- rope_weight: bfloat16 [1536, 4096], P(None, 'head'), may hold values from -0.15625 to 0.15625
- value_weight: bfloat16 [512, 8192], P(None, 'head'), may hold values from -0.25 to 0.25
- out_weight: bfloat16 [8192, 7168], P('head', 'fsdp'), may hold values from -0.0625 to 0.0625
- latent_cache: bfloat16 [128, 8192, 512], P('fsdp'), may hold values from -6 to 6
- rope_cache: bfloat16 [128, 64, 8192], P('fsdp'), may hold values from -6 to 6
- new_latent: bfloat16 [8, 128, 512], P(None, 'fsdp'), may hold values from -6 to 6
- new_rope: bfloat16 [8, 128, 64], P(None, 'fsdp'), may hold values from -6 to 6
- lengths: int32 [128], P('fsdp'), may hold values from 1 to 8192, as said below
Outputs:
- new_params: float32 [2048, 8192], P('fsdp', 'head')
- new_one: float32 [2048, 8192], P('fsdp', 'head')
- new_two: float32 [2048, 8192], P('fsdp', 'head')
- decoded: bfloat16 [8, 128, 7168], P(None, 'fsdp')
The draws below stay inside these ranges and needn't reach their ends.
Inputs may be any that keep to these rules, and one draw needn't show every extreme that they name: `lengths`: some sequence has exactly 8192 filled slots.
All inputs are finite; a program needn't handle non-finite values.
Results may differ from the reference program's by a relative error of at most 0.02.
Values may be sent and summed in bfloat16 or wider, within the bound.
No kernel may reach another device: no remote copies, remote signals or barrier semaphores. Data moves between devices by JAX's collectives and lax.ppermute only.
A program may use at most 256 MiB of HBM per device.

```python
import math
import jax
import jax.numpy as jnp
from jax import lax

D = 7168
HEADS = 64
HDIM = 128
ROPE = 64
KV = 512
QR = 1536
STEPS = 8
CACHE = 8192
SEQS = 128
REPLICAS = 8
ROWS = 2048
COLS = 8192


def cache_lengths(key):
    key = jax.random.fold_in(key, 7)
    drawn = jax.random.randint(key, (SEQS,), 1, CACHE + 1, dtype=jnp.int32)
    return drawn.at[0].set(CACHE)


def draw_lengths(key, part):
    return cache_lengths(key)


def draw_params(key, part):
    key = jax.random.fold_in(key, 11)
    drawn = jnp.clip(jax.random.normal(key, (QR + KV, HEADS * HDIM), jnp.float32), -6.0, 6.0) / math.sqrt(QR)
    return drawn


def draw_query_latent(key, part):
    key = jax.random.fold_in(key, 13)
    drawn = jnp.clip(jax.random.normal(key, (STEPS, SEQS, QR), jnp.float32), -6.0, 6.0)
    return drawn.astype(jnp.bfloat16)


def draw_latent_cache(key, part):
    key = jax.random.fold_in(key, 17)
    drawn = jnp.clip(jax.random.normal(key, (SEQS, CACHE, KV), jnp.float32), -6.0, 6.0)
    return drawn.astype(jnp.bfloat16)


def block_levels(rng, dims, shards, low, largest):
    def one(dim, blocks):
        steps = jax.random.uniform(jax.random.fold_in(jax.random.fold_in(rng, 6), dim), (blocks,), jnp.float32, low / len(shards), largest / len(shards))
        return jnp.repeat(jnp.exp(steps), dims[dim] // blocks).reshape((-1,) + (1,) * (len(dims) - dim - 1))

    level = one(*shards[0])
    for cut in shards[1:]:
        level = level * one(*cut)
    return level


def scatter_about(key, extent, deviation, most, pieces=(), kind=jnp.bfloat16):
    level = block_levels(key, extent, pieces, -0.22, 0.18) if pieces else 1.0
    values = jax.random.normal(key, extent, jnp.float32) * deviation * level
    return jnp.minimum(jnp.maximum(values, -most), most).astype(kind)


def setup_inputs(seed: int = 0) -> dict:
    key_list = jax.random.split(jax.random.key(seed), 14)
    return {
        "grad_parts": scatter_about(key_list[0], (REPLICAS, ROWS, COLS), 1.0, 6.0, ((0, 8), (1, 16))),
        "params": draw_params(jax.random.fold_in(key_list[13], 71), 0),
        "moment_one": scatter_about(key_list[2], (ROWS, COLS), 0.3, 3.0, ((0, 16), (1, 8)), jnp.float32),
        "moment_two": jnp.clip(jnp.exp(math.log(0.01) - 4.6051702 * jax.random.uniform(key_list[3], (ROWS, COLS), jnp.float32) ** block_levels(key_list[3], (ROWS, COLS), ((0, 16), (1, 8)), -0.2, 0.2)), 0.0001, 0.01),
        "query_latent": draw_query_latent(jax.random.fold_in(key_list[13], 71), 0),
        "rope_weight": scatter_about(key_list[5], (QR, HEADS * ROPE), QR ** -0.5, 0.15625, ((1, 8),)),
        "value_weight": scatter_about(key_list[6], (KV, COLS), KV ** -0.5, 0.25, ((1, 8),)),
        "out_weight": scatter_about(key_list[7], (COLS, D), COLS ** -0.5, 0.0625, ((0, 8), (1, 16))),
        "latent_cache": draw_latent_cache(jax.random.fold_in(key_list[13], 71), 0),
        "rope_cache": scatter_about(key_list[9], (SEQS, ROPE, CACHE), 1.0, 6.0, ((0, 16),)),
        "new_latent": scatter_about(key_list[10], (STEPS, SEQS, KV), 1.0, 6.0, ((1, 16),)),
        "new_rope": scatter_about(key_list[11], (STEPS, SEQS, ROPE), 1.0, 6.0, ((1, 16),)),
        "lengths": draw_lengths(jax.random.fold_in(key_list[13], 71), 0),
    }


first_fix = 1.0 - math.exp(100.0 * math.log(0.9))
second_fix = 1.0 - math.exp(100.0 * math.log(0.999))

def rotate(vector, position):
    half = vector.shape[-1] // 2
    index_f = jnp.arange(half, dtype=jnp.float32)
    frequency = jnp.exp(-math.log(10000.0) * 2.0 * index_f / vector.shape[-1])
    angle = position[..., None] * frequency
    first = vector[..., :half]
    second = vector[..., half:]
    cosine = jnp.cos(angle)
    sine = jnp.sin(angle)
    return jnp.concatenate([first * cosine - second * sine, first * sine + second * cosine], axis=-1)

def adam_update(weights, first, second, grad):
    first = 0.9 * first + 0.1 * grad
    second = 0.999 * second + 0.001 * grad * grad
    step_size = 0.003 / first_fix
    denom = jnp.sqrt(second / second_fix) + 1e-08
    return (weights - step_size * first / denom, first, second)

def attend(items):
    query_lat, query_rope, latent, rotary, new_lat, new_rot, length = items
    steps_n = query_lat.shape[0]
    scale = 1.0 / math.sqrt(HDIM + ROPE)
    ql = query_lat.astype(jnp.float32)
    qr = query_rope.astype(jnp.float32)
    score_cache = (jnp.einsum('thk,jk->thj', ql, latent.astype(jnp.float32)) + jnp.einsum('thr,rj->thj', qr, rotary.astype(jnp.float32))) * scale
    score_new = (jnp.einsum('thk,uk->thu', ql, new_lat.astype(jnp.float32)) + jnp.einsum('thr,ur->thu', qr, new_rot.astype(jnp.float32))) * scale
    mask_cache = (jnp.arange(latent.shape[0], dtype=jnp.int32) < length)[None, None, :]
    mask_new = (jnp.arange(steps_n, dtype=jnp.int32)[None, :] <= jnp.arange(steps_n, dtype=jnp.int32)[:, None])[:, None, :]
    top = jnp.maximum(lax.optimization_barrier(jnp.max(jnp.where(mask_cache, score_cache, -1e+30), axis=-1)), lax.optimization_barrier(jnp.max(jnp.where(mask_new, score_new, -1e+30), axis=-1)))
    expo_cache = jnp.where(mask_cache, jnp.exp(score_cache - top[..., None]), 0.0)
    expo_new = jnp.where(mask_new, jnp.exp(score_new - top[..., None]), 0.0)
    total = lax.optimization_barrier(jnp.sum(expo_cache, axis=-1)) + lax.optimization_barrier(jnp.sum(expo_new, axis=-1))
    prob_cache = (expo_cache / total[..., None]).astype(jnp.bfloat16)
    prob_new = (expo_new / total[..., None]).astype(jnp.bfloat16)
    mixed = jnp.einsum('thj,jk->thk', prob_cache.astype(jnp.float32), latent.astype(jnp.float32)) + jnp.einsum('thu,uk->thk', prob_new.astype(jnp.float32), new_lat.astype(jnp.float32))
    return mixed.astype(jnp.bfloat16)

def reference(grad_parts, params, moment_one, moment_two, query_latent, rope_weight, value_weight, out_weight, latent_cache, rope_cache, new_latent, new_rope, lengths):
    grad = lax.optimization_barrier(jnp.sum(grad_parts.astype(jnp.float32), axis=0))
    new_params, new_one, new_two = adam_update(params, moment_one, moment_two, grad)
    weights = new_params.astype(jnp.bfloat16)
    up_query = weights[:QR].reshape(QR, HEADS, HDIM).astype(jnp.float32)
    up_key = weights[QR:].reshape(KV, HEADS, HDIM).astype(jnp.float32)
    latent_f = query_latent.astype(jnp.float32)
    query_nope = jnp.einsum('tsq,qhd->tshd', latent_f, up_query).astype(jnp.bfloat16)
    query_lat = jnp.einsum('tshd,khd->tshk', query_nope.astype(jnp.float32), up_key).astype(jnp.bfloat16)
    query_rope = jnp.einsum('tsq,qhr->tshr', latent_f, rope_weight.reshape(QR, HEADS, ROPE).astype(jnp.float32))
    position = (lengths[None, :] + jnp.arange(STEPS, dtype=jnp.int32)[:, None]).astype(jnp.float32)[:, :, None]
    query_rope = rotate(query_rope, position).astype(jnp.bfloat16)
    attended = lax.map(attend, (jnp.transpose(query_lat, (1, 0, 2, 3)), jnp.transpose(query_rope, (1, 0, 2, 3)), latent_cache, rope_cache, jnp.transpose(new_latent, (1, 0, 2)), jnp.transpose(new_rope, (1, 0, 2)), lengths))
    attended = jnp.transpose(attended, (1, 0, 2, 3))
    values = jnp.einsum('tshk,khd->tshd', attended.astype(jnp.float32), value_weight.reshape(KV, HEADS, HDIM).astype(jnp.float32)).astype(jnp.bfloat16)
    values = values.reshape(STEPS * SEQS, HEADS * HDIM)
    decoded = jnp.dot(values, out_weight, preferred_element_type=jnp.float32).astype(jnp.bfloat16)
    return (new_params, new_one, new_two, decoded.reshape(STEPS, SEQS, D))
```

```python
import functools
import itertools
import math

import jax
import jax.numpy as jnp
import numpy as np
from jax import lax
from jax.experimental import pallas as pl
from jax.experimental.pallas import tpu as pltpu
from jax.sharding import PartitionSpec as P

HDIM = 128
ROPE = 64
SIDE = 4
BLOCK = 1024
SLOTS = 12
MIB = 1024 * 1024

first_fix = 1.0 - math.exp(100.0 * math.log(0.9))
second_fix = 1.0 - math.exp(100.0 * math.log(0.999))
NEG = -1e30
LOG2E = math.log2(math.e)

NT = (((1,), (1,)), ((), ()))
NN = (((1,), (0,)), ((), ()))


def dot(a, b, dims):
    return lax.dot_general(a, b, dims, preferred_element_type=jnp.float32)


def moves(axis, direction):
    perm = []
    for z in range(SIDE):
        for x in range(SIDE):
            for y in range(SIDE):
                for c in range(2):
                    d = direction * (1 - 2 * c)
                    to = {"x": x, "y": y, "z": z}
                    to[axis] = (to[axis] + d) % SIDE
                    perm.append(
                        (
                            (z * SIDE + x) * 2 * SIDE + y * 2 + c,
                            (to["z"] * SIDE + to["x"]) * 2 * SIDE + to["y"] * 2 + c,
                        )
                    )
    return perm


def forth(v, axis):
    return lax.ppermute(v, ("fsdp", "head"), moves(axis, 1))


def back(v, axis):
    return lax.ppermute(v, ("fsdp", "head"), moves(axis, -1))


def other_core(v):
    return lax.ppermute(v, "head", [(i, i ^ 1) for i in range(2 * SIDE)])


def ring(own, axis):
    one = forth(own, axis)
    two = back(own, axis)
    return own, one, two, forth(one, axis)


def ring_sum(blocks, axis):
    near, far = blocks[1], forth(blocks[3], axis)
    two = back(blocks[2], axis)
    one = forth((near.astype(jnp.float32) + far.astype(jnp.float32)).astype(near.dtype), axis)
    return blocks[0], one, two


VMEM = pl.BlockSpec(memory_space=pltpu.VMEM)
SMEM = pl.BlockSpec(memory_space=pltpu.SMEM)
HBM = pl.BlockSpec(memory_space=pl.ANY)
F32 = jnp.float32
BF16 = jnp.bfloat16


def pack_body(idx_ref, g_ref, o_ref, buf, in_sem, out_sem):
    cols = buf.shape[2]

    def come(j):
        at = pl.multiple_of(idx_ref[j] * cols, 128)
        return pltpu.make_async_copy(g_ref.at[:, pl.ds(at, cols)], buf.at[j], in_sem.at[j])

    def go(j):
        return pltpu.make_async_copy(buf.at[j], o_ref.at[j], out_sem.at[j])

    for j in range(SIDE):
        come(j).start()
    for j in range(SIDE):
        come(j).wait()
        go(j).start()
    for j in range(SIDE):
        go(j).wait()


def pack(idx, g):
    shape = (SIDE, g.shape[0], g.shape[1] // (2 * SIDE))
    return pl.pallas_call(
        pack_body,
        in_specs=[SMEM, HBM],
        out_specs=HBM,
        out_shape=jax.ShapeDtypeStruct(shape, g.dtype),
        scratch_shapes=[
            pltpu.VMEM(shape, g.dtype),
            pltpu.SemaphoreType.DMA((SIDE,)),
            pltpu.SemaphoreType.DMA((SIDE,)),
        ],
        name="pack_columns",
    )(idx, g)


def add_body(idx_ref, g_ref, got, o0, o1, o2, o3, buf, sem):
    cols = buf.shape[2]

    def come(j):
        at = pl.multiple_of(idx_ref[j] * cols, 128)
        return pltpu.make_async_copy(g_ref.at[:, pl.ds(at, cols)], buf.at[j], sem.at[j])

    outs = (o0, o1, o2, o3)
    for j in (3, 2, 1, 0):
        come(j).start()
    for j in (3, 2, 1, 0):
        come(j).wait()
        outs[j][...] = (buf[j].astype(F32) + got[j].astype(F32)).astype(outs[j].dtype)


def add_pairs(idx, g, got):
    shape = got.shape
    return pl.pallas_call(
        add_body,
        in_specs=[SMEM, HBM, VMEM],
        out_specs=[VMEM] * SIDE,
        out_shape=[jax.ShapeDtypeStruct(shape[1:], F32)]
        + [jax.ShapeDtypeStruct(shape[1:], BF16)] * 3,
        scratch_shapes=[pltpu.VMEM(shape, g.dtype), pltpu.SemaphoreType.DMA((SIDE,))],
        name="add_pairs",
    )(idx, g, got)


def adam_body(r0, r1, r2, p, one, two, new_p, new_one, new_two, wa, wb):
    grad = r0[...]
    for r in (r1, r2):
        grad += r[...].astype(F32)
    first = 0.9 * one[...] + 0.1 * grad
    second = 0.999 * two[...] + 0.001 * grad * grad
    step_size = 0.003 / first_fix
    denom = jnp.sqrt(second / second_fix) + 1e-08
    params = p[...] - step_size * first / denom
    new_p[...] = params
    new_one[...] = first
    new_two[...] = second
    rounded = params.astype(BF16)

    @pl.when(pl.program_id(0) == 0)
    def _():
        wa[...] = rounded

    @pl.when(pl.program_id(0) == 1)
    def _():
        wb[...] = rounded


def adam(parts, p, one, two):
    rows, cols = p.shape
    step = rows // 2
    tile = pl.BlockSpec((step, cols), lambda i: (i, 0))
    whole = pl.BlockSpec((step, cols), lambda i: (0, 0))
    full = jax.ShapeDtypeStruct((rows, cols), F32)
    half = jax.ShapeDtypeStruct((step, cols), BF16)
    return pl.pallas_call(
        adam_body,
        grid=(2,),
        in_specs=[tile] * 6,
        out_specs=[tile] * 3 + [whole] * 2,
        out_shape=[full] * 3 + [half] * 2,
        name="adam",
    )(*parts, p, one, two)


def stack_body(*refs):
    out = refs[-1]
    rows = refs[0].shape[0]
    for k, ref in enumerate(refs[:-1]):
        out[k * rows : (k + 1) * rows, :] = ref[...]


def stack_rows(blocks):
    rows, cols = blocks[0].shape
    return pl.pallas_call(
        stack_body,
        in_specs=[VMEM] * len(blocks),
        out_specs=VMEM,
        out_shape=jax.ShapeDtypeStruct((len(blocks) * rows, cols), blocks[0].dtype),
        name="stack_rows",
    )(*blocks)


def query_body(place_ref, ql_ref, *refs, seqs, steps, heads, q_rank):
    units = refs[:8]
    keep_ref, send_ref, w_buf, lat_buf, sem = refs[8:]
    z, x, sign = place_ref[0], place_ref[1], place_ref[2]
    offsets = (0, SIDE - sign, SIDE + sign, 2)
    shard = w_buf.shape[0] // (SIDE * SIDE)
    half = shard // 2
    copies = []
    for part in range(2):
        for major in range(SIDE):
            for minor in range(SIDE):
                zo, xo = (major, minor) if part == 0 else (minor, major)
                f = lax.rem(z + offsets[zo], SIDE) * SIDE + lax.rem(x + offsets[xo], SIDE)
                at = pl.multiple_of(f * shard + part * half, 64)
                copies.append(
                    pltpu.make_async_copy(
                        units[part * SIDE + major].at[pl.ds(minor * half, half), :],
                        w_buf.at[pl.ds(at, half), :],
                        sem.at[len(copies)],
                    )
                )
    for copy in copies:
        copy.start()
    for copy in copies:
        copy.wait()
    nope = dot(ql_ref[...], w_buf[:q_rank, :], NN).astype(BF16)
    for h in range(heads):
        cols = slice(h * HDIM, (h + 1) * HDIM)
        lat = dot(nope[:, cols], w_buf[q_rank:, cols], NT)
        lat_buf[:, h * steps : (h + 1) * steps, :] = lat.reshape(seqs, steps, -1)
    keep_ref[...] = lat_buf[: seqs // 2].astype(BF16)
    send_ref[...] = lat_buf[seqs // 2 :].astype(BF16)


def queries(place, ql, units, w_rows, seqs, q_rank):
    cols = units[0].shape[1]
    heads = cols // HDIM
    steps = ql.shape[0] // seqs
    lat_rank = w_rows - q_rank
    out = jax.ShapeDtypeStruct((seqs // 2, heads * steps, lat_rank), BF16)
    return pl.pallas_call(
        functools.partial(query_body, seqs=seqs, steps=steps, heads=heads, q_rank=q_rank),
        in_specs=[SMEM, VMEM] + [HBM] * 8,
        out_specs=[VMEM] * 2,
        out_shape=[out] * 2,
        scratch_shapes=[
            pltpu.VMEM((w_rows, cols), BF16),
            pltpu.VMEM((seqs, heads * steps, lat_rank), F32),
            pltpu.SemaphoreType.DMA((32,)),
        ],
        compiler_params=pltpu.CompilerParams(vmem_limit_bytes=24 * MIB),
        name="queries",
    )(place, ql, *units)


def attention_body(
    order_ref,
    len_ref,
    q_own,
    q_got,
    r_own,
    r_got,
    nl_ref,
    nr_ref,
    lat_hbm,
    rope_hbm,
    keep_ref,
    send_ref,
    lat_buf,
    rope_buf,
    q_buf,
    qr_buf,
    acc,
    m_ref,
    l_ref,
    p0,
    p1,
    a0,
    a1,
    seq_of,
    blk_of,
    lat_sem,
    rope_sem,
    *,
    steps,
):
    seqs, rows, _ = q_buf.shape
    part = rows // 2
    factor = LOG2E / math.sqrt(HDIM + ROPE)

    def listing(s, at):
        blocks = lax.div(len_ref[s] + (BLOCK - 1), BLOCK)

        def put(j, at):
            seq_of[at] = s
            blk_of[at] = j
            return at + 1

        return lax.fori_loop(0, blocks, put, at)

    count = lax.fori_loop(0, seqs, listing, 0)

    def lat_copy(i):
        slot = lax.rem(i, SLOTS)
        start = pl.multiple_of(blk_of[i] * BLOCK, BLOCK)
        return pltpu.make_async_copy(
            lat_hbm.at[order_ref[seq_of[i]], pl.ds(start, BLOCK), :],
            lat_buf.at[slot],
            lat_sem.at[slot],
        )

    def rope_copy(i):
        slot = lax.rem(i, SLOTS)
        start = pl.multiple_of(blk_of[i] * BLOCK, BLOCK)
        return pltpu.make_async_copy(
            rope_hbm.at[order_ref[seq_of[i]], :, pl.ds(start, BLOCK)],
            rope_buf.at[slot],
            rope_sem.at[slot],
        )

    def fetch(i):
        @pl.when(i < count)
        def _():
            lat_copy(i).start()
            rope_copy(i).start()

    for i in range(SLOTS - 1):
        fetch(i)

    q_buf[:, :part, :] = q_own[...]
    q_buf[:, part:, :] = q_got[...]
    qr_buf[:, :part, :] = r_own[...]
    qr_buf[:, part:, :] = r_got[...]

    width = nl_ref.shape[1]
    token = lax.broadcasted_iota(jnp.int32, (rows, width), 1)
    step = lax.rem(lax.broadcasted_iota(jnp.int32, (rows, width), 0), steps)
    seen = token <= step
    for s in range(seqs):
        score = dot(q_buf[s], nl_ref[s], NT) + dot(qr_buf[s], nr_ref[s], NT)
        score = jnp.where(seen, score, NEG)
        top = jnp.max(score, axis=1, keepdims=True)
        prob = jnp.exp2((score - top) * factor)
        m_ref[s] = jnp.broadcast_to(top, (rows, 128))
        l_ref[s] = prob
        acc[s] = dot(prob.astype(BF16), nl_ref[s], NN)

    lane = lax.broadcasted_iota(jnp.int32, (rows, BLOCK), 1)

    def scores(i, p_ref, a_ref):
        slot = lax.rem(i, SLOTS)
        s = seq_of[i]
        lat_copy(i).wait()
        rope_copy(i).wait()
        score = dot(q_buf[s], lat_buf[slot], NT) + dot(qr_buf[s], rope_buf[slot], NN)
        score = jnp.where(lane < len_ref[s] - blk_of[i] * BLOCK, score, NEG)
        before = m_ref[s]
        top = jnp.maximum(before, jnp.max(score, axis=1, keepdims=True))
        prob = jnp.exp2((score - top[:, :1]) * factor)
        alpha = jnp.exp2((before - top) * factor)
        total = l_ref[s] * alpha
        for k in range(BLOCK // 128):
            total += prob[:, k * 128 : (k + 1) * 128]
        m_ref[s] = top
        l_ref[s] = total
        a_ref[...] = alpha
        p_ref[...] = prob.astype(BF16)

    def gather(i, p_ref, a_ref):
        slot = lax.rem(i, SLOTS)
        s = seq_of[i]
        acc[s] = acc[s] * a_ref[:, :1] + dot(p_ref[...], lat_buf[slot], NN)

    scores(0, p0, a0)

    def pair(k, carry):
        i = 2 * k
        fetch(i + SLOTS - 1)
        gather(i, p0, a0)
        scores(i + 1, p1, a1)
        fetch(i + SLOTS)
        gather(i + 1, p1, a1)
        scores(i + 2, p0, a0)
        return carry

    pairs = lax.div(count - 1, 2)
    lax.fori_loop(0, pairs, pair, 0)

    @pl.when(2 * pairs + 1 < count)
    def _():
        fetch(2 * pairs + SLOTS - 1)
        gather(2 * pairs, p0, a0)
        scores(2 * pairs + 1, p1, a1)
        gather(2 * pairs + 1, p1, a1)

    @pl.when(2 * pairs + 1 >= count)
    def _():
        gather(2 * pairs, p0, a0)

    for s in range(seqs):
        mixed = (acc[s] / jnp.sum(l_ref[s], axis=1, keepdims=True)).astype(BF16)
        keep_ref[s] = mixed[:part]
        send_ref[s] = mixed[part:]


def attention(order, lengths, q_own, q_got, r_own, r_got, nl, nr, lat, rope, steps):
    seqs, part, lat_rank = q_own.shape
    rows = 2 * part
    most = seqs * (lat.shape[1] // BLOCK) + 1
    out = jax.ShapeDtypeStruct(q_own.shape, BF16)
    return pl.pallas_call(
        functools.partial(attention_body, steps=steps),
        in_specs=[SMEM, SMEM] + [VMEM] * 6 + [HBM] * 2,
        out_specs=[VMEM] * 2,
        out_shape=[out] * 2,
        scratch_shapes=[
            pltpu.VMEM((SLOTS, BLOCK, lat_rank), BF16),
            pltpu.VMEM((SLOTS, ROPE, BLOCK), BF16),
            pltpu.VMEM((seqs, rows, lat_rank), BF16),
            pltpu.VMEM((seqs, rows, ROPE), BF16),
            pltpu.VMEM((seqs, rows, lat_rank), F32),
            pltpu.VMEM((seqs, rows, 128), F32),
            pltpu.VMEM((seqs, rows, 128), F32),
            pltpu.VMEM((rows, BLOCK), BF16),
            pltpu.VMEM((rows, BLOCK), BF16),
            pltpu.VMEM((rows, 128), F32),
            pltpu.VMEM((rows, 128), F32),
            pltpu.SMEM((most,), jnp.int32),
            pltpu.SMEM((most,), jnp.int32),
            pltpu.SemaphoreType.DMA((SLOTS,)),
            pltpu.SemaphoreType.DMA((SLOTS,)),
        ],
        compiler_params=pltpu.CompilerParams(vmem_limit_bytes=40 * MIB),
        name="attention",
    )(order, lengths, q_own, q_got, r_own, r_got, nl, nr, lat, rope)


def values_body(order_ref, step_ref, own, got, vw_ref, out_ref, mixed, flat):
    half, rows, lat_rank = own.shape
    seqs = 2 * half
    heads = vw_ref.shape[1] // HDIM
    steps = rows // heads
    mixed[:half] = own[...].astype(F32)
    mixed[half:] = got[...].astype(F32)
    for h in range(heads):
        cols = slice(h * HDIM, (h + 1) * HDIM)
        part = mixed[:, h * steps : (h + 1) * steps, :].reshape(seqs * steps, lat_rank)
        flat[:, cols] = dot(part.astype(BF16), vw_ref[:, cols], NN).astype(BF16)
    count = seqs * steps
    row = lax.broadcasted_iota(jnp.int32, (count, count), 0)
    col = lax.broadcasted_iota(jnp.int32, (count, count), 1)
    want_step = jnp.zeros((count, count), jnp.int32)
    want_seq = jnp.zeros((count, count), jnp.int32)
    for k in range(steps):
        want_step = jnp.where(lax.div(row, seqs) == k, step_ref[k], want_step)
    for k in range(seqs):
        want_seq = jnp.where(lax.div(col, steps) == k, order_ref[k], want_seq)
    same = (want_step == lax.rem(col, steps)) & (want_seq == lax.rem(row, seqs))
    pick = jnp.where(same, 1.0, 0.0).astype(BF16)
    out_ref[...] = dot(pick, flat[...], NN).astype(BF16)


def project_values(order, step_order, own, got, vw):
    half, rows, lat_rank = own.shape
    cols = vw.shape[1]
    count = 2 * half * rows * HDIM // cols
    return pl.pallas_call(
        values_body,
        in_specs=[SMEM, SMEM] + [VMEM] * 3,
        out_specs=VMEM,
        out_shape=jax.ShapeDtypeStruct((count, cols), BF16),
        scratch_shapes=[
            pltpu.VMEM((2 * half, rows, lat_rank), F32),
            pltpu.VMEM((count, cols), BF16),
        ],
        compiler_params=pltpu.CompilerParams(vmem_limit_bytes=24 * MIB),
        name="project_values",
    )(order, step_order, own, got, vw)


def output_body(place_ref, *refs, seqs):
    tokens, weights = refs[:4], refs[4:8]
    send_ref, keep_ref, v_buf, w_buf, v_sem, w_sem = refs[8:]
    x, sign = place_ref[1], place_ref[2]
    offsets = (0, SIDE - sign, SIDE + sign, 2)
    depth = v_buf.shape[2]
    part = weights[0].shape[0]
    copies = []
    for k in range(SIDE):
        to = lax.rem(offsets[k], SIDE) if k else 0
        copies.append(pltpu.make_async_copy(tokens[k], v_buf.at[to], v_sem.at[k]))
    for k in range(SIDE):
        at = pl.multiple_of(lax.rem(x + offsets[k], SIDE) * part, 64)
        copies.append(
            pltpu.make_async_copy(weights[k], w_buf.at[pl.ds(at, part), :], w_sem.at[k])
        )
    for copy in copies:
        copy.start()
    for copy in copies:
        copy.wait()
    tokens_all = v_buf[...].reshape(-1, depth)
    width = 256
    for n in range(w_buf.shape[0] // width):
        cols = slice(n * width, (n + 1) * width)
        res = dot(tokens_all, w_buf[cols, :], NT).reshape(SIDE, 2 * SIDE, seqs, width)
        for b in range(SIDE):
            for z in range(SIDE):
                send_ref[b, z, :, cols] = res[z, b].astype(BF16)
                keep_ref[b, z, :, cols] = res[z, SIDE + b].astype(BF16)


def output_blocks(place, tokens, weights, seqs):
    count, depth = tokens[0].shape
    cols = SIDE * weights[0].shape[0]
    out = jax.ShapeDtypeStruct((SIDE, SIDE, seqs, cols), BF16)
    return pl.pallas_call(
        functools.partial(output_body, seqs=seqs),
        in_specs=[SMEM] + [HBM] * 8,
        out_specs=[VMEM] * 2,
        out_shape=[out] * 2,
        scratch_shapes=[
            pltpu.VMEM((SIDE, count, depth), BF16),
            pltpu.VMEM((cols, depth), BF16),
            pltpu.SemaphoreType.DMA((SIDE,)),
            pltpu.SemaphoreType.DMA((SIDE,)),
        ],
        compiler_params=pltpu.CompilerParams(vmem_limit_bytes=24 * MIB),
        name="output_blocks",
    )(place, *tokens, *weights)


def join_body(a, b, o0, o1, o2, o3):
    for j, o in enumerate((o0, o1, o2, o3)):
        o[...] = (a[j].astype(F32) + b[j].astype(F32)).astype(o.dtype)


def join_pairs(a, b):
    out = jax.ShapeDtypeStruct(a.shape[1:], BF16)
    return pl.pallas_call(
        join_body,
        in_specs=[VMEM] * 2,
        out_specs=[VMEM] * SIDE,
        out_shape=[out] * SIDE,
        name="join_pairs",
    )(a, b)


def total_body(a, b, c, o0, o1, o2, o3):
    for j, o in enumerate((o0, o1, o2, o3)):
        o[...] = (a[j].astype(F32) + b[j].astype(F32) + c[j].astype(F32)).astype(o.dtype)


def total_blocks(parts):
    out = jax.ShapeDtypeStruct(parts[0].shape[1:], BF16)
    return pl.pallas_call(
        total_body,
        in_specs=[VMEM] * 3,
        out_specs=[VMEM] * SIDE,
        out_shape=[out] * SIDE,
        name="total_blocks",
    )(*parts)


def columns_body(at_ref, *refs):
    out = refs[-1]
    width = refs[0].shape[1]
    for k, ref in enumerate(refs[:-1]):
        out[:, pl.ds(pl.multiple_of(at_ref[k] * width, 128), width)] = ref[...]


def join_columns(at, blocks):
    rows, width = blocks[0].shape
    return pl.pallas_call(
        columns_body,
        in_specs=[SMEM] + [VMEM] * SIDE,
        out_specs=VMEM,
        out_shape=jax.ShapeDtypeStruct((rows, SIDE * width), BF16),
        name="join_columns",
    )(at, *blocks)


def settle_body(idx_ref, *refs):
    out = refs[-1]
    for k, ref in enumerate(refs[:-1]):
        out[idx_ref[k]] = ref[...]


def settle(idx, blocks):
    return pl.pallas_call(
        settle_body,
        in_specs=[SMEM] + [VMEM] * 8,
        out_specs=VMEM,
        out_shape=jax.ShapeDtypeStruct((8,) + blocks[0].shape, BF16),
        name="settle",
    )(idx, *blocks)


def splits(seqs):
    table = []
    for rest in itertools.combinations(range(1, seqs), seqs // 2 - 1):
        mine = (0,) + rest
        table.append(mine + tuple(s for s in range(seqs) if s not in mine))
    return np.array(table, np.int32)


def balanced_order(lengths):
    seqs = lengths.shape[0]
    table = splits(seqs)
    member = np.zeros((table.shape[0], seqs), np.int32)
    for i, row in enumerate(table):
        member[i, row[: seqs // 2]] = 1
    blocks = lax.div(lengths + (BLOCK - 1), BLOCK)
    first = jnp.sum(member * blocks[None, :], axis=1)
    larger = jnp.maximum(first, jnp.sum(blocks) - first)
    index = np.arange(table.shape[0], dtype=np.int32)
    score = larger * table.shape[0] + index
    chosen = (score == jnp.min(score)).astype(jnp.int32)
    return jnp.sum(chosen[:, None] * table, axis=0)


def rotate(vector, position):
    half = vector.shape[-1] // 2
    index_f = jnp.arange(half, dtype=jnp.float32)
    frequency = jnp.exp(-math.log(10000.0) * 2.0 * index_f / vector.shape[-1])
    angle = position[..., None] * frequency
    first = vector[..., :half]
    second = vector[..., half:]
    cosine = jnp.cos(angle)
    sine = jnp.sin(angle)
    return jnp.concatenate(
        [first * cosine - second * sine, first * sine + second * cosine], axis=-1
    )


def body(
    grad_parts,
    params,
    moment_one,
    moment_two,
    query_latent,
    rope_weight,
    value_weight,
    out_weight,
    latent_cache,
    rope_cache,
    new_latent,
    new_rope,
    lengths,
):
    head = lax.axis_index("head")
    y, core = lax.div(head, 2), lax.rem(head, 2)
    fsdp = lax.axis_index("fsdp")
    z, x = lax.div(fsdp, SIDE), lax.rem(fsdp, SIDE)
    sign = 1 - 2 * core
    place = jnp.stack([z, x, sign])

    def turned(base, s):
        return lax.rem(jnp.stack([base, base + SIDE + s, base + SIDE - s, base + 2]), SIDE)

    send_idx = 2 * turned(y, -sign) + (1 - core)
    keep_idx = 2 * turned(y, sign) + core

    grad = grad_parts[0]
    got = other_core(pack(send_idx, grad))
    parts = ring_sum(add_pairs(keep_idx, grad, got), "y")
    new_params, new_one, new_two, w_a, w_b = adam(parts, params, moment_one, moment_two)

    w_t = out_weight.T
    w_one, w_two = forth(w_t, "x"), back(w_t, "x")
    w_one, w_a, w_b = lax.optimization_barrier((w_one, w_a, w_b))

    units = []
    for piece, first, then in ((w_a, "x", "z"), (w_b, "z", "x")):
        units += list(ring(stack_rows(ring(piece, first)), then))
    out_weights = (w_t, w_one, w_two, forth(w_one, "x"))

    steps_n, seq_local, q_rank = query_latent.shape
    heads_local = value_weight.shape[1] // HDIM
    half = seq_local // 2
    order = balanced_order(lengths)
    order = jnp.where(core == 0, order, jnp.concatenate([order[half:], order[:half]]))
    chosen = order[:, None] == jnp.arange(seq_local, dtype=jnp.int32)[None, :]
    lengths_in = jnp.sum(jnp.where(chosen, lengths[None, :], 0), axis=1)
    chosen = chosen.astype(BF16)

    def arrange(which, arrays):
        return jnp.einsum("ps,tsq->ptq", which, arrays, preferred_element_type=F32).astype(BF16)

    by_seq = arrange(chosen, query_latent).reshape(seq_local * steps_n, q_rank)
    query_rope = jnp.dot(by_seq, rope_weight, preferred_element_type=F32).reshape(
        seq_local, steps_n, heads_local, ROPE
    )
    position = (lengths_in[:, None] + jnp.arange(steps_n, dtype=jnp.int32)[None, :]).astype(F32)[
        :, :, None
    ]
    query_rope = rotate(query_rope, position).astype(BF16)
    query_rope = jnp.transpose(query_rope, (0, 2, 1, 3)).reshape(
        seq_local, heads_local * steps_n, ROPE
    )
    r_own, r_got = query_rope[:half], other_core(query_rope[half:])
    pad = ((0, 0), (0, 128 - steps_n), (0, 0))
    nl = jnp.pad(arrange(chosen[:half], new_latent), pad)
    nr = jnp.pad(arrange(chosen[:half], new_rope), pad)

    w_rows = SIDE * SIDE * params.shape[0]
    q_own, q_send = queries(place, by_seq, units, w_rows, seq_local, q_rank)
    mixed, mixed_send = attention(
        order,
        lengths_in[:half],
        q_own,
        other_core(q_send),
        r_own,
        r_got,
        nl,
        nr,
        latent_cache,
        rope_cache,
        steps_n,
    )
    step_order = jnp.concatenate([send_idx, keep_idx])
    values = project_values(order, step_order, mixed, other_core(mixed_send), value_weight)

    send, keep = output_blocks(place, ring(values, "z"), out_weights, seq_local)
    parts = ring_sum(join_pairs(keep, other_core(send)), "y")
    blocks = total_blocks(parts)

    arrived = [blocks[0]]
    for d in range(1, SIDE):
        perm = [
            (zz * SIDE + xx, ((zz + d) % SIDE) * SIDE + xx)
            for zz in range(SIDE)
            for xx in range(SIDE)
        ]
        arrived.append(lax.ppermute(blocks[d], "fsdp", perm))
    back_z = lax.rem(z + SIDE - jnp.arange(SIDE, dtype=jnp.int32), SIDE)
    mine = join_columns(back_z, arrived)

    column = list(ring(mine, "y"))
    column += [other_core(b) for b in column]
    from_own = 2 * turned(y, -sign) + core
    from_other = 2 * turned(y, sign) + (1 - core)
    decoded = settle(jnp.concatenate([from_own, from_other]), column)
    return (new_params, new_one, new_two, decoded)


def solution(mesh):
    return jax.shard_map(
        body,
        mesh=mesh,
        in_specs=(
            P("head", "fsdp", None),
            P("fsdp", "head"),
            P("fsdp", "head"),
            P("fsdp", "head"),
            P(None, "fsdp", None),
            P(None, "head"),
            P(None, "head"),
            P("head", "fsdp"),
            P("fsdp", None, None),
            P("fsdp", None, None),
            P(None, "fsdp", None),
            P(None, "fsdp", None),
            P("fsdp"),
        ),
        out_specs=(P("fsdp", "head"), P("fsdp", "head"), P("fsdp", "head"), P(None, "fsdp", None)),
        check_vma=False,
    )
```

```python
import functools
import itertools
import math

import jax
import jax.numpy as jnp
import numpy as np
from jax import lax
from jax.experimental import pallas as pl
from jax.experimental.pallas import tpu as pltpu
from jax.sharding import PartitionSpec as P

HDIM = 128
ROPE = 64
SIDE = 4
BLOCK = 1024
SLOTS = 12
MIB = 1024 * 1024

first_fix = 1.0 - math.exp(100.0 * math.log(0.9))
second_fix = 1.0 - math.exp(100.0 * math.log(0.999))
NEG = -1e30
LOG2E = math.log2(math.e)

NT = (((1,), (1,)), ((), ()))
NN = (((1,), (0,)), ((), ()))


def dot(a, b, dims):
    return lax.dot_general(a, b, dims, preferred_element_type=jnp.float32)


def moves(step):
    perm = []
    for z in range(SIDE):
        for x in range(SIDE):
            for y in range(SIDE):
                for c in range(2):
                    axis, d = step(c)
                    to = {"x": x, "y": y, "z": z}
                    to[axis] = (to[axis] + d) % SIDE
                    perm.append(
                        (
                            (z * SIDE + x) * 2 * SIDE + y * 2 + c,
                            (to["z"] * SIDE + to["x"]) * 2 * SIDE + to["y"] * 2 + c,
                        )
                    )
    return perm


def shift(v, step):
    return lax.ppermute(v, ("fsdp", "head"), moves(step))


def forth(v, axis):
    return shift(v, lambda c: (axis, 1 - 2 * c))


def back(v, axis):
    return shift(v, lambda c: (axis, 2 * c - 1))


def first(v, d):
    return shift(v, lambda c: (("x", "z")[c], d))


def second(v, d):
    return shift(v, lambda c: (("z", "x")[c], d))


def other_core(v):
    return lax.ppermute(v, "head", [(i, i ^ 1) for i in range(2 * SIDE)])


def ring(own, axis):
    one = forth(own, axis)
    two = back(own, axis)
    return own, one, two, forth(one, axis)


def ring_sum(blocks, axis):
    far = forth(blocks[3], axis)
    two = back(blocks[2], axis)
    one = forth(add_two(blocks[1], far), axis)
    return blocks[0], one, two


def here():
    f = lax.axis_index("fsdp")
    h = lax.axis_index("head")
    return lax.div(f, SIDE), lax.rem(f, SIDE), lax.div(h, 2), lax.rem(h, 2)


def turned(base, s):
    return [lax.rem(base + d, SIDE) for d in (0, SIDE + s, SIDE - s, 2)]


VMEM = pl.BlockSpec(memory_space=pltpu.VMEM)
SMEM = pl.BlockSpec(memory_space=pltpu.SMEM)
HBM = pl.BlockSpec(memory_space=pltpu.HBM)
F32 = jnp.float32
BF16 = jnp.bfloat16


def room(mib):
    return pltpu.CompilerParams(vmem_limit_bytes=mib * MIB)


def add_two_body(a, b, o):
    o[...] = (a[...].astype(F32) + b[...].astype(F32)).astype(o.dtype)


def add_two(a, b):
    return pl.pallas_call(
        add_two_body,
        in_specs=[VMEM] * 2,
        out_specs=VMEM,
        out_shape=jax.ShapeDtypeStruct(a.shape, BF16),
        compiler_params=room(8),
        name="add_two",
    )(a, b)


def pack_body(g_ref, send_ref, keep_ref, sem):
    _, _, y, core = here()
    sign = 1 - 2 * core
    cols = send_ref.shape[2]
    copies = []
    for ref, ys, c in (
        (send_ref, turned(y, -sign), 1 - core),
        (keep_ref, turned(y, sign), core),
    ):
        for j in range(SIDE):
            at = pl.multiple_of((2 * ys[j] + c) * cols, 128)
            copies.append(
                pltpu.make_async_copy(
                    g_ref.at[:, pl.ds(at, cols)], ref.at[j], sem.at[len(copies)]
                )
            )
    for copy in copies:
        copy.start()
    for copy in copies:
        copy.wait()


def pack(g):
    out = jax.ShapeDtypeStruct((SIDE, g.shape[0], g.shape[1] // (2 * SIDE)), g.dtype)
    return pl.pallas_call(
        pack_body,
        in_specs=[HBM],
        out_specs=[VMEM] * 2,
        out_shape=[out] * 2,
        scratch_shapes=[pltpu.SemaphoreType.DMA((2 * SIDE,))],
        compiler_params=room(8),
        name="pack_columns",
    )(g)


def add_body(keep, got, o0, o1, o2, o3):
    for j, o in ((3, o3), (2, o2), (1, o1), (0, o0)):
        o[...] = (keep[j].astype(F32) + got[j].astype(F32)).astype(o.dtype)


def add_pairs(keep, got, kind):
    shape = got.shape[1:]
    return pl.pallas_call(
        add_body,
        in_specs=[VMEM] * 2,
        out_specs=[VMEM] * SIDE,
        out_shape=[jax.ShapeDtypeStruct(shape, kind)] + [jax.ShapeDtypeStruct(shape, BF16)] * 3,
        compiler_params=room(8),
        name="add_pairs",
    )(keep, got)


def adam_body(r0, r1, r2, p, one, two, new_p, new_one, new_two, w):
    grad = r0[...] + r1[...].astype(F32) + r2[...].astype(F32)
    moment = 0.9 * one[...] + 0.1 * grad
    second_moment = 0.999 * two[...] + 0.001 * grad * grad
    step_size = 0.003 / first_fix
    denom = jnp.sqrt(second_moment / second_fix) + 1e-08
    params = p[...] - step_size * moment / denom
    w[...] = params.astype(BF16)
    new_p[...] = params
    new_one[...] = moment
    new_two[...] = second_moment


def adam(parts, p, one, two):
    full = jax.ShapeDtypeStruct(p.shape, F32)
    return pl.pallas_call(
        adam_body,
        in_specs=[VMEM] * 6,
        out_specs=[VMEM] * 4,
        out_shape=[full] * 3 + [jax.ShapeDtypeStruct(p.shape, BF16)],
        compiler_params=room(12),
        name="adam",
    )(*parts, p, one, two)


def stack_body(a, b, out):
    rows = a.shape[0]
    out[:rows, :] = a[...]
    out[rows:, :] = b[...]


def stack_rows(a, b):
    rows, cols = a.shape
    return pl.pallas_call(
        stack_body,
        in_specs=[VMEM] * 2,
        out_specs=VMEM,
        out_shape=jax.ShapeDtypeStruct((2 * rows, cols), a.dtype),
        compiler_params=room(8),
        name="stack_rows",
    )(a, b)


def query_body(ql_ref, *refs, seqs, steps, heads, q_rank):
    units = refs[:8]
    keep_ref, send_ref, w_buf, lat_buf = refs[8:]
    z, x, _, core = here()
    shard = w_buf.shape[0] // (SIDE * SIDE)
    far = (0, SIDE - 1, 1, 2)
    for k in range(SIDE):
        for m in range(SIDE):
            zo = jnp.where(core == 0, far[k], far[m])
            xo = jnp.where(core == 0, far[m], far[k])
            f = lax.rem(z + zo, SIDE) * SIDE + lax.rem(x + xo, SIDE)
            at = pl.multiple_of(f * shard, shard)
            rows = slice((m % 2) * shard, (m % 2 + 1) * shard)
            w_buf[pl.ds(at, shard), :] = units[2 * k + m // 2][rows, :]
    nope = dot(ql_ref[...], w_buf[:q_rank, :], NN).astype(BF16)
    for h in range(heads):
        cols = slice(h * HDIM, (h + 1) * HDIM)
        lat = dot(nope[:, cols], w_buf[q_rank:, cols], NT)
        lat_buf[:, h * steps : (h + 1) * steps, :] = lat.reshape(seqs, steps, -1)
    keep_ref[...] = lat_buf[: seqs // 2].astype(BF16)
    send_ref[...] = lat_buf[seqs // 2 :].astype(BF16)


def queries(ql, units, w_rows, seqs, q_rank):
    cols = units[0].shape[1]
    heads = cols // HDIM
    steps = ql.shape[0] // seqs
    lat_rank = w_rows - q_rank
    out = jax.ShapeDtypeStruct((seqs // 2, heads * steps, lat_rank), BF16)
    return pl.pallas_call(
        functools.partial(query_body, seqs=seqs, steps=steps, heads=heads, q_rank=q_rank),
        in_specs=[VMEM] * 9,
        out_specs=[VMEM] * 2,
        out_shape=[out] * 2,
        scratch_shapes=[
            pltpu.VMEM((w_rows, cols), BF16),
            pltpu.VMEM((seqs, heads * steps, lat_rank), F32),
        ],
        compiler_params=room(16),
        name="queries",
    )(ql, *units)


def attention_body(
    order_ref,
    len_ref,
    q_own,
    q_got,
    r_own,
    r_got,
    nl_ref,
    nr_ref,
    lat_hbm,
    rope_hbm,
    keep_ref,
    send_ref,
    lat_buf,
    rope_buf,
    q_buf,
    qr_buf,
    acc,
    m_ref,
    l_ref,
    p0,
    p1,
    a0,
    a1,
    seq_of,
    blk_of,
    lat_sem,
    rope_sem,
    *,
    steps,
):
    seqs, rows, _ = q_buf.shape
    part = rows // 2
    factor = LOG2E / math.sqrt(HDIM + ROPE)

    def listing(s, at):
        blocks = lax.div(len_ref[s] + (BLOCK - 1), BLOCK)

        def put(j, at):
            seq_of[at] = s
            blk_of[at] = j
            return at + 1

        return lax.fori_loop(0, blocks, put, at)

    count = lax.fori_loop(0, seqs, listing, 0)

    def lat_copy(i):
        slot = lax.rem(i, SLOTS)
        start = pl.multiple_of(blk_of[i] * BLOCK, BLOCK)
        return pltpu.make_async_copy(
            lat_hbm.at[order_ref[seq_of[i]], pl.ds(start, BLOCK), :],
            lat_buf.at[slot],
            lat_sem.at[slot],
        )

    def rope_copy(i):
        slot = lax.rem(i, SLOTS)
        start = pl.multiple_of(blk_of[i] * BLOCK, BLOCK)
        return pltpu.make_async_copy(
            rope_hbm.at[order_ref[seq_of[i]], :, pl.ds(start, BLOCK)],
            rope_buf.at[slot],
            rope_sem.at[slot],
        )

    def fetch(i):
        @pl.when(i < count)
        def _():
            lat_copy(i).start()
            rope_copy(i).start()

    for i in range(SLOTS - 2):
        fetch(i)

    q_buf[:, :part, :] = q_own[...]
    q_buf[:, part:, :] = q_got[...]
    qr_buf[:, :part, :] = r_own[...]
    qr_buf[:, part:, :] = r_got[...]

    width = nl_ref.shape[1]
    token = lax.broadcasted_iota(jnp.int32, (rows, width), 1)
    step = lax.rem(lax.broadcasted_iota(jnp.int32, (rows, width), 0), steps)
    seen = token <= step
    for s in range(seqs):
        score = dot(q_buf[s], nl_ref[s], NT) + dot(qr_buf[s], nr_ref[s], NT)
        score = jnp.where(seen, score, NEG)
        top = jnp.max(score, axis=1, keepdims=True)
        prob = jnp.exp2((score - top) * factor)
        m_ref[s] = jnp.broadcast_to(top, (rows, 128))
        l_ref[s] = prob
        acc[s] = dot(prob.astype(BF16), nl_ref[s], NN)

    lane = lax.broadcasted_iota(jnp.int32, (rows, BLOCK), 1)

    def arrive(i):
        lat_copy(i).wait()
        rope_copy(i).wait()

    def scores(i):
        slot = lax.rem(i, SLOTS)
        s = seq_of[i]
        return dot(q_buf[s], lat_buf[slot], NT) + dot(qr_buf[s], rope_buf[slot], NN)

    def weigh(i, score, p_ref, a_ref):
        s = seq_of[i]
        score = jnp.where(lane < len_ref[s] - blk_of[i] * BLOCK, score, NEG)
        before = m_ref[s]
        top = jnp.maximum(before, jnp.max(score, axis=1, keepdims=True))
        prob = jnp.exp2((score - top[:, :1]) * factor)
        alpha = jnp.exp2((before - top) * factor)
        total = l_ref[s] * alpha
        for k in range(BLOCK // 128):
            total += prob[:, k * 128 : (k + 1) * 128]
        m_ref[s] = top
        l_ref[s] = total
        a_ref[...] = alpha
        p_ref[...] = prob.astype(BF16)

    def gather(i, p_ref, a_ref):
        slot = lax.rem(i, SLOTS)
        s = seq_of[i]
        acc[s] = acc[s] * a_ref[:, :1] + dot(p_ref[...], lat_buf[slot], NN)

    arrive(0)
    weigh(0, scores(0), p0, a0)

    def pair(k, carry):
        i = 2 * k
        fetch(i + SLOTS - 2)
        fetch(i + SLOTS - 1)
        arrive(i + 1)
        arrive(i + 2)
        odd = scores(i + 1)
        gather(i, p0, a0)
        even = scores(i + 2)
        weigh(i + 1, odd, p1, a1)
        gather(i + 1, p1, a1)
        weigh(i + 2, even, p0, a0)
        return carry

    pairs = lax.div(count - 1, 2)
    lax.fori_loop(0, pairs, pair, 0)

    @pl.when(2 * pairs + 1 < count)
    def _():
        arrive(2 * pairs + 1)
        odd = scores(2 * pairs + 1)
        gather(2 * pairs, p0, a0)
        weigh(2 * pairs + 1, odd, p1, a1)
        gather(2 * pairs + 1, p1, a1)

    @pl.when(2 * pairs + 1 >= count)
    def _():
        gather(2 * pairs, p0, a0)

    for s in range(seqs):
        mixed = (acc[s] / jnp.sum(l_ref[s], axis=1, keepdims=True)).astype(BF16)
        keep_ref[s] = mixed[:part]
        send_ref[s] = mixed[part:]


def attention(order, lengths, q_own, q_got, r_own, r_got, nl, nr, lat, rope, steps):
    seqs, part, lat_rank = q_own.shape
    rows = 2 * part
    most = seqs * (lat.shape[1] // BLOCK) + 1
    out = jax.ShapeDtypeStruct(q_own.shape, BF16)
    return pl.pallas_call(
        functools.partial(attention_body, steps=steps),
        in_specs=[SMEM, SMEM] + [VMEM] * 6 + [HBM] * 2,
        out_specs=[VMEM] * 2,
        out_shape=[out] * 2,
        scratch_shapes=[
            pltpu.VMEM((SLOTS, BLOCK, lat_rank), BF16),
            pltpu.VMEM((SLOTS, ROPE, BLOCK), BF16),
            pltpu.VMEM((seqs, rows, lat_rank), BF16),
            pltpu.VMEM((seqs, rows, ROPE), BF16),
            pltpu.VMEM((seqs, rows, lat_rank), F32),
            pltpu.VMEM((seqs, rows, 128), F32),
            pltpu.VMEM((seqs, rows, 128), F32),
            pltpu.VMEM((rows, BLOCK), BF16),
            pltpu.VMEM((rows, BLOCK), BF16),
            pltpu.VMEM((rows, 128), F32),
            pltpu.VMEM((rows, 128), F32),
            pltpu.SMEM((most,), jnp.int32),
            pltpu.SMEM((most,), jnp.int32),
            pltpu.SemaphoreType.DMA((SLOTS,)),
            pltpu.SemaphoreType.DMA((SLOTS,)),
        ],
        compiler_params=room(36),
        name="attention",
    )(order, lengths, q_own, q_got, r_own, r_got, nl, nr, lat, rope)


def values_body(order_ref, own, got, vw_ref, out_ref, mixed, flat):
    half, rows, lat_rank = own.shape
    seqs = 2 * half
    heads = vw_ref.shape[1] // HDIM
    steps = rows // heads
    mixed[:half] = own[...].astype(F32)
    mixed[half:] = got[...].astype(F32)
    for h in range(heads):
        cols = slice(h * HDIM, (h + 1) * HDIM)
        part = mixed[:, h * steps : (h + 1) * steps, :].reshape(seqs * steps, lat_rank)
        flat[:, cols] = dot(part.astype(BF16), vw_ref[:, cols], NN).astype(BF16)
    _, _, y, core = here()
    sign = 1 - 2 * core
    step_of = [2 * v + (1 - core) for v in turned(y, -sign)]
    step_of += [2 * v + core for v in turned(y, sign)]
    count = seqs * steps
    row = lax.broadcasted_iota(jnp.int32, (count, count), 0)
    col = lax.broadcasted_iota(jnp.int32, (count, count), 1)
    want_step = jnp.zeros((count, count), jnp.int32)
    want_seq = jnp.zeros((count, count), jnp.int32)
    for k in range(steps):
        want_step = jnp.where(lax.div(row, seqs) == k, step_of[k], want_step)
    for k in range(seqs):
        want_seq = jnp.where(lax.div(col, steps) == k, order_ref[k], want_seq)
    same = (want_step == lax.rem(col, steps)) & (want_seq == lax.rem(row, seqs))
    pick = jnp.where(same, 1.0, 0.0).astype(BF16)
    out_ref[...] = dot(pick, flat[...], NN).astype(BF16)


def project_values(order, own, got, vw):
    half, rows, lat_rank = own.shape
    cols = vw.shape[1]
    count = 2 * half * rows * HDIM // cols
    return pl.pallas_call(
        values_body,
        in_specs=[SMEM] + [VMEM] * 3,
        out_specs=VMEM,
        out_shape=jax.ShapeDtypeStruct((count, cols), BF16),
        scratch_shapes=[
            pltpu.VMEM((2 * half, rows, lat_rank), F32),
            pltpu.VMEM((count, cols), BF16),
        ],
        compiler_params=room(12),
        name="project_values",
    )(order, own, got, vw)


def output_body(*refs, seqs):
    tokens, weights = refs[:4], refs[4:8]
    send_ref, keep_ref, v_buf, w_buf = refs[8:]
    _, x, _, core = here()
    sign = 1 - 2 * core
    offsets = (0, SIDE - sign, SIDE + sign, 2)
    depth = v_buf.shape[2]
    part = weights[0].shape[0]
    for k in range(SIDE):
        v_buf[lax.rem(offsets[k], SIDE) if k in (1, 2) else offsets[k]] = tokens[k][...]
        at = pl.multiple_of(lax.rem(x + offsets[k], SIDE) * part, 64)
        w_buf[pl.ds(at, part), :] = weights[k][...]
    tokens_all = v_buf[...].reshape(-1, depth)
    width = 256
    for n in range(w_buf.shape[0] // width):
        cols = slice(n * width, (n + 1) * width)
        res = dot(tokens_all, w_buf[cols, :], NT).reshape(SIDE, 2 * SIDE, seqs, width)
        for b in range(SIDE):
            for z in range(SIDE):
                send_ref[b, z, :, cols] = res[z, b].astype(BF16)
                keep_ref[b, z, :, cols] = res[z, SIDE + b].astype(BF16)


def output_blocks(tokens, weights, seqs):
    count, depth = tokens[0].shape
    cols = SIDE * weights[0].shape[0]
    out = jax.ShapeDtypeStruct((SIDE, SIDE, seqs, cols), BF16)
    return pl.pallas_call(
        functools.partial(output_body, seqs=seqs),
        in_specs=[VMEM] * 8,
        out_specs=[VMEM] * 2,
        out_shape=[out] * 2,
        scratch_shapes=[
            pltpu.VMEM((SIDE, count, depth), BF16),
            pltpu.VMEM((cols, depth), BF16),
        ],
        compiler_params=room(16),
        name="output_blocks",
    )(*tokens, *weights)


def total_body(a, b, c, o0, o1, o2, o3):
    for j, o in enumerate((o0, o1, o2, o3)):
        o[...] = (a[j].astype(F32) + b[j].astype(F32) + c[j].astype(F32)).astype(o.dtype)


def total_blocks(parts):
    out = jax.ShapeDtypeStruct(parts[0].shape[1:], BF16)
    return pl.pallas_call(
        total_body,
        in_specs=[VMEM] * 3,
        out_specs=[VMEM] * SIDE,
        out_shape=[out] * SIDE,
        compiler_params=room(8),
        name="total_blocks",
    )(*parts)


def columns_body(*refs):
    out = refs[-1]
    width = refs[0].shape[1]
    z = here()[0]
    for d, ref in enumerate(refs[:-1]):
        at = lax.rem(z + SIDE - d, SIDE) * width
        out[:, pl.ds(pl.multiple_of(at, 128), width)] = ref[...]


def join_columns(blocks):
    rows, width = blocks[0].shape
    return pl.pallas_call(
        columns_body,
        in_specs=[VMEM] * SIDE,
        out_specs=VMEM,
        out_shape=jax.ShapeDtypeStruct((rows, SIDE * width), BF16),
        compiler_params=room(8),
        name="join_columns",
    )(*blocks)


def settle_body(*refs):
    out = refs[-1]
    _, _, y, core = here()
    sign = 1 - 2 * core
    steps = [2 * v + core for v in turned(y, -sign)]
    steps += [2 * v + (1 - core) for v in turned(y, sign)]
    for step, ref in zip(steps, refs[:-1]):
        out[step] = ref[...]


def settle(blocks):
    return pl.pallas_call(
        settle_body,
        in_specs=[VMEM] * 8,
        out_specs=VMEM,
        out_shape=jax.ShapeDtypeStruct((8,) + blocks[0].shape, BF16),
        compiler_params=room(8),
        name="settle",
    )(*blocks)


def splits(seqs):
    table = []
    for rest in itertools.combinations(range(1, seqs), seqs // 2 - 1):
        mine = (0,) + rest
        table.append(mine + tuple(s for s in range(seqs) if s not in mine))
    return np.array(table, np.int32)


def balanced_order(lengths):
    seqs = lengths.shape[0]
    table = splits(seqs)
    member = np.zeros((table.shape[0], seqs), np.int32)
    for i, row in enumerate(table):
        member[i, row[: seqs // 2]] = 1
    blocks = lax.div(lengths + (BLOCK - 1), BLOCK)
    first = jnp.sum(member * blocks[None, :], axis=1)
    larger = jnp.maximum(first, jnp.sum(blocks) - first)
    index = np.arange(table.shape[0], dtype=np.int32)
    score = larger * table.shape[0] + index
    chosen = (score == jnp.min(score)).astype(jnp.int32)
    return jnp.sum(chosen[:, None] * table, axis=0)


def rotate(vector, position):
    half = vector.shape[-1] // 2
    index_f = jnp.arange(half, dtype=jnp.float32)
    frequency = jnp.exp(-math.log(10000.0) * 2.0 * index_f / vector.shape[-1])
    angle = position[..., None] * frequency
    first = vector[..., :half]
    second = vector[..., half:]
    cosine = jnp.cos(angle)
    sine = jnp.sin(angle)
    return jnp.concatenate(
        [first * cosine - second * sine, first * sine + second * cosine], axis=-1
    )


def body(
    grad_parts,
    params,
    moment_one,
    moment_two,
    query_latent,
    rope_weight,
    value_weight,
    out_weight,
    latent_cache,
    rope_cache,
    new_latent,
    new_rope,
    lengths,
):
    core = lax.rem(lax.axis_index("head"), 2)

    send, keep = pack(grad_parts[0])
    sums = add_pairs(keep, other_core(send), F32)
    parts = ring_sum(sums, "y")
    new_params, new_one, new_two, w = adam(parts, params, moment_one, moment_two)

    w_t = out_weight.T
    w_one, w_two = forth(w_t, "x"), back(w_t, "x")
    w_one, w = lax.optimization_barrier((w_one, w))

    above, below = first(w, 1), first(w, -1)
    top = stack_rows(w, above)
    bottom = stack_rows(below, first(above, 1))
    top_above, top_below = second(top, 1), second(top, -1)
    bottom_above, bottom_below = second(bottom, 1), second(bottom, -1)
    units = [top, bottom, top_above, bottom_above, top_below, bottom_below]
    units += [second(top_above, 1), second(bottom_below, -1)]
    out_weights = (w_t, w_one, w_two, forth(w_one, "x"))

    steps_n, seq_local, q_rank = query_latent.shape
    heads_local = value_weight.shape[1] // HDIM
    half = seq_local // 2
    lengths, _ = lax.optimization_barrier((lengths, sums[3]))
    order = balanced_order(lengths)
    order = jnp.where(core == 0, order, jnp.concatenate([order[half:], order[:half]]))
    chosen = order[:, None] == jnp.arange(seq_local, dtype=jnp.int32)[None, :]
    lengths_in = jnp.sum(jnp.where(chosen, lengths[None, :], 0), axis=1)
    chosen = chosen.astype(BF16)

    def arrange(which, arrays):
        return jnp.einsum("ps,tsq->ptq", which, arrays, preferred_element_type=F32).astype(BF16)

    by_seq = arrange(chosen, query_latent).reshape(seq_local * steps_n, q_rank)
    by_seq_late, rope_late, _ = lax.optimization_barrier((by_seq, rope_weight, bottom))
    query_rope = jnp.dot(by_seq_late, rope_late, preferred_element_type=F32).reshape(
        seq_local, steps_n, heads_local, ROPE
    )
    position = (lengths_in[:, None] + jnp.arange(steps_n, dtype=jnp.int32)[None, :]).astype(F32)[
        :, :, None
    ]
    query_rope = rotate(query_rope, position).astype(BF16)
    query_rope = jnp.transpose(query_rope, (0, 2, 1, 3)).reshape(
        seq_local, heads_local * steps_n, ROPE
    )
    r_own, r_got = query_rope[:half], other_core(query_rope[half:])
    pad = ((0, 0), (0, 128 - steps_n), (0, 0))
    nl = jnp.pad(arrange(chosen[:half], new_latent), pad)
    nr = jnp.pad(arrange(chosen[:half], new_rope), pad)

    w_rows = SIDE * SIDE * params.shape[0]
    q_own, q_send = queries(by_seq, units, w_rows, seq_local, q_rank)
    mixed, mixed_send = attention(
        order,
        lengths_in[:half],
        q_own,
        other_core(q_send),
        r_own,
        r_got,
        nl,
        nr,
        latent_cache,
        rope_cache,
        steps_n,
    )
    values = project_values(order, mixed, other_core(mixed_send), value_weight)

    send, keep = output_blocks(ring(values, "z"), out_weights, seq_local)
    parts = ring_sum(add_pairs(keep, other_core(send), BF16), "y")
    blocks = total_blocks(parts)

    arrived = [blocks[0]]
    for d in range(1, SIDE):
        perm = [
            (zz * SIDE + xx, ((zz + d) % SIDE) * SIDE + xx)
            for zz in range(SIDE)
            for xx in range(SIDE)
        ]
        arrived.append(lax.ppermute(blocks[d], "fsdp", perm))
    mine = join_columns(arrived)

    column = list(ring(mine, "y"))
    column += [other_core(b) for b in column]
    decoded = settle(column)
    return (new_params, new_one, new_two, decoded)


def solution(mesh):
    return jax.shard_map(
        body,
        mesh=mesh,
        in_specs=(
            P("head", "fsdp", None),
            P("fsdp", "head"),
            P("fsdp", "head"),
            P("fsdp", "head"),
            P(None, "fsdp", None),
            P(None, "head"),
            P(None, "head"),
            P("head", "fsdp"),
            P("fsdp", None, None),
            P("fsdp", None, None),
            P(None, "fsdp", None),
            P(None, "fsdp", None),
            P("fsdp"),
        ),
        out_specs=(P("fsdp", "head"), P("fsdp", "head"), P("fsdp", "head"), P(None, "fsdp", None)),
        check_vma=False,
    )
```

```python
import functools
import itertools
import math

import jax
import jax.numpy as jnp
import numpy as np
from jax import lax
from jax.experimental import pallas as pl
from jax.experimental.pallas import tpu as pltpu
from jax.sharding import PartitionSpec as P

HDIM = 128
ROPE = 64
SIDE = 4
BLOCK = 1024
SLOTS = 12
MIB = 1024 * 1024

first_fix = 1.0 - math.exp(100.0 * math.log(0.9))
second_fix = 1.0 - math.exp(100.0 * math.log(0.999))
NEG = -1e30
LOG2E = math.log2(math.e)

NT = (((1,), (1,)), ((), ()))
NN = (((1,), (0,)), ((), ()))


def dot(a, b, dims):
    return lax.dot_general(a, b, dims, preferred_element_type=jnp.float32)


def moves(step):
    perm = []
    for z in range(SIDE):
        for x in range(SIDE):
            for y in range(SIDE):
                for c in range(2):
                    axis, to_place = step(c)
                    to = {"x": x, "y": y, "z": z}
                    to[axis] = to_place(to[axis]) % SIDE
                    perm.append(
                        (
                            (z * SIDE + x) * 2 * SIDE + y * 2 + c,
                            (to["z"] * SIDE + to["x"]) * 2 * SIDE + to["y"] * 2 + c,
                        )
                    )
    return perm


def shift(v, step):
    return lax.ppermute(v, ("fsdp", "head"), moves(step))


def forth(v, axis):
    return shift(v, lambda c: (axis, lambda i: i + 1 - 2 * c))


def back(v, axis):
    return shift(v, lambda c: (axis, lambda i: i + 2 * c - 1))


def first(v, d):
    return shift(v, lambda c: (("x", "z")[c], lambda i: i + d))


def second(v, d):
    return shift(v, lambda c: (("z", "x")[c], lambda i: i + d))


NEAR = ((1, 3), (3, 1))


def swap(v, axis, turn):
    return shift(v, lambda c: (axis, lambda i: i ^ NEAR[c][turn]))


def other_core(v):
    return lax.ppermute(v, "head", [(i, i ^ 1) for i in range(2 * SIDE)])


def gather_pairs(own, axis):
    pair = stack_two(own, swap(own, axis, 0))
    return pair, swap(pair, axis, 1)


def here():
    f = lax.axis_index("fsdp")
    h = lax.axis_index("head")
    return lax.div(f, SIDE), lax.rem(f, SIDE), lax.div(h, 2), lax.rem(h, 2)


def near(core):
    return jnp.where(core == 0, 1, 3), jnp.where(core == 0, 3, 1)


def spots(base, core):
    one, two = near(core)
    return [base, base ^ two, base ^ one, base ^ 2]


VMEM = pl.BlockSpec(memory_space=pltpu.VMEM)
SMEM = pl.BlockSpec(memory_space=pltpu.SMEM)
HBM = pl.BlockSpec(memory_space=pltpu.HBM)
F32 = jnp.float32
BF16 = jnp.bfloat16


def room(mib):
    return pltpu.CompilerParams(vmem_limit_bytes=mib * MIB)


def stack_two_body(a, b, o):
    o[0] = a[...]
    o[1] = b[...]


def stack_two(a, b):
    return pl.pallas_call(
        stack_two_body,
        in_specs=[VMEM] * 2,
        out_specs=VMEM,
        out_shape=jax.ShapeDtypeStruct((2,) + a.shape, a.dtype),
        compiler_params=room(8),
        name="stack_two",
    )(a, b)


def add_last_body(a, b, o):
    o[...] = (a[...].astype(F32) + b[1].astype(F32)).astype(o.dtype)


def add_last(a, b):
    return pl.pallas_call(
        add_last_body,
        in_specs=[VMEM] * 2,
        out_specs=VMEM,
        out_shape=jax.ShapeDtypeStruct(a.shape, BF16),
        compiler_params=room(8),
        name="add_last",
    )(a, b)


def sum_pairs(own, second_sum, send, axis):
    got = swap(send, axis, 0)
    return own, got, swap(add_last(second_sum, got), axis, 1)


def pack_body(g_ref, o_ref):
    _, _, y, core = here()
    cols = o_ref.shape[2]
    for j, place in enumerate(spots(y, 1 - core)):
        at = pl.multiple_of((2 * place + 1 - core) * cols, 128)
        o_ref[j] = g_ref[:, pl.ds(at, cols)]


def pack(g):
    return pl.pallas_call(
        pack_body,
        in_specs=[VMEM],
        out_specs=VMEM,
        out_shape=jax.ShapeDtypeStruct((SIDE, g.shape[0], g.shape[1] // (2 * SIDE)), g.dtype),
        compiler_params=room(8),
        name="pack_columns",
    )(g)


def add_columns_body(g_ref, got, own, second_sum, send):
    _, _, y, core = here()
    rows, cols = own.shape
    places = spots(y, core)
    for j, ref in ((2, send.at[0]), (3, send.at[1]), (1, second_sum), (0, own)):
        at = pl.multiple_of((2 * places[j] + core) * cols, 128)
        for r in range(0, rows, 16):
            part = slice(r, r + 16)
            mine = g_ref[part, pl.ds(at, cols)].astype(F32)
            ref[part, :] = (mine + got[j, part, :].astype(F32)).astype(ref.dtype)


def add_columns(g, got):
    shape = got.shape[1:]
    return pl.pallas_call(
        add_columns_body,
        in_specs=[VMEM] * 2,
        out_specs=[VMEM] * 3,
        out_shape=[
            jax.ShapeDtypeStruct(shape, F32),
            jax.ShapeDtypeStruct(shape, BF16),
            jax.ShapeDtypeStruct((2,) + shape, BF16),
        ],
        compiler_params=room(8),
        name="add_columns",
    )(g, got)


def adam_body(r0, r1, r2, p, one, two, new_p, new_one, new_two, w):
    step_size = 0.003 / first_fix
    for r in range(0, p.shape[0], 16):
        part = slice(r, r + 16)
        grad = r0[part] + r1[0, part, :].astype(F32) + r2[part].astype(F32)
        moment = 0.9 * one[part] + 0.1 * grad
        second_moment = 0.999 * two[part] + 0.001 * grad * grad
        denom = jnp.sqrt(second_moment / second_fix) + 1e-08
        params = p[part] - step_size * moment / denom
        w[part] = params.astype(BF16)
        new_p[part] = params
        new_one[part] = moment
        new_two[part] = second_moment


def adam(parts, p, one, two):
    full = jax.ShapeDtypeStruct(p.shape, F32)
    return pl.pallas_call(
        adam_body,
        in_specs=[VMEM] * 6,
        out_specs=[VMEM] * 4,
        out_shape=[full] * 3 + [jax.ShapeDtypeStruct(p.shape, BF16)],
        compiler_params=room(12),
        name="adam",
    )(*parts, p, one, two)


def stack_body(a, b, out):
    rows = a.shape[0]
    out[:rows, :] = a[...]
    out[rows:, :] = b[...]


def stack_rows(a, b):
    rows, cols = a.shape
    return pl.pallas_call(
        stack_body,
        in_specs=[VMEM] * 2,
        out_specs=VMEM,
        out_shape=jax.ShapeDtypeStruct((2 * rows, cols), a.dtype),
        compiler_params=room(8),
        name="stack_rows",
    )(a, b)


def query_body(ql_ref, *refs, seqs, steps, heads, q_rank):
    units = refs[:8]
    keep_ref, send_ref, w_buf, lat_buf = refs[8:]
    z, x, _, core = here()
    shard = w_buf.shape[0] // (SIDE * SIDE)
    far = (0, SIDE - 1, 1, 2)
    for k in range(SIDE):
        for m in range(SIDE):
            zo = jnp.where(core == 0, far[k], far[m])
            xo = jnp.where(core == 0, far[m], far[k])
            f = lax.rem(z + zo, SIDE) * SIDE + lax.rem(x + xo, SIDE)
            at = pl.multiple_of(f * shard, shard)
            rows = slice((m % 2) * shard, (m % 2 + 1) * shard)
            w_buf[pl.ds(at, shard), :] = units[2 * k + m // 2][rows, :]
    nope = dot(ql_ref[...], w_buf[:q_rank, :], NN).astype(BF16)
    for h in range(heads):
        cols = slice(h * HDIM, (h + 1) * HDIM)
        lat = dot(nope[:, cols], w_buf[q_rank:, cols], NT)
        lat_buf[:, h * steps : (h + 1) * steps, :] = lat.reshape(seqs, steps, -1)
    keep_ref[...] = lat_buf[: seqs // 2].astype(BF16)
    send_ref[...] = lat_buf[seqs // 2 :].astype(BF16)


def queries(ql, units, w_rows, seqs, q_rank):
    cols = units[0].shape[1]
    heads = cols // HDIM
    steps = ql.shape[0] // seqs
    lat_rank = w_rows - q_rank
    out = jax.ShapeDtypeStruct((seqs // 2, heads * steps, lat_rank), BF16)
    return pl.pallas_call(
        functools.partial(query_body, seqs=seqs, steps=steps, heads=heads, q_rank=q_rank),
        in_specs=[VMEM] * 9,
        out_specs=[VMEM] * 2,
        out_shape=[out] * 2,
        scratch_shapes=[
            pltpu.VMEM((w_rows, cols), BF16),
            pltpu.VMEM((seqs, heads * steps, lat_rank), F32),
        ],
        compiler_params=room(16),
        name="queries",
    )(ql, *units)


def attention_body(
    order_ref,
    len_ref,
    q_own,
    q_got,
    r_own,
    r_got,
    nl_ref,
    nr_ref,
    lat_hbm,
    rope_hbm,
    keep_ref,
    send_ref,
    lat_buf,
    rope_buf,
    q_buf,
    qr_buf,
    acc,
    m_ref,
    l_ref,
    p0,
    p1,
    a0,
    a1,
    seq_of,
    blk_of,
    lat_sem,
    rope_sem,
    *,
    steps,
):
    seqs, rows, _ = q_buf.shape
    part = rows // 2
    factor = LOG2E / math.sqrt(HDIM + ROPE)

    def listing(s, at):
        blocks = lax.div(len_ref[s] + (BLOCK - 1), BLOCK)

        def put(j, at):
            seq_of[at] = s
            blk_of[at] = j
            return at + 1

        return lax.fori_loop(0, blocks, put, at)

    count = lax.fori_loop(0, seqs, listing, 0)

    def lat_copy(i):
        slot = lax.rem(i, SLOTS)
        start = pl.multiple_of(blk_of[i] * BLOCK, BLOCK)
        return pltpu.make_async_copy(
            lat_hbm.at[order_ref[seq_of[i]], pl.ds(start, BLOCK), :],
            lat_buf.at[slot],
            lat_sem.at[slot],
        )

    def rope_copy(i):
        slot = lax.rem(i, SLOTS)
        start = pl.multiple_of(blk_of[i] * BLOCK, BLOCK)
        return pltpu.make_async_copy(
            rope_hbm.at[order_ref[seq_of[i]], :, pl.ds(start, BLOCK)],
            rope_buf.at[slot],
            rope_sem.at[slot],
        )

    def fetch(i):
        @pl.when(i < count)
        def _():
            lat_copy(i).start()
            rope_copy(i).start()

    for i in range(SLOTS - 2):
        fetch(i)

    q_buf[:, :part, :] = q_own[...]
    q_buf[:, part:, :] = q_got[...]
    qr_buf[:, :part, :] = r_own[...]
    qr_buf[:, part:, :] = r_got[...]

    width = nl_ref.shape[1]
    token = lax.broadcasted_iota(jnp.int32, (rows, width), 1)
    step = lax.rem(lax.broadcasted_iota(jnp.int32, (rows, width), 0), steps)
    seen = token <= step
    for s in range(seqs):
        score = dot(q_buf[s], nl_ref[s], NT) + dot(qr_buf[s], nr_ref[s], NT)
        score = jnp.where(seen, score, NEG)
        top = jnp.max(score, axis=1, keepdims=True)
        prob = jnp.exp2((score - top) * factor)
        m_ref[s] = jnp.broadcast_to(top, (rows, 128))
        l_ref[s] = prob
        acc[s] = dot(prob.astype(BF16), nl_ref[s], NN)

    lane = lax.broadcasted_iota(jnp.int32, (rows, BLOCK), 1)

    def arrive(i):
        lat_copy(i).wait()
        rope_copy(i).wait()

    def scores(i):
        slot = lax.rem(i, SLOTS)
        s = seq_of[i]
        return dot(q_buf[s], lat_buf[slot], NT) + dot(qr_buf[s], rope_buf[slot], NN)

    def weigh(i, score, p_ref, a_ref):
        s = seq_of[i]
        score = jnp.where(lane < len_ref[s] - blk_of[i] * BLOCK, score, NEG)
        before = m_ref[s]
        top = jnp.maximum(before, jnp.max(score, axis=1, keepdims=True))
        prob = jnp.exp2((score - top[:, :1]) * factor)
        alpha = jnp.exp2((before - top) * factor)
        total = l_ref[s] * alpha
        for k in range(BLOCK // 128):
            total += prob[:, k * 128 : (k + 1) * 128]
        m_ref[s] = top
        l_ref[s] = total
        a_ref[...] = alpha
        p_ref[...] = prob.astype(BF16)

    def gather(i, p_ref, a_ref):
        slot = lax.rem(i, SLOTS)
        s = seq_of[i]
        acc[s] = acc[s] * a_ref[:, :1] + dot(p_ref[...], lat_buf[slot], NN)

    arrive(0)
    weigh(0, scores(0), p0, a0)

    def pair(k, carry):
        i = 2 * k
        fetch(i + SLOTS - 2)
        fetch(i + SLOTS - 1)
        arrive(i + 1)
        arrive(i + 2)
        odd = scores(i + 1)
        gather(i, p0, a0)
        even = scores(i + 2)
        weigh(i + 1, odd, p1, a1)
        gather(i + 1, p1, a1)
        weigh(i + 2, even, p0, a0)
        return carry

    pairs = lax.div(count - 1, 2)
    lax.fori_loop(0, pairs, pair, 0)

    @pl.when(2 * pairs + 1 < count)
    def _():
        arrive(2 * pairs + 1)
        odd = scores(2 * pairs + 1)
        gather(2 * pairs, p0, a0)
        weigh(2 * pairs + 1, odd, p1, a1)
        gather(2 * pairs + 1, p1, a1)

    @pl.when(2 * pairs + 1 >= count)
    def _():
        gather(2 * pairs, p0, a0)

    for s in range(seqs):
        mixed = (acc[s] / jnp.sum(l_ref[s], axis=1, keepdims=True)).astype(BF16)
        keep_ref[s] = mixed[:part]
        send_ref[s] = mixed[part:]


def attention(order, lengths, q_own, q_got, r_own, r_got, nl, nr, lat, rope, steps):
    seqs, part, lat_rank = q_own.shape
    rows = 2 * part
    most = seqs * (lat.shape[1] // BLOCK) + 1
    out = jax.ShapeDtypeStruct(q_own.shape, BF16)
    return pl.pallas_call(
        functools.partial(attention_body, steps=steps),
        in_specs=[SMEM, SMEM] + [VMEM] * 6 + [HBM] * 2,
        out_specs=[VMEM] * 2,
        out_shape=[out] * 2,
        scratch_shapes=[
            pltpu.VMEM((SLOTS, BLOCK, lat_rank), BF16),
            pltpu.VMEM((SLOTS, ROPE, BLOCK), BF16),
            pltpu.VMEM((seqs, rows, lat_rank), BF16),
            pltpu.VMEM((seqs, rows, ROPE), BF16),
            pltpu.VMEM((seqs, rows, lat_rank), F32),
            pltpu.VMEM((seqs, rows, 128), F32),
            pltpu.VMEM((seqs, rows, 128), F32),
            pltpu.VMEM((rows, BLOCK), BF16),
            pltpu.VMEM((rows, BLOCK), BF16),
            pltpu.VMEM((rows, 128), F32),
            pltpu.VMEM((rows, 128), F32),
            pltpu.SMEM((most,), jnp.int32),
            pltpu.SMEM((most,), jnp.int32),
            pltpu.SemaphoreType.DMA((SLOTS,)),
            pltpu.SemaphoreType.DMA((SLOTS,)),
        ],
        compiler_params=room(54),
        name="attention",
    )(order, lengths, q_own, q_got, r_own, r_got, nl, nr, lat, rope)


def values_body(order_ref, own, got, vw_ref, out_ref, mixed, flat):
    half, rows, lat_rank = own.shape
    seqs = 2 * half
    heads = vw_ref.shape[1] // HDIM
    steps = rows // heads
    mixed[:half] = own[...].astype(F32)
    mixed[half:] = got[...].astype(F32)
    for h in range(heads):
        cols = slice(h * HDIM, (h + 1) * HDIM)
        part = mixed[:, h * steps : (h + 1) * steps, :].reshape(seqs * steps, lat_rank)
        flat[:, cols] = dot(part.astype(BF16), vw_ref[:, cols], NN).astype(BF16)
    _, _, y, core = here()
    step_of = [2 * v + (1 - core) for v in spots(y, 1 - core)]
    step_of += [2 * v + core for v in spots(y, core)]
    count = seqs * steps
    row = lax.broadcasted_iota(jnp.int32, (count, count), 0)
    col = lax.broadcasted_iota(jnp.int32, (count, count), 1)
    want_step = jnp.zeros((count, count), jnp.int32)
    want_seq = jnp.zeros((count, count), jnp.int32)
    for k in range(steps):
        want_step = jnp.where(lax.div(row, seqs) == k, step_of[k], want_step)
    for k in range(seqs):
        want_seq = jnp.where(lax.div(col, steps) == k, order_ref[k], want_seq)
    same = (want_step == lax.rem(col, steps)) & (want_seq == lax.rem(row, seqs))
    pick = jnp.where(same, 1.0, 0.0).astype(BF16)
    out_ref[...] = dot(pick, flat[...], NN).astype(BF16)


def project_values(order, own, got, vw):
    half, rows, lat_rank = own.shape
    cols = vw.shape[1]
    count = 2 * half * rows * HDIM // cols
    return pl.pallas_call(
        values_body,
        in_specs=[SMEM] + [VMEM] * 3,
        out_specs=VMEM,
        out_shape=jax.ShapeDtypeStruct((count, cols), BF16),
        scratch_shapes=[
            pltpu.VMEM((2 * half, rows, lat_rank), F32),
            pltpu.VMEM((count, cols), BF16),
        ],
        compiler_params=room(12),
        name="project_values",
    )(order, own, got, vw)


def output_body(*refs, seqs):
    (pair, other), weights = refs[:2], refs[2:6]
    send_ref, keep_ref, v_buf, w_buf = refs[6:]
    _, x, _, core = here()
    one, two = near(core)
    v_buf[0] = pair[0]
    v_buf[one] = pair[1]
    v_buf[two] = other[0]
    v_buf[2] = other[1]
    sign = 1 - 2 * core
    depth = v_buf.shape[2]
    part = weights[0].shape[0]
    for k, offset in enumerate((0, SIDE - sign, SIDE + sign, 2)):
        at = pl.multiple_of(lax.rem(x + offset, SIDE) * part, 64)
        w_buf[pl.ds(at, part), :] = weights[k][...]
    tokens_all = v_buf[...].reshape(-1, depth)
    width = 256
    for n in range(w_buf.shape[0] // width):
        cols = slice(n * width, (n + 1) * width)
        res = dot(tokens_all, w_buf[cols, :], NT).reshape(SIDE, 2 * SIDE, seqs, width)
        for b in range(SIDE):
            for z in range(SIDE):
                send_ref[b, z, :, cols] = res[z, b].astype(BF16)
                keep_ref[b, z, :, cols] = res[z, SIDE + b].astype(BF16)


def output_blocks(tokens, weights, seqs):
    _, count, depth = tokens[0].shape
    cols = SIDE * weights[0].shape[0]
    out = jax.ShapeDtypeStruct((SIDE, SIDE, seqs, cols), BF16)
    return pl.pallas_call(
        functools.partial(output_body, seqs=seqs),
        in_specs=[VMEM] * 6,
        out_specs=[VMEM] * 2,
        out_shape=[out] * 2,
        scratch_shapes=[
            pltpu.VMEM((SIDE, count, depth), BF16),
            pltpu.VMEM((cols, depth), BF16),
        ],
        compiler_params=room(16),
        name="output_blocks",
    )(*tokens, *weights)


def add_blocks_body(keep, got, own, second_sum, send):
    for j, ref in ((2, send.at[0]), (3, send.at[1]), (1, second_sum), (0, own)):
        for k in range(SIDE):
            ref[k] = (keep[j, k].astype(F32) + got[j, k].astype(F32)).astype(ref.dtype)


def add_blocks(keep, got):
    one = jax.ShapeDtypeStruct(got.shape[1:], BF16)
    return pl.pallas_call(
        add_blocks_body,
        in_specs=[VMEM] * 2,
        out_specs=[VMEM] * 3,
        out_shape=[one, one, jax.ShapeDtypeStruct((2,) + got.shape[1:], BF16)],
        compiler_params=room(8),
        name="add_blocks",
    )(keep, got)


def total_body(a, b, c, own, second_out, send):
    one, two = near(here()[3])

    def total(k):
        return (a[k].astype(F32) + b[0, k].astype(F32) + c[k].astype(F32)).astype(BF16)

    send[0] = total(one)
    send[1] = total(2)
    second_out[...] = total(two)
    own[...] = total(0)


def total_blocks(parts):
    one = jax.ShapeDtypeStruct(parts[0].shape[1:], BF16)
    return pl.pallas_call(
        total_body,
        in_specs=[VMEM] * 3,
        out_specs=[VMEM] * 3,
        out_shape=[one, one, jax.ShapeDtypeStruct((2,) + one.shape, BF16)],
        compiler_params=room(8),
        name="total_blocks",
    )(*parts)


def pass_on_body(a, b, o):
    o[0] = a[...]
    o[1] = b[1]


def pass_on(a, b):
    return pl.pallas_call(
        pass_on_body,
        in_specs=[VMEM] * 2,
        out_specs=VMEM,
        out_shape=jax.ShapeDtypeStruct(b.shape, b.dtype),
        compiler_params=room(8),
        name="pass_on",
    )(a, b)


def columns_body(own, got, far, out):
    width = own.shape[1]
    z, _, _, core = here()
    here_z, two, one, opposite = spots(z, core)
    for place, block in (
        (here_z, own[...]),
        (one, got[0]),
        (two, far[0]),
        (opposite, far[1]),
    ):
        out[:, pl.ds(pl.multiple_of(place * width, 128), width)] = block


def join_columns(own, got, far):
    rows, width = own.shape
    return pl.pallas_call(
        columns_body,
        in_specs=[VMEM] * 3,
        out_specs=VMEM,
        out_shape=jax.ShapeDtypeStruct((rows, SIDE * width), BF16),
        compiler_params=room(8),
        name="join_columns",
    )(own, got, far)


def settle_body(pair, far, pair_other, far_other, out):
    _, _, y, core = here()
    for a, b, c in ((pair, far, core), (pair_other, far_other, 1 - core)):
        here_y, two, one, opposite = spots(y, c)
        out[2 * here_y + c] = a[0]
        out[2 * one + c] = a[1]
        out[2 * two + c] = b[0]
        out[2 * opposite + c] = b[1]


def settle(blocks):
    return pl.pallas_call(
        settle_body,
        in_specs=[VMEM] * 4,
        out_specs=VMEM,
        out_shape=jax.ShapeDtypeStruct((8,) + blocks[0].shape[1:], BF16),
        compiler_params=room(8),
        name="settle",
    )(*blocks)


def splits(seqs):
    table = []
    for rest in itertools.combinations(range(1, seqs), seqs // 2 - 1):
        mine = (0,) + rest
        table.append(mine + tuple(s for s in range(seqs) if s not in mine))
    return np.array(table, np.int32)


def balanced_order(lengths):
    seqs = lengths.shape[0]
    table = splits(seqs)
    member = np.zeros((table.shape[0], seqs), np.int32)
    for i, row in enumerate(table):
        member[i, row[: seqs // 2]] = 1
    blocks = lax.div(lengths + (BLOCK - 1), BLOCK)
    first = jnp.sum(member * blocks[None, :], axis=1)
    larger = jnp.maximum(first, jnp.sum(blocks) - first)
    index = np.arange(table.shape[0], dtype=np.int32)
    score = larger * table.shape[0] + index
    chosen = (score == jnp.min(score)).astype(jnp.int32)
    return jnp.sum(chosen[:, None] * table, axis=0)


def rotate(vector, position):
    half = vector.shape[-1] // 2
    index_f = jnp.arange(half, dtype=jnp.float32)
    frequency = jnp.exp(-math.log(10000.0) * 2.0 * index_f / vector.shape[-1])
    angle = position[..., None] * frequency
    first = vector[..., :half]
    second = vector[..., half:]
    cosine = jnp.cos(angle)
    sine = jnp.sin(angle)
    return jnp.concatenate(
        [first * cosine - second * sine, first * sine + second * cosine], axis=-1
    )


def body(
    grad_parts,
    params,
    moment_one,
    moment_two,
    query_latent,
    rope_weight,
    value_weight,
    out_weight,
    latent_cache,
    rope_cache,
    new_latent,
    new_rope,
    lengths,
):
    core = lax.rem(lax.axis_index("head"), 2)

    grad = grad_parts[0]
    own_sum, second_sum, send_sum = add_columns(grad, other_core(pack(grad)))
    parts = sum_pairs(own_sum, second_sum, send_sum, "y")
    new_params, new_one, new_two, w = adam(parts, params, moment_one, moment_two)

    w_t = out_weight.T
    w_one, w_two = forth(w_t, "x"), back(w_t, "x")

    above, below = first(w, 1), first(w, -1)
    top = stack_rows(w, above)
    bottom = stack_rows(below, first(above, 1))
    top_above, top_below = second(top, 1), second(top, -1)
    bottom_above, bottom_below = second(bottom, 1), second(bottom, -1)
    bottom_on, top_above = lax.optimization_barrier((bottom_above, top_above))
    units = [top, bottom, top_above, bottom_above, top_below, bottom_below]
    units += [second(top_below, -1), second(bottom_on, 1)]

    steps_n, seq_local, q_rank = query_latent.shape
    heads_local = value_weight.shape[1] // HDIM
    half = seq_local // 2
    lengths, _ = lax.optimization_barrier((lengths, send_sum))
    order = balanced_order(lengths)
    order = jnp.where(core == 0, order, jnp.concatenate([order[half:], order[:half]]))
    chosen = order[:, None] == jnp.arange(seq_local, dtype=jnp.int32)[None, :]
    lengths_in = jnp.sum(jnp.where(chosen, lengths[None, :], 0), axis=1)
    chosen = chosen.astype(BF16)

    def arrange(which, arrays):
        return jnp.einsum("ps,tsq->ptq", which, arrays, preferred_element_type=F32).astype(BF16)

    by_seq = arrange(chosen, query_latent).reshape(seq_local * steps_n, q_rank)
    by_seq_late, rope_late, _ = lax.optimization_barrier((by_seq, rope_weight, bottom))
    query_rope = jnp.dot(by_seq_late, rope_late, preferred_element_type=F32).reshape(
        seq_local, steps_n, heads_local, ROPE
    )
    position = (lengths_in[:, None] + jnp.arange(steps_n, dtype=jnp.int32)[None, :]).astype(F32)[
        :, :, None
    ]
    query_rope = rotate(query_rope, position).astype(BF16)
    query_rope = jnp.transpose(query_rope, (0, 2, 1, 3)).reshape(
        seq_local, heads_local * steps_n, ROPE
    )
    r_own, r_got = query_rope[:half], other_core(query_rope[half:])
    pad = ((0, 0), (0, 128 - steps_n), (0, 0))
    nl = jnp.pad(arrange(chosen[:half], new_latent), pad)
    nr = jnp.pad(arrange(chosen[:half], new_rope), pad)

    w_rows = SIDE * SIDE * params.shape[0]
    q_own, q_send = queries(by_seq, units, w_rows, seq_local, q_rank)
    w_one, q_send = lax.optimization_barrier((w_one, q_send))
    out_weights = (w_t, w_one, w_two, forth(w_one, "x"))
    mixed, mixed_send = attention(
        order,
        lengths_in[:half],
        q_own,
        other_core(q_send),
        r_own,
        r_got,
        nl,
        nr,
        latent_cache,
        rope_cache,
        steps_n,
    )
    values = project_values(order, mixed, other_core(mixed_send), value_weight)

    send, keep = output_blocks(gather_pairs(values, "z"), out_weights, seq_local)
    parts = sum_pairs(*add_blocks(keep, other_core(send)), "y")
    own, second_out, send = total_blocks(parts)

    got = swap(send, "z", 0)
    far = swap(pass_on(second_out, got), "z", 1)
    mine = join_columns(own, got, far)

    pair, far = gather_pairs(mine, "y")
    decoded = settle((pair, far, other_core(pair), other_core(far)))
    return (new_params, new_one, new_two, decoded)


def solution(mesh):
    return jax.shard_map(
        body,
        mesh=mesh,
        in_specs=(
            P("head", "fsdp", None),
            P("fsdp", "head"),
            P("fsdp", "head"),
            P("fsdp", "head"),
            P(None, "fsdp", None),
            P(None, "head"),
            P(None, "head"),
            P("head", "fsdp"),
            P("fsdp", None, None),
            P("fsdp", None, None),
            P(None, "fsdp", None),
            P(None, "fsdp", None),
            P("fsdp"),
        ),
        out_specs=(P("fsdp", "head"), P("fsdp", "head"), P("fsdp", "head"), P(None, "fsdp", None)),
        check_vma=False,
    )
```

```python
import functools
import itertools
import math

import jax
import jax.numpy as jnp
import numpy as np
from jax import lax
from jax.experimental import pallas as pl
from jax.experimental.pallas import tpu as pltpu
from jax.sharding import PartitionSpec as P

HDIM = 128
ROPE = 64
SIDE = 4
BLOCK = 1024
SLOTS = 12
MIB = 1024 * 1024

first_fix = 1.0 - math.exp(100.0 * math.log(0.9))
second_fix = 1.0 - math.exp(100.0 * math.log(0.999))
NEG = -1e30
LOG2E = math.log2(math.e)

NT = (((1,), (1,)), ((), ()))
NN = (((1,), (0,)), ((), ()))


def dot(a, b, dims):
    return lax.dot_general(a, b, dims, preferred_element_type=jnp.float32)


def moves(step):
    perm = []
    for z in range(SIDE):
        for x in range(SIDE):
            for y in range(SIDE):
                for c in range(2):
                    axis, to_place = step(c)
                    to = {"x": x, "y": y, "z": z}
                    to[axis] = to_place(to[axis]) % SIDE
                    perm.append(
                        (
                            (z * SIDE + x) * 2 * SIDE + y * 2 + c,
                            (to["z"] * SIDE + to["x"]) * 2 * SIDE + to["y"] * 2 + c,
                        )
                    )
    return perm


def shift(v, step):
    return lax.ppermute(v, ("fsdp", "head"), moves(step))


def forth(v, axis):
    return shift(v, lambda c: (axis, lambda i: i + 1 - 2 * c))


def back(v, axis):
    return shift(v, lambda c: (axis, lambda i: i + 2 * c - 1))


def first(v, d):
    return shift(v, lambda c: (("x", "z")[c], lambda i: i + d))


def second(v, d):
    return shift(v, lambda c: (("z", "x")[c], lambda i: i + d))


def other_core(v):
    return lax.ppermute(v, "head", [(i, i ^ 1) for i in range(2 * SIDE)])


def ring(own, axis):
    one = forth(own, axis)
    two = back(own, axis)
    return own, one, two, forth(one, axis)


def ring_sum(blocks, axis):
    far = forth(blocks[2], axis)
    two = back(blocks[1], axis)
    return forth(add_two(blocks[0], far), axis), two


def here():
    f = lax.axis_index("fsdp")
    h = lax.axis_index("head")
    return lax.div(f, SIDE), lax.rem(f, SIDE), lax.div(h, 2), lax.rem(h, 2)


def turned(base, s):
    return [lax.rem(base + d, SIDE) for d in (0, SIDE + s, SIDE - s, 2)]


VMEM = pl.BlockSpec(memory_space=pltpu.VMEM)
SMEM = pl.BlockSpec(memory_space=pltpu.SMEM)
HBM = pl.BlockSpec(memory_space=pltpu.HBM)
F32 = jnp.float32
BF16 = jnp.bfloat16


def in_hbm(v):
    return pltpu.with_memory_space_constraint(v, pltpu.HBM)


def room(mib):
    return pltpu.CompilerParams(vmem_limit_bytes=mib * MIB)


def add_two_body(a, b, o):
    o[...] = (a[...].astype(F32) + b[...].astype(F32)).astype(o.dtype)


def add_two(a, b):
    return pl.pallas_call(
        add_two_body,
        in_specs=[VMEM] * 2,
        out_specs=VMEM,
        out_shape=jax.ShapeDtypeStruct(a.shape, BF16),
        compiler_params=room(8),
        name="add_two",
    )(a, b)


def pack_body(g_ref, p, one, two, send_ref, keep_ref, p_out, one_out, two_out, sem):
    _, _, y, core = here()
    sign = 1 - 2 * core
    cols = send_ref.shape[2]
    copies = []
    for ref, places, c in (
        (send_ref, turned(y, -sign), 1 - core),
        (keep_ref, turned(y, sign), core),
    ):
        for j, place in enumerate(places):
            at = pl.multiple_of((2 * place + c) * cols, 128)
            copies.append(
                pltpu.make_async_copy(
                    g_ref.at[:, pl.ds(at, cols)], ref.at[j], sem.at[len(copies)]
                )
            )
    for src, dst in ((p, p_out), (one, one_out), (two, two_out)):
        copies.append(pltpu.make_async_copy(src, dst, sem.at[len(copies)]))
    for copy in copies:
        copy.start()
    for copy in copies:
        copy.wait()


def pack(g, p, one, two):
    out = jax.ShapeDtypeStruct((SIDE, g.shape[0], g.shape[1] // (2 * SIDE)), g.dtype)
    return pl.pallas_call(
        pack_body,
        in_specs=[HBM] * 4,
        out_specs=[VMEM] * 5,
        out_shape=[out] * 2 + [jax.ShapeDtypeStruct(p.shape, F32)] * 3,
        scratch_shapes=[pltpu.SemaphoreType.DMA((2 * SIDE + 3,))],
        compiler_params=room(8),
        name="pack_columns",
    )(*(in_hbm(v) for v in (g, p, one, two)))


def add_columns_body(keep, got, own, *parts):
    rows, cols = own.shape
    width = cols // 2
    for j in (3, 2, 1, 0):
        for r in range(0, rows, 16):
            part = slice(r, r + 16)
            total = keep[j, part, :].astype(F32) + got[j, part, :].astype(F32)
            if j == 0:
                own[part, :] = total
            else:
                parts[j - 1][part, :] = total[:, :width].astype(BF16)
                parts[j + 2][part, :] = total[:, width:].astype(BF16)


def add_columns(keep, got):
    rows, cols = got.shape[1:]
    half = jax.ShapeDtypeStruct((rows, cols // 2), BF16)
    return pl.pallas_call(
        add_columns_body,
        in_specs=[VMEM] * 2,
        out_specs=[VMEM] * 7,
        out_shape=[jax.ShapeDtypeStruct((rows, cols), F32)] + [half] * 6,
        compiler_params=room(8),
        name="add_columns",
    )(keep, got)


def adam_step(grad, p, one, two):
    step_size = 0.003 / first_fix
    moment = 0.9 * one + 0.1 * grad
    second_moment = 0.999 * two + 0.001 * grad * grad
    denom = jnp.sqrt(second_moment / second_fix) + 1e-08
    return p - step_size * moment / denom, moment, second_moment


def adam_first_body(r0, r1, r2, p, one, two, w):
    width = w.shape[1]
    cols = slice(0, width)
    for r in range(0, p.shape[0], 16):
        part = slice(r, r + 16)
        grad = r0[part, cols] + r1[part].astype(F32) + r2[part].astype(F32)
        w[part] = adam_step(grad, p[part, cols], one[part, cols], two[part, cols])[0].astype(BF16)


def adam_first(own, parts, p, one, two):
    rows, cols = p.shape
    return pl.pallas_call(
        adam_first_body,
        in_specs=[VMEM] * 6,
        out_specs=VMEM,
        out_shape=jax.ShapeDtypeStruct((rows, cols // 2), BF16),
        compiler_params=room(12),
        name="adam_first",
    )(own, *parts, p, one, two)


def adam_body(r0, a1, a2, b1, b2, p, one, two, after, new_p, new_one, new_two, w):
    del after
    width = w.shape[1]
    for r in range(0, p.shape[0], 16):
        part = slice(r, r + 16)
        for k, (r1, r2) in ((1, (b1, b2)), (0, (a1, a2))):
            cols = slice(k * width, (k + 1) * width)
            grad = r0[part, cols] + r1[part].astype(F32) + r2[part].astype(F32)
            params, moment, second_moment = adam_step(
                grad, p[part, cols], one[part, cols], two[part, cols]
            )
            if k:
                w[part] = params.astype(BF16)
            new_p[part, cols] = params
            new_one[part, cols] = moment
            new_two[part, cols] = second_moment


def adam(own, parts, p, one, two, after):
    rows, cols = p.shape
    full = jax.ShapeDtypeStruct(p.shape, F32)
    return pl.pallas_call(
        adam_body,
        in_specs=[VMEM] * 8 + [pl.BlockSpec(memory_space=pl.ANY)],
        out_specs=[VMEM] * 4,
        out_shape=[full] * 3 + [jax.ShapeDtypeStruct((rows, cols // 2), BF16)],
        compiler_params=room(12),
        name="adam",
    )(own, *parts, p, one, two, after)


def stack_body(*refs):
    out = refs[-1]
    rows = refs[0].shape[0]
    for k, ref in enumerate(refs[:-1]):
        out[k * rows : (k + 1) * rows, :] = ref[...]


def stack_rows(*blocks):
    rows, cols = blocks[0].shape
    return pl.pallas_call(
        stack_body,
        in_specs=[VMEM] * len(blocks),
        out_specs=VMEM,
        out_shape=jax.ShapeDtypeStruct((len(blocks) * rows, cols), blocks[0].dtype),
        compiler_params=room(8),
        name="stack_rows",
    )(*blocks)


def spread(w, d, also=()):
    above, below = first(w, 1), first(w, -1)
    unit = stack_rows(w, above, below, first(above if d > 0 else below, d))
    unit, *also = lax.optimization_barrier((unit,) + tuple(also))
    up, down = second(unit, 1), second(unit, -1)
    return also, [unit, up, down, second(up if d > 0 else down, d)]


def query_body(ql_ref, *refs, seqs, steps, heads, q_rank):
    units = refs[:8]
    keep_ref, send_ref, w_buf, lat_buf = refs[8:]
    z, x, _, core = here()
    shard = w_buf.shape[0] // (SIDE * SIDE)
    far = (0, SIDE - 1, 1, 2)
    width = w_buf.shape[1] // 2
    for k in range(SIDE):
        for m in range(SIDE):
            zo = jnp.where(core == 0, far[k], far[m])
            xo = jnp.where(core == 0, far[m], far[k])
            f = lax.rem(z + zo, SIDE) * SIDE + lax.rem(x + xo, SIDE)
            at = pl.multiple_of(f * shard, shard)
            rows = slice(m * shard, (m + 1) * shard)
            for h in range(2):
                cols = slice(h * width, (h + 1) * width)
                w_buf[pl.ds(at, shard), cols] = units[4 * h + k][rows, :]
    nope = dot(ql_ref[...], w_buf[:q_rank, :], NN).astype(BF16)
    for h in range(heads):
        cols = slice(h * HDIM, (h + 1) * HDIM)
        lat = dot(nope[:, cols], w_buf[q_rank:, cols], NT)
        lat_buf[:, h * steps : (h + 1) * steps, :] = lat.reshape(seqs, steps, -1)
    keep_ref[...] = lat_buf[: seqs // 2].astype(BF16)
    send_ref[...] = lat_buf[seqs // 2 :].astype(BF16)


def queries(ql, units, w_rows, seqs, q_rank):
    cols = 2 * units[0].shape[1]
    heads = cols // HDIM
    steps = ql.shape[0] // seqs
    lat_rank = w_rows - q_rank
    out = jax.ShapeDtypeStruct((seqs // 2, heads * steps, lat_rank), BF16)
    return pl.pallas_call(
        functools.partial(query_body, seqs=seqs, steps=steps, heads=heads, q_rank=q_rank),
        in_specs=[VMEM] * 9,
        out_specs=[VMEM] * 2,
        out_shape=[out] * 2,
        scratch_shapes=[
            pltpu.VMEM((w_rows, cols), BF16),
            pltpu.VMEM((seqs, heads * steps, lat_rank), F32),
        ],
        compiler_params=room(16),
        name="queries",
    )(ql, *units)


def attention_body(
    order_ref,
    len_ref,
    q_own,
    q_got,
    r_own,
    r_got,
    nl_ref,
    nr_ref,
    lat_hbm,
    rope_hbm,
    keep_ref,
    send_ref,
    lat_buf,
    rope_buf,
    q_buf,
    qr_buf,
    acc,
    m_ref,
    l_ref,
    p0,
    p1,
    a0,
    a1,
    seq_of,
    blk_of,
    lat_sem,
    rope_sem,
    *,
    steps,
):
    seqs, rows, _ = q_buf.shape
    part = rows // 2
    factor = LOG2E / math.sqrt(HDIM + ROPE)

    def listing(s, at):
        blocks = lax.div(len_ref[s] + (BLOCK - 1), BLOCK)

        def put(j, at):
            seq_of[at] = s
            blk_of[at] = j
            return at + 1

        return lax.fori_loop(0, blocks, put, at)

    count = lax.fori_loop(0, seqs, listing, 0)

    def lat_copy(i):
        slot = lax.rem(i, SLOTS)
        start = pl.multiple_of(blk_of[i] * BLOCK, BLOCK)
        return pltpu.make_async_copy(
            lat_hbm.at[order_ref[seq_of[i]], pl.ds(start, BLOCK), :],
            lat_buf.at[slot],
            lat_sem.at[slot],
        )

    def rope_copy(i):
        slot = lax.rem(i, SLOTS)
        start = pl.multiple_of(blk_of[i] * BLOCK, BLOCK)
        return pltpu.make_async_copy(
            rope_hbm.at[order_ref[seq_of[i]], :, pl.ds(start, BLOCK)],
            rope_buf.at[slot],
            rope_sem.at[slot],
        )

    def fetch(i):
        @pl.when(i < count)
        def _():
            lat_copy(i).start()
            rope_copy(i).start()

    for i in range(SLOTS - 2):
        fetch(i)

    q_buf[:, :part, :] = q_own[...]
    q_buf[:, part:, :] = q_got[...]
    qr_buf[:, :part, :] = r_own[...]
    qr_buf[:, part:, :] = r_got[...]

    width = nl_ref.shape[1]
    token = lax.broadcasted_iota(jnp.int32, (rows, width), 1)
    step = lax.rem(lax.broadcasted_iota(jnp.int32, (rows, width), 0), steps)
    seen = token <= step
    for s in range(seqs):
        score = dot(q_buf[s], nl_ref[s], NT) + dot(qr_buf[s], nr_ref[s], NT)
        score = jnp.where(seen, score, NEG)
        top = jnp.max(score, axis=1, keepdims=True)
        prob = jnp.exp2((score - top) * factor)
        m_ref[s] = jnp.broadcast_to(top, (rows, 128))
        l_ref[s] = prob
        acc[s] = dot(prob.astype(BF16), nl_ref[s], NN)

    lane = lax.broadcasted_iota(jnp.int32, (rows, BLOCK), 1)

    def arrive(i):
        lat_copy(i).wait()
        rope_copy(i).wait()

    def scores(i):
        slot = lax.rem(i, SLOTS)
        s = seq_of[i]
        return dot(q_buf[s], lat_buf[slot], NT) + dot(qr_buf[s], rope_buf[slot], NN)

    def weigh(i, score, p_ref, a_ref):
        s = seq_of[i]
        score = jnp.where(lane < len_ref[s] - blk_of[i] * BLOCK, score, NEG)
        before = m_ref[s]
        top = jnp.maximum(before, jnp.max(score, axis=1, keepdims=True))
        prob = jnp.exp2((score - top[:, :1]) * factor)
        alpha = jnp.exp2((before - top) * factor)
        total = l_ref[s] * alpha
        for k in range(BLOCK // 128):
            total += prob[:, k * 128 : (k + 1) * 128]
        m_ref[s] = top
        l_ref[s] = total
        a_ref[...] = alpha
        p_ref[...] = prob.astype(BF16)

    def gather(i, p_ref, a_ref):
        slot = lax.rem(i, SLOTS)
        s = seq_of[i]
        acc[s] = acc[s] * a_ref[:, :1] + dot(p_ref[...], lat_buf[slot], NN)

    arrive(0)
    weigh(0, scores(0), p0, a0)

    def pair(k, carry):
        i = 2 * k
        fetch(i + SLOTS - 2)
        fetch(i + SLOTS - 1)
        arrive(i + 1)
        arrive(i + 2)
        odd = scores(i + 1)
        gather(i, p0, a0)
        even = scores(i + 2)
        weigh(i + 1, odd, p1, a1)
        gather(i + 1, p1, a1)
        weigh(i + 2, even, p0, a0)
        return carry

    pairs = lax.div(count - 1, 2)
    lax.fori_loop(0, pairs, pair, 0)

    @pl.when(2 * pairs + 1 < count)
    def _():
        arrive(2 * pairs + 1)
        odd = scores(2 * pairs + 1)
        gather(2 * pairs, p0, a0)
        weigh(2 * pairs + 1, odd, p1, a1)
        gather(2 * pairs + 1, p1, a1)

    @pl.when(2 * pairs + 1 >= count)
    def _():
        gather(2 * pairs, p0, a0)

    for s in range(seqs):
        mixed = (acc[s] / jnp.sum(l_ref[s], axis=1, keepdims=True)).astype(BF16)
        keep_ref[s] = mixed[:part]
        send_ref[s] = mixed[part:]


def attention(order, lengths, q_own, q_got, r_own, r_got, nl, nr, lat, rope, steps):
    seqs, part, lat_rank = q_own.shape
    rows = 2 * part
    most = seqs * (lat.shape[1] // BLOCK) + 1
    out = jax.ShapeDtypeStruct(q_own.shape, BF16)
    return pl.pallas_call(
        functools.partial(attention_body, steps=steps),
        in_specs=[SMEM, SMEM] + [VMEM] * 6 + [HBM] * 2,
        out_specs=[VMEM] * 2,
        out_shape=[out] * 2,
        scratch_shapes=[
            pltpu.VMEM((SLOTS, BLOCK, lat_rank), BF16),
            pltpu.VMEM((SLOTS, ROPE, BLOCK), BF16),
            pltpu.VMEM((seqs, rows, lat_rank), BF16),
            pltpu.VMEM((seqs, rows, ROPE), BF16),
            pltpu.VMEM((seqs, rows, lat_rank), F32),
            pltpu.VMEM((seqs, rows, 128), F32),
            pltpu.VMEM((seqs, rows, 128), F32),
            pltpu.VMEM((rows, BLOCK), BF16),
            pltpu.VMEM((rows, BLOCK), BF16),
            pltpu.VMEM((rows, 128), F32),
            pltpu.VMEM((rows, 128), F32),
            pltpu.SMEM((most,), jnp.int32),
            pltpu.SMEM((most,), jnp.int32),
            pltpu.SemaphoreType.DMA((SLOTS,)),
            pltpu.SemaphoreType.DMA((SLOTS,)),
        ],
        compiler_params=room(40),
        name="attention",
    )(order, lengths, q_own, q_got, r_own, r_got, nl, nr, in_hbm(lat), in_hbm(rope))


def values_body(order_ref, own, got, vw_ref, out_ref, mixed, flat):
    half, rows, lat_rank = own.shape
    seqs = 2 * half
    heads = vw_ref.shape[1] // HDIM
    steps = rows // heads
    mixed[:half] = own[...].astype(F32)
    mixed[half:] = got[...].astype(F32)
    for h in range(heads):
        cols = slice(h * HDIM, (h + 1) * HDIM)
        part = mixed[:, h * steps : (h + 1) * steps, :].reshape(seqs * steps, lat_rank)
        flat[:, cols] = dot(part.astype(BF16), vw_ref[:, cols], NN).astype(BF16)
    _, _, y, core = here()
    sign = 1 - 2 * core
    step_of = [2 * v + (1 - core) for v in turned(y, -sign)]
    step_of += [2 * v + core for v in turned(y, sign)]
    count = seqs * steps
    row = lax.broadcasted_iota(jnp.int32, (count, count), 0)
    col = lax.broadcasted_iota(jnp.int32, (count, count), 1)
    want_step = jnp.zeros((count, count), jnp.int32)
    want_seq = jnp.zeros((count, count), jnp.int32)
    for k in range(steps):
        want_step = jnp.where(lax.div(row, seqs) == k, step_of[k], want_step)
    for k in range(seqs):
        want_seq = jnp.where(lax.div(col, steps) == k, order_ref[k], want_seq)
    same = (want_step == lax.rem(col, steps)) & (want_seq == lax.rem(row, seqs))
    pick = jnp.where(same, 1.0, 0.0).astype(BF16)
    out_ref[...] = dot(pick, flat[...], NN).astype(BF16)


def project_values(order, own, got, vw):
    half, rows, lat_rank = own.shape
    cols = vw.shape[1]
    count = 2 * half * rows * HDIM // cols
    return pl.pallas_call(
        values_body,
        in_specs=[SMEM] + [VMEM] * 3,
        out_specs=VMEM,
        out_shape=jax.ShapeDtypeStruct((count, cols), BF16),
        scratch_shapes=[
            pltpu.VMEM((2 * half, rows, lat_rank), F32),
            pltpu.VMEM((count, cols), BF16),
        ],
        compiler_params=room(12),
        name="project_values",
    )(order, own, got, vw)


def output_body(*refs, seqs):
    tokens, weights = refs[:4], refs[4:8]
    send_ref, keep_ref, v_buf, w_buf = refs[8:]
    _, x, _, core = here()
    sign = 1 - 2 * core
    v_buf[0] = tokens[0][...]
    v_buf[lax.rem(SIDE - sign, SIDE)] = tokens[1][...]
    v_buf[lax.rem(SIDE + sign, SIDE)] = tokens[2][...]
    v_buf[2] = tokens[3][...]
    depth = v_buf.shape[2]
    part = weights[0].shape[0]
    for k, offset in enumerate((0, SIDE - sign, SIDE + sign, 2)):
        at = pl.multiple_of(lax.rem(x + offset, SIDE) * part, 64)
        w_buf[pl.ds(at, part), :] = weights[k][...]
    tokens_all = v_buf[...].reshape(-1, depth)
    width = 256
    for n in range(w_buf.shape[0] // width):
        cols = slice(n * width, (n + 1) * width)
        res = dot(tokens_all, w_buf[cols, :], NT).reshape(SIDE, 2 * SIDE, seqs, width)
        for b in range(SIDE):
            for z in range(SIDE):
                send_ref[b, z, :, cols] = res[z, b].astype(BF16)
                keep_ref[b, z, :, cols] = res[z, SIDE + b].astype(BF16)


def output_blocks(tokens, weights, seqs):
    count, depth = tokens[0].shape
    cols = SIDE * weights[0].shape[0]
    out = jax.ShapeDtypeStruct((SIDE, SIDE, seqs, cols), BF16)
    return pl.pallas_call(
        functools.partial(output_body, seqs=seqs),
        in_specs=[VMEM] * 8,
        out_specs=[VMEM] * 2,
        out_shape=[out] * 2,
        scratch_shapes=[
            pltpu.VMEM((SIDE, count, depth), BF16),
            pltpu.VMEM((cols, depth), BF16),
        ],
        compiler_params=room(16),
        name="output_blocks",
    )(*tokens, *weights)


def add_blocks_body(keep, got, *outs):
    for j in (3, 2, 1, 0):
        for k in range(SIDE):
            outs[j][k] = (keep[j, k].astype(F32) + got[j, k].astype(F32)).astype(BF16)


def add_blocks(keep, got):
    one = jax.ShapeDtypeStruct(got.shape[1:], BF16)
    return pl.pallas_call(
        add_blocks_body,
        in_specs=[VMEM] * 2,
        out_specs=[VMEM] * 4,
        out_shape=[one] * 4,
        compiler_params=room(8),
        name="add_blocks",
    )(keep, got)


def total_body(a, b, c, *outs):
    for k in (2, 1, 3, 0):
        outs[k][...] = (a[k].astype(F32) + b[k].astype(F32) + c[k].astype(F32)).astype(BF16)


def total_blocks(parts):
    one = jax.ShapeDtypeStruct(parts[0].shape[1:], BF16)
    return pl.pallas_call(
        total_body,
        in_specs=[VMEM] * 3,
        out_specs=[VMEM] * 4,
        out_shape=[one] * 4,
        compiler_params=room(8),
        name="total_blocks",
    )(*parts)


def columns_body(*refs):
    out = refs[-1]
    width = refs[0].shape[1]
    z = here()[0]
    for d, ref in enumerate(refs[:-1]):
        at = lax.rem(z + SIDE - d, SIDE) * width
        out[:, pl.ds(pl.multiple_of(at, 128), width)] = ref[...]


def join_columns(blocks):
    rows, width = blocks[0].shape
    return pl.pallas_call(
        columns_body,
        in_specs=[VMEM] * SIDE,
        out_specs=VMEM,
        out_shape=jax.ShapeDtypeStruct((rows, SIDE * width), BF16),
        compiler_params=room(8),
        name="join_columns",
    )(*blocks)


def settle_body(*refs):
    out = refs[-1]
    _, _, y, core = here()
    sign = 1 - 2 * core
    steps = [2 * v + core for v in turned(y, -sign)]
    steps += [2 * v + (1 - core) for v in turned(y, sign)]
    for step, ref in zip(steps, refs[:-1]):
        out[step] = ref[...]


def settle(blocks):
    return pl.pallas_call(
        settle_body,
        in_specs=[VMEM] * 8,
        out_specs=VMEM,
        out_shape=jax.ShapeDtypeStruct((8,) + blocks[0].shape, BF16),
        compiler_params=room(8),
        name="settle",
    )(*blocks)


def splits(seqs):
    for rest in itertools.combinations(range(1, seqs), seqs // 2 - 1):
        mine = (0,) + rest
        yield mine + tuple(s for s in range(seqs) if s not in mine)


def prepare_body(
    len_ref,
    ql_ref,
    rw_ref,
    nl_ref,
    nr_ref,
    order_ref,
    length_ref,
    by_seq_ref,
    r_own,
    r_send,
    nl_out,
    nr_out,
    r_buf,
    *,
    core_of,
):
    core = core_of()
    steps, seqs, q_rank = ql_ref.shape
    half = seqs // 2
    count = steps * seqs

    blocks = [lax.div(len_ref[s] + (BLOCK - 1), BLOCK) for s in range(seqs)]
    whole = sum(blocks[1:], blocks[0])
    least, code = None, None
    for row in splits(seqs):
        part = blocks[0] + blocks[row[1]] + blocks[row[2]] + blocks[row[3]]
        larger = jnp.maximum(part, whole - part)
        digits = sum(s << (3 * k) for k, s in enumerate(row))
        if least is None:
            least, code = larger, jnp.int32(digits)
        else:
            code = jnp.where(larger < least, digits, code)
            least = jnp.minimum(larger, least)
    order, lengths = [], []
    for k in range(seqs):
        shift_by = jnp.where(core == 0, 3 * k, 3 * ((k + half) % seqs))
        order.append(lax.shift_right_logical(code, shift_by) & 7)
        lengths.append(len_ref[order[k]])
        order_ref[k] = order[k]
        length_ref[k] = lengths[k]

    def by_place(place, values):
        out = jnp.zeros(place.shape, jnp.int32)
        for k, value in enumerate(values):
            out = jnp.where(place == k, value, out)
        return out

    def pick(rows, depth, used):
        row = lax.broadcasted_iota(jnp.int32, (rows, count), 0)
        col = lax.broadcasted_iota(jnp.int32, (rows, count), 1)
        same = (by_place(lax.div(row, depth), order[:used]) == lax.rem(col, seqs)) & (
            lax.rem(row, depth) == lax.div(col, seqs)
        )
        return jnp.where(same, 1.0, 0.0).astype(BF16)

    by_seq = dot(pick(count, steps, seqs), ql_ref[...].reshape(count, q_rank), NN).astype(BF16)
    by_seq_ref[...] = by_seq

    turn = dot(by_seq, rw_ref[...], NN)
    cols = turn.shape[1]
    row = lax.broadcasted_iota(jnp.int32, (count, 128), 0)
    lane = lax.broadcasted_iota(jnp.int32, (count, 128), 1)
    position = (by_place(lax.div(row, steps), lengths) + lax.rem(row, steps)).astype(F32)
    index_f = lax.rem(lane, ROPE // 2).astype(F32)
    angle = position * jnp.exp(-math.log(10000.0) * 2.0 * index_f / ROPE)
    is_first = lax.rem(lane, ROPE) < ROPE // 2
    cosine = jnp.concatenate([jnp.cos(angle)] * (cols // 128), axis=1)
    sine = jnp.sin(angle)
    sine = jnp.concatenate([jnp.where(is_first, -sine, sine)] * (cols // 128), axis=1)
    is_first = lax.rem(lax.broadcasted_iota(jnp.int32, (count, cols), 1), ROPE) < ROPE // 2
    other = jnp.where(
        is_first,
        pltpu.roll(turn, cols - ROPE // 2, 1),
        pltpu.roll(turn, ROPE // 2, 1),
    )
    turn = turn * cosine + other * sine
    for h in range(cols // ROPE):
        piece = turn[:, h * ROPE : (h + 1) * ROPE].reshape(seqs, steps, ROPE)
        r_buf[:, h * steps : (h + 1) * steps, :] = piece
    r_own[...] = r_buf[:half].astype(BF16)
    r_send[...] = r_buf[half:].astype(BF16)

    width = nl_out.shape[1]
    chosen = pick(half * width, width, half)
    for src, out in ((nl_ref, nl_out), (nr_ref, nr_out)):
        rank = src.shape[2]
        rows = dot(chosen, src[...].reshape(count, rank), NN).astype(BF16)
        out[...] = rows.reshape(half, width, rank)


def prepare(lengths, ql, rw, nl, nr, core_of):
    steps, seqs, q_rank = ql.shape
    half = seqs // 2
    rows = rw.shape[1] // ROPE * steps
    turned_rows = jax.ShapeDtypeStruct((half, rows, ROPE), BF16)
    return pl.pallas_call(
        functools.partial(prepare_body, core_of=core_of),
        in_specs=[SMEM] + [VMEM] * 4,
        out_specs=[SMEM] * 2 + [VMEM] * 5,
        out_shape=[jax.ShapeDtypeStruct((seqs,), jnp.int32)] * 2
        + [jax.ShapeDtypeStruct((steps * seqs, q_rank), BF16)]
        + [turned_rows] * 2
        + [jax.ShapeDtypeStruct((half, 128, v.shape[2]), BF16) for v in (nl, nr)],
        scratch_shapes=[pltpu.VMEM((seqs, rows, ROPE), F32)],
        compiler_params=room(12),
        name="prepare",
    )(lengths, ql, rw, nl, nr)


def body(
    grad_parts,
    params,
    moment_one,
    moment_two,
    query_latent,
    rope_weight,
    value_weight,
    out_weight,
    latent_cache,
    rope_cache,
    new_latent,
    new_rope,
    lengths,
):
    send, keep, params, moment_one, moment_two = pack(
        grad_parts[0], params, moment_one, moment_two
    )
    own_sum, *sums = add_columns(keep, other_core(send))
    parts_a = ring_sum(sums[:3], "y")
    parts_b = ring_sum(sums[3:], "y")
    w_a = adam_first(own_sum, parts_a, params, moment_one, moment_two)
    new_params, new_one, new_two, w_b = adam(
        own_sum, parts_a + parts_b, params, moment_one, moment_two, w_a
    )

    w_t = out_weight.T
    w_one, w_two = forth(w_t, "x"), back(w_t, "x")

    lengths, _ = lax.optimization_barrier((lengths, sums[5]))
    steps_n, seq_local, q_rank = query_latent.shape
    order, lengths_in, by_seq, r_own, r_send, nl, nr = prepare(
        lengths, query_latent, rope_weight, new_latent, new_rope, lambda: here()[3]
    )
    r_got = other_core(r_send)

    (w_one, w_two), units = spread(w_a, 1, (w_one, w_two))
    _, more = spread(w_b, -1)
    units += more

    w_rows = SIDE * SIDE * params.shape[0]
    q_own, q_send = queries(by_seq, units, w_rows, seq_local, q_rank)
    mixed, mixed_send = attention(
        order,
        lengths_in,
        q_own,
        other_core(q_send),
        r_own,
        r_got,
        nl,
        nr,
        latent_cache,
        rope_cache,
        steps_n,
    )
    w_one, mixed = lax.optimization_barrier((w_one, mixed))
    out_weights = (w_t, w_one, w_two, forth(w_one, "x"))
    values = project_values(order, mixed, other_core(mixed_send), value_weight)

    send, keep = output_blocks(ring(values, "z"), out_weights, seq_local)
    own, *sums = add_blocks(keep, other_core(send))
    blocks = total_blocks((own,) + ring_sum(sums, "y"))

    arrived = [blocks[0]]
    for d in range(1, SIDE):
        perm = [
            (zz * SIDE + xx, ((zz + d) % SIDE) * SIDE + xx)
            for zz in range(SIDE)
            for xx in range(SIDE)
        ]
        arrived.append(lax.ppermute(blocks[d], "fsdp", perm))
    mine = join_columns(arrived)

    column = list(ring(mine, "y"))
    column += [other_core(b) for b in column]
    decoded = settle(column)
    return (new_params, new_one, new_two, decoded)


def solution(mesh):
    return jax.shard_map(
        body,
        mesh=mesh,
        in_specs=(
            P("head", "fsdp", None),
            P("fsdp", "head"),
            P("fsdp", "head"),
            P("fsdp", "head"),
            P(None, "fsdp", None),
            P(None, "head"),
            P(None, "head"),
            P("head", "fsdp"),
            P("fsdp", None, None),
            P("fsdp", None, None),
            P(None, "fsdp", None),
            P(None, "fsdp", None),
            P("fsdp"),
        ),
        out_specs=(P("fsdp", "head"), P("fsdp", "head"), P("fsdp", "head"), P(None, "fsdp", None)),
        check_vma=False,
    )
```

```python
import functools
import itertools
import math

import jax
import jax.numpy as jnp
import numpy as np
from jax import lax
from jax.experimental import pallas as pl
from jax.experimental.pallas import tpu as pltpu
from jax.sharding import PartitionSpec as P

HDIM = 128
ROPE = 64
SIDE = 4
BLOCK = 1024
SLOTS = 12
MIB = 1024 * 1024

first_fix = 1.0 - math.exp(100.0 * math.log(0.9))
second_fix = 1.0 - math.exp(100.0 * math.log(0.999))
NEG = -1e30
LOG2E = math.log2(math.e)

NT = (((1,), (1,)), ((), ()))
NN = (((1,), (0,)), ((), ()))


def dot(a, b, dims):
    return lax.dot_general(a, b, dims, preferred_element_type=jnp.float32)


def moves(step):
    perm = []
    for z in range(SIDE):
        for x in range(SIDE):
            for y in range(SIDE):
                for c in range(2):
                    axis, to_place = step(c)
                    to = {"x": x, "y": y, "z": z}
                    to[axis] = to_place(to[axis]) % SIDE
                    perm.append(
                        (
                            (z * SIDE + x) * 2 * SIDE + y * 2 + c,
                            (to["z"] * SIDE + to["x"]) * 2 * SIDE + to["y"] * 2 + c,
                        )
                    )
    return perm


def shift(v, step):
    return lax.ppermute(v, ("fsdp", "head"), moves(step))


def forth(v, axis):
    return shift(v, lambda c: (axis, lambda i: i + 1 - 2 * c))


def back(v, axis):
    return shift(v, lambda c: (axis, lambda i: i + 2 * c - 1))


def first(v, d):
    return shift(v, lambda c: (("x", "z")[c], lambda i: i + d))


def second(v, d):
    return shift(v, lambda c: (("z", "x")[c], lambda i: i + d))


def other_core(v):
    return lax.ppermute(v, "head", [(i, i ^ 1) for i in range(2 * SIDE)])


def ring(own, axis):
    one = forth(own, axis)
    two = back(own, axis)
    return own, one, two, forth(one, axis)


def ring_sum(blocks, axis):
    far = forth(blocks[2], axis)
    two = back(blocks[1], axis)
    return forth(add_two(blocks[0], far), axis), two


def here():
    f = lax.axis_index("fsdp")
    h = lax.axis_index("head")
    return lax.div(f, SIDE), lax.rem(f, SIDE), lax.div(h, 2), lax.rem(h, 2)


def turned(base, s):
    return [lax.rem(base + d, SIDE) for d in (0, SIDE + s, SIDE - s, 2)]


VMEM = pl.BlockSpec(memory_space=pltpu.VMEM)
SMEM = pl.BlockSpec(memory_space=pltpu.SMEM)
HBM = pl.BlockSpec(memory_space=pltpu.HBM)
F32 = jnp.float32
BF16 = jnp.bfloat16


def in_hbm(v):
    return pltpu.with_memory_space_constraint(v, pltpu.HBM)


def room(mib):
    return pltpu.CompilerParams(vmem_limit_bytes=mib * MIB)


def add_two_body(a, b, o):
    o[...] = (a[...].astype(F32) + b[...].astype(F32)).astype(o.dtype)


def add_two(a, b):
    return pl.pallas_call(
        add_two_body,
        in_specs=[VMEM] * 2,
        out_specs=VMEM,
        out_shape=jax.ShapeDtypeStruct(a.shape, BF16),
        compiler_params=room(8),
        name="add_two",
    )(a, b)


def pack_body(g_ref, p, one, two, send_ref, keep_ref, p_out, one_out, two_out, sem):
    _, _, y, core = here()
    sign = 1 - 2 * core
    cols = send_ref.shape[2]
    copies = []
    for ref, places, c in (
        (send_ref, turned(y, -sign), 1 - core),
        (keep_ref, turned(y, sign), core),
    ):
        for j, place in enumerate(places):
            at = pl.multiple_of((2 * place + c) * cols, 128)
            copies.append(
                pltpu.make_async_copy(
                    g_ref.at[:, pl.ds(at, cols)], ref.at[j], sem.at[len(copies)]
                )
            )
    for src, dst in ((p, p_out), (one, one_out), (two, two_out)):
        copies.append(pltpu.make_async_copy(src, dst, sem.at[len(copies)]))
    for copy in copies:
        copy.start()
    for copy in copies:
        copy.wait()


def pack(g, p, one, two):
    out = jax.ShapeDtypeStruct((SIDE, g.shape[0], g.shape[1] // (2 * SIDE)), g.dtype)
    return pl.pallas_call(
        pack_body,
        in_specs=[HBM] * 4,
        out_specs=[VMEM] * 5,
        out_shape=[out] * 2 + [jax.ShapeDtypeStruct(p.shape, F32)] * 3,
        scratch_shapes=[pltpu.SemaphoreType.DMA((2 * SIDE + 3,))],
        compiler_params=room(8),
        name="pack_columns",
    )(*(in_hbm(v) for v in (g, p, one, two)))


def add_columns_body(keep, got, own, *parts):
    rows, cols = own.shape
    width = cols // 2
    for j in (3, 2, 1, 0):
        for r in range(0, rows, 16):
            part = slice(r, r + 16)
            total = keep[j, part, :].astype(F32) + got[j, part, :].astype(F32)
            if j == 0:
                own[part, :] = total
            else:
                parts[j - 1][part, :] = total[:, :width].astype(BF16)
                parts[j + 2][part, :] = total[:, width:].astype(BF16)


def add_columns(keep, got):
    rows, cols = got.shape[1:]
    half = jax.ShapeDtypeStruct((rows, cols // 2), BF16)
    return pl.pallas_call(
        add_columns_body,
        in_specs=[VMEM] * 2,
        out_specs=[VMEM] * 7,
        out_shape=[jax.ShapeDtypeStruct((rows, cols), F32)] + [half] * 6,
        compiler_params=room(8),
        name="add_columns",
    )(keep, got)


def adam_step(grad, p, one, two):
    step_size = 0.003 / first_fix
    moment = 0.9 * one + 0.1 * grad
    second_moment = 0.999 * two + 0.001 * grad * grad
    denom = jnp.sqrt(second_moment / second_fix) + 1e-08
    return p - step_size * moment / denom, moment, second_moment


def adam_first_body(r0, r1, r2, p, one, two, w):
    width = w.shape[1]
    cols = slice(0, width)
    for r in range(0, p.shape[0], 16):
        part = slice(r, r + 16)
        grad = r0[part, cols] + r1[part].astype(F32) + r2[part].astype(F32)
        w[part] = adam_step(grad, p[part, cols], one[part, cols], two[part, cols])[0].astype(BF16)


def adam_first(own, parts, p, one, two):
    rows, cols = p.shape
    return pl.pallas_call(
        adam_first_body,
        in_specs=[VMEM] * 6,
        out_specs=VMEM,
        out_shape=jax.ShapeDtypeStruct((rows, cols // 2), BF16),
        compiler_params=room(12),
        name="adam_first",
    )(own, *parts, p, one, two)


def adam_body(r0, a1, a2, b1, b2, p, one, two, after, new_p, new_one, new_two, w):
    del after
    width = w.shape[1]
    for r in range(0, p.shape[0], 16):
        part = slice(r, r + 16)
        for k, (r1, r2) in ((1, (b1, b2)), (0, (a1, a2))):
            cols = slice(k * width, (k + 1) * width)
            grad = r0[part, cols] + r1[part].astype(F32) + r2[part].astype(F32)
            params, moment, second_moment = adam_step(
                grad, p[part, cols], one[part, cols], two[part, cols]
            )
            if k:
                w[part] = params.astype(BF16)
            new_p[part, cols] = params
            new_one[part, cols] = moment
            new_two[part, cols] = second_moment


def adam(own, parts, p, one, two, after):
    rows, cols = p.shape
    full = jax.ShapeDtypeStruct(p.shape, F32)
    return pl.pallas_call(
        adam_body,
        in_specs=[VMEM] * 8 + [pl.BlockSpec(memory_space=pl.ANY)],
        out_specs=[VMEM] * 4,
        out_shape=[full] * 3 + [jax.ShapeDtypeStruct((rows, cols // 2), BF16)],
        compiler_params=room(12),
        name="adam",
    )(own, *parts, p, one, two, after)


def stack_body(*refs):
    out = refs[-1]
    rows = refs[0].shape[0]
    for k, ref in enumerate(refs[:-1]):
        out[k * rows : (k + 1) * rows, :] = ref[...]


def stack_rows(*blocks):
    rows, cols = blocks[0].shape
    return pl.pallas_call(
        stack_body,
        in_specs=[VMEM] * len(blocks),
        out_specs=VMEM,
        out_shape=jax.ShapeDtypeStruct((len(blocks) * rows, cols), blocks[0].dtype),
        compiler_params=room(8),
        name="stack_rows",
    )(*blocks)


def spread(w, d, also=()):
    above, below = first(w, 1), first(w, -1)
    unit = stack_rows(w, above, below, first(above if d > 0 else below, d))
    unit, *also = lax.optimization_barrier((unit,) + tuple(also))
    up, down = second(unit, 1), second(unit, -1)
    return also, [unit, up, down, second(up if d > 0 else down, d)]


def query_body(ql_ref, *refs, seqs, steps, heads, q_rank):
    units = refs[:8]
    keep_ref, send_ref, w_buf, lat_buf = refs[8:]
    z, x, _, core = here()
    shard = w_buf.shape[0] // (SIDE * SIDE)
    far = (0, SIDE - 1, 1, 2)
    width = w_buf.shape[1] // 2
    for k in range(SIDE):
        for m in range(SIDE):
            zo = jnp.where(core == 0, far[k], far[m])
            xo = jnp.where(core == 0, far[m], far[k])
            f = lax.rem(z + zo, SIDE) * SIDE + lax.rem(x + xo, SIDE)
            at = pl.multiple_of(f * shard, shard)
            rows = slice(m * shard, (m + 1) * shard)
            for h in range(2):
                cols = slice(h * width, (h + 1) * width)
                w_buf[pl.ds(at, shard), cols] = units[4 * h + k][rows, :]
    nope = dot(ql_ref[...], w_buf[:q_rank, :], NN).astype(BF16)
    for h in range(heads):
        cols = slice(h * HDIM, (h + 1) * HDIM)
        lat = dot(nope[:, cols], w_buf[q_rank:, cols], NT)
        lat_buf[:, h * steps : (h + 1) * steps, :] = lat.reshape(seqs, steps, -1)
    keep_ref[...] = lat_buf[: seqs // 2].astype(BF16)
    send_ref[...] = lat_buf[seqs // 2 :].astype(BF16)


def queries(ql, units, w_rows, seqs, q_rank):
    cols = 2 * units[0].shape[1]
    heads = cols // HDIM
    steps = ql.shape[0] // seqs
    lat_rank = w_rows - q_rank
    out = jax.ShapeDtypeStruct((seqs // 2, heads * steps, lat_rank), BF16)
    return pl.pallas_call(
        functools.partial(query_body, seqs=seqs, steps=steps, heads=heads, q_rank=q_rank),
        in_specs=[VMEM] * 9,
        out_specs=[VMEM] * 2,
        out_shape=[out] * 2,
        scratch_shapes=[
            pltpu.VMEM((w_rows, cols), BF16),
            pltpu.VMEM((seqs, heads * steps, lat_rank), F32),
        ],
        compiler_params=room(16),
        name="queries",
    )(ql, *units)


def attention_body(
    order_ref,
    len_ref,
    q_own,
    q_got,
    r_own,
    r_got,
    nl_ref,
    nr_ref,
    vw_own,
    vw_got,
    lat_hbm,
    rope_hbm,
    out_ref,
    lat_buf,
    rope_buf,
    q_buf,
    qr_buf,
    acc,
    m_ref,
    l_ref,
    flat,
    p0,
    p1,
    a0,
    a1,
    seq_of,
    blk_of,
    lat_sem,
    rope_sem,
    *,
    steps,
):
    seqs, rows, _ = q_buf.shape
    part = rows // 2
    factor = LOG2E / math.sqrt(HDIM + ROPE)

    def listing(s, at):
        blocks = lax.div(len_ref[s] + (BLOCK - 1), BLOCK)

        def put(j, at):
            seq_of[at] = s
            blk_of[at] = j
            return at + 1

        return lax.fori_loop(0, blocks, put, at)

    count = lax.fori_loop(0, seqs, listing, 0)

    def lat_copy(i):
        slot = lax.rem(i, SLOTS)
        start = pl.multiple_of(blk_of[i] * BLOCK, BLOCK)
        return pltpu.make_async_copy(
            lat_hbm.at[order_ref[seq_of[i]], pl.ds(start, BLOCK), :],
            lat_buf.at[slot],
            lat_sem.at[slot],
        )

    def rope_copy(i):
        slot = lax.rem(i, SLOTS)
        start = pl.multiple_of(blk_of[i] * BLOCK, BLOCK)
        return pltpu.make_async_copy(
            rope_hbm.at[order_ref[seq_of[i]], :, pl.ds(start, BLOCK)],
            rope_buf.at[slot],
            rope_sem.at[slot],
        )

    def fetch(i):
        @pl.when(i < count)
        def _():
            lat_copy(i).start()
            rope_copy(i).start()

    for i in range(SLOTS - 2):
        fetch(i)

    q_buf[:, :part, :] = q_own[...]
    q_buf[:, part:, :] = q_got[...]
    qr_buf[:, :part, :] = r_own[...]
    qr_buf[:, part:, :] = r_got[...]

    width = nl_ref.shape[1]
    token = lax.broadcasted_iota(jnp.int32, (rows, width), 1)
    step = lax.rem(lax.broadcasted_iota(jnp.int32, (rows, width), 0), steps)
    seen = token <= step
    for s in range(seqs):
        score = dot(q_buf[s], nl_ref[s], NT) + dot(qr_buf[s], nr_ref[s], NT)
        score = jnp.where(seen, score, NEG)
        top = jnp.max(score, axis=1, keepdims=True)
        prob = jnp.exp2((score - top) * factor)
        m_ref[s] = jnp.broadcast_to(top, (rows, 128))
        l_ref[s] = prob
        acc[s] = dot(prob.astype(BF16), nl_ref[s], NN)

    lane = lax.broadcasted_iota(jnp.int32, (rows, BLOCK), 1)

    def arrive(i):
        lat_copy(i).wait()
        rope_copy(i).wait()

    def scores(i):
        slot = lax.rem(i, SLOTS)
        s = seq_of[i]
        return dot(q_buf[s], lat_buf[slot], NT) + dot(qr_buf[s], rope_buf[slot], NN)

    def weigh(i, score, p_ref, a_ref):
        s = seq_of[i]
        score = jnp.where(lane < len_ref[s] - blk_of[i] * BLOCK, score, NEG)
        before = m_ref[s]
        top = jnp.maximum(before, jnp.max(score, axis=1, keepdims=True))
        prob = jnp.exp2((score - top[:, :1]) * factor)
        alpha = jnp.exp2((before - top) * factor)
        total = l_ref[s] * alpha
        for k in range(BLOCK // 128):
            total += prob[:, k * 128 : (k + 1) * 128]
        m_ref[s] = top
        l_ref[s] = total
        a_ref[...] = alpha
        p_ref[...] = prob.astype(BF16)

    def gather(i, p_ref, a_ref):
        slot = lax.rem(i, SLOTS)
        s = seq_of[i]
        acc[s] = acc[s] * a_ref[:, :1] + dot(p_ref[...], lat_buf[slot], NN)

    arrive(0)
    weigh(0, scores(0), p0, a0)

    def pair(k, carry):
        i = 2 * k
        fetch(i + SLOTS - 2)
        fetch(i + SLOTS - 1)
        arrive(i + 1)
        arrive(i + 2)
        odd = scores(i + 1)
        gather(i, p0, a0)
        even = scores(i + 2)
        weigh(i + 1, odd, p1, a1)
        gather(i + 1, p1, a1)
        weigh(i + 2, even, p0, a0)
        return carry

    pairs = lax.div(count - 1, 2)
    lax.fori_loop(0, pairs, pair, 0)

    @pl.when(2 * pairs + 1 < count)
    def _():
        arrive(2 * pairs + 1)
        odd = scores(2 * pairs + 1)
        gather(2 * pairs, p0, a0)
        weigh(2 * pairs + 1, odd, p1, a1)
        gather(2 * pairs + 1, p1, a1)

    @pl.when(2 * pairs + 1 >= count)
    def _():
        gather(2 * pairs, p0, a0)

    for s in range(seqs):
        acc[s] = acc[s] / jnp.sum(l_ref[s], axis=1, keepdims=True)
    cols = vw_own.shape[1]
    for k, vw in enumerate((vw_own, vw_got)):
        for h in range(cols // HDIM):
            at = k * part + h * steps
            mixed = acc[:, at : at + steps, :].reshape(seqs * steps, -1).astype(BF16)
            value = dot(mixed, vw[:, h * HDIM : (h + 1) * HDIM], NN)
            flat[:, k * cols + h * HDIM : k * cols + (h + 1) * HDIM] = value.astype(BF16)
    _, _, y, core = here()
    count = seqs * steps
    each = steps // SIDE
    row = lax.broadcasted_iota(jnp.int32, (count, count), 0)
    col = lax.broadcasted_iota(jnp.int32, (count, count), 1)
    step = jnp.zeros((count, count), jnp.int32)
    for j, place in enumerate(turned(y, 1 - 2 * core)):
        step = jnp.where(lax.div(row, each * seqs) == j, each * place, step)
    step += lax.rem(lax.div(row, seqs), each)
    same = (step == lax.rem(col, steps)) & (lax.rem(row, seqs) == lax.div(col, steps))
    pick = jnp.where(same, 1.0, 0.0).astype(BF16)
    out_ref[...] = dot(pick, flat[...], NN).astype(BF16)


def attention(order, lengths, q_own, q_got, r_own, r_got, nl, nr, vw_own, vw_got, lat, rope):
    seqs, part, lat_rank = q_own.shape
    rows = 2 * part
    most = seqs * (lat.shape[1] // BLOCK) + 1
    steps = part * HDIM // vw_own.shape[1]
    out = jax.ShapeDtypeStruct((seqs * steps, 2 * vw_own.shape[1]), BF16)
    return pl.pallas_call(
        functools.partial(attention_body, steps=steps),
        in_specs=[SMEM, SMEM] + [VMEM] * 8 + [HBM] * 2,
        out_specs=VMEM,
        out_shape=out,
        scratch_shapes=[
            pltpu.VMEM((SLOTS, BLOCK, lat_rank), BF16),
            pltpu.VMEM((SLOTS, ROPE, BLOCK), BF16),
            pltpu.VMEM((seqs, rows, lat_rank), BF16),
            pltpu.VMEM((seqs, rows, ROPE), BF16),
            pltpu.VMEM((seqs, rows, lat_rank), F32),
            pltpu.VMEM((seqs, rows, 128), F32),
            pltpu.VMEM((seqs, rows, 128), F32),
            pltpu.VMEM(out.shape, BF16),
            pltpu.VMEM((rows, BLOCK), BF16),
            pltpu.VMEM((rows, BLOCK), BF16),
            pltpu.VMEM((rows, 128), F32),
            pltpu.VMEM((rows, 128), F32),
            pltpu.SMEM((most,), jnp.int32),
            pltpu.SMEM((most,), jnp.int32),
            pltpu.SemaphoreType.DMA((SLOTS,)),
            pltpu.SemaphoreType.DMA((SLOTS,)),
        ],
        compiler_params=room(40),
        name="attention",
    )(
        order,
        lengths,
        q_own,
        q_got,
        r_own,
        r_got,
        nl,
        nr,
        vw_own,
        vw_got,
        in_hbm(lat),
        in_hbm(rope),
    )


def output_body(*refs, rows):
    tokens, own_w, got_w, outs = refs[:4], refs[4:8], refs[8:12], refs[12:16]
    v_buf, w_buf = refs[16:]
    _, x, _, core = here()
    sign = 1 - 2 * core
    for place, ref in zip(turned(0, -sign), tokens):
        v_buf[place] = ref[...]
    part, depth = own_w[0].shape
    for k, (weights, way) in enumerate(((own_w, -sign), (got_w, sign))):
        for place, ref in zip(turned(x, way), weights):
            at = pl.multiple_of(place * part, 64)
            w_buf[pl.ds(at, part), k * depth : (k + 1) * depth] = ref[...]
    tokens_all = v_buf[...].reshape(-1, v_buf.shape[2])
    width = 256
    for n in range(w_buf.shape[0] // width):
        cols = slice(n * width, (n + 1) * width)
        res = dot(tokens_all, w_buf[cols, :], NT).reshape(SIDE, SIDE, rows, width)
        for j in range(SIDE):
            for z in range(SIDE):
                outs[j][z, :, cols] = res[z, j].astype(BF16)


def output_blocks(tokens, own_w, got_w):
    count, depth = tokens[0].shape
    cols = SIDE * own_w[0].shape[0]
    rows = count // SIDE
    out = jax.ShapeDtypeStruct((SIDE, rows, cols), BF16)
    return pl.pallas_call(
        functools.partial(output_body, rows=rows),
        in_specs=[VMEM] * 12,
        out_specs=[VMEM] * 4,
        out_shape=[out] * 4,
        scratch_shapes=[
            pltpu.VMEM((SIDE, count, depth), BF16),
            pltpu.VMEM((cols, depth), BF16),
        ],
        compiler_params=room(24),
        name="output_blocks",
    )(*tokens, *own_w, *got_w)


def total_body(a, b, c, *outs):
    for k in (2, 1, 3, 0):
        outs[k][...] = (a[k].astype(F32) + b[k].astype(F32) + c[k].astype(F32)).astype(BF16)


def total_blocks(parts):
    one = jax.ShapeDtypeStruct(parts[0].shape[1:], BF16)
    return pl.pallas_call(
        total_body,
        in_specs=[VMEM] * 3,
        out_specs=[VMEM] * 4,
        out_shape=[one] * 4,
        compiler_params=room(8),
        name="total_blocks",
    )(*parts)


def columns_body(*refs):
    out = refs[-1]
    width = refs[0].shape[1]
    z = here()[0]
    for d, ref in enumerate(refs[:-1]):
        at = lax.rem(z + SIDE - d, SIDE) * width
        out[:, pl.ds(pl.multiple_of(at, 128), width)] = ref[...]


def join_columns(blocks):
    rows, width = blocks[0].shape
    return pl.pallas_call(
        columns_body,
        in_specs=[VMEM] * SIDE,
        out_specs=VMEM,
        out_shape=jax.ShapeDtypeStruct((rows, SIDE * width), BF16),
        compiler_params=room(8),
        name="join_columns",
    )(*blocks)


def settle_body(order_ref, *refs):
    blocks, out, buf = refs[:8], refs[8], refs[9]
    steps, seqs, cols = out.shape
    half = seqs // 2
    each = steps // SIDE
    count = steps * seqs
    size = each * half
    _, _, y, core = here()
    sign = 1 - 2 * core
    for k, ref in enumerate(blocks):
        buf[k * size : (k + 1) * size, :] = ref[...].astype(F32)
    row = lax.broadcasted_iota(jnp.int32, (count, count), 0)
    col = lax.broadcasted_iota(jnp.int32, (count, count), 1)
    step = jnp.zeros((count, count), jnp.int32)
    for k, place in enumerate(turned(y, -sign) + turned(y, sign)):
        step = jnp.where(lax.div(col, size) == k, each * place, step)
    step += lax.rem(lax.div(col, half), each)
    place = half * lax.div(col, SIDE * size) + lax.rem(col, half)
    seq = jnp.zeros((count, count), jnp.int32)
    for k in range(seqs):
        seq = jnp.where(place == k, order_ref[k], seq)
    same = (step == lax.div(row, seqs)) & (seq == lax.rem(row, seqs))
    pick = jnp.where(same, 1.0, 0.0).astype(BF16)
    width = 1024
    for n in range(cols // width):
        part = slice(n * width, (n + 1) * width)
        res = dot(pick, buf[:, part].astype(BF16), NN)
        out[:, :, part] = res.reshape(steps, seqs, width).astype(BF16)


def settle(order, blocks):
    rows, cols = blocks[0].shape
    return pl.pallas_call(
        settle_body,
        in_specs=[SMEM] + [VMEM] * 8,
        out_specs=VMEM,
        out_shape=jax.ShapeDtypeStruct((rows, 8, cols), BF16),
        scratch_shapes=[pltpu.VMEM((8 * rows, cols), F32)],
        compiler_params=room(12),
        name="settle",
    )(order, *blocks)


def splits(seqs):
    for rest in itertools.combinations(range(1, seqs), seqs // 2 - 1):
        mine = (0,) + rest
        yield mine + tuple(s for s in range(seqs) if s not in mine)


def prepare_body(
    len_ref,
    ql_ref,
    rw_ref,
    nl_ref,
    nr_ref,
    order_ref,
    length_ref,
    by_seq_ref,
    r_own,
    r_send,
    nl_out,
    nr_out,
    r_buf,
    *,
    core_of,
):
    core = core_of()
    steps, seqs, q_rank = ql_ref.shape
    half = seqs // 2
    count = steps * seqs

    blocks = [lax.div(len_ref[s] + (BLOCK - 1), BLOCK) for s in range(seqs)]
    whole = sum(blocks[1:], blocks[0])
    least, code = None, None
    for row in splits(seqs):
        part = blocks[0] + blocks[row[1]] + blocks[row[2]] + blocks[row[3]]
        larger = jnp.maximum(part, whole - part)
        digits = sum(s << (3 * k) for k, s in enumerate(row))
        if least is None:
            least, code = larger, jnp.int32(digits)
        else:
            code = jnp.where(larger < least, digits, code)
            least = jnp.minimum(larger, least)
    order, lengths = [], []
    for k in range(seqs):
        shift_by = jnp.where(core == 0, 3 * k, 3 * ((k + half) % seqs))
        order.append(lax.shift_right_logical(code, shift_by) & 7)
        lengths.append(len_ref[order[k]])
        order_ref[k] = order[k]
        length_ref[k] = lengths[k]

    def by_place(place, values):
        out = jnp.zeros(place.shape, jnp.int32)
        for k, value in enumerate(values):
            out = jnp.where(place == k, value, out)
        return out

    def pick(rows, depth, used):
        row = lax.broadcasted_iota(jnp.int32, (rows, count), 0)
        col = lax.broadcasted_iota(jnp.int32, (rows, count), 1)
        same = (by_place(lax.div(row, depth), order[:used]) == lax.rem(col, seqs)) & (
            lax.rem(row, depth) == lax.div(col, seqs)
        )
        return jnp.where(same, 1.0, 0.0).astype(BF16)

    by_seq = dot(pick(count, steps, seqs), ql_ref[...].reshape(count, q_rank), NN).astype(BF16)
    by_seq_ref[...] = by_seq

    turn = dot(by_seq, rw_ref[...], NN)
    cols = turn.shape[1]
    row = lax.broadcasted_iota(jnp.int32, (count, 128), 0)
    lane = lax.broadcasted_iota(jnp.int32, (count, 128), 1)
    position = (by_place(lax.div(row, steps), lengths) + lax.rem(row, steps)).astype(F32)
    index_f = lax.rem(lane, ROPE // 2).astype(F32)
    angle = position * jnp.exp(-math.log(10000.0) * 2.0 * index_f / ROPE)
    is_first = lax.rem(lane, ROPE) < ROPE // 2
    cosine = jnp.concatenate([jnp.cos(angle)] * (cols // 128), axis=1)
    sine = jnp.sin(angle)
    sine = jnp.concatenate([jnp.where(is_first, -sine, sine)] * (cols // 128), axis=1)
    is_first = lax.rem(lax.broadcasted_iota(jnp.int32, (count, cols), 1), ROPE) < ROPE // 2
    other = jnp.where(
        is_first,
        pltpu.roll(turn, cols - ROPE // 2, 1),
        pltpu.roll(turn, ROPE // 2, 1),
    )
    turn = turn * cosine + other * sine
    for h in range(cols // ROPE):
        piece = turn[:, h * ROPE : (h + 1) * ROPE].reshape(seqs, steps, ROPE)
        r_buf[:, h * steps : (h + 1) * steps, :] = piece
    r_own[...] = r_buf[:half].astype(BF16)
    r_send[...] = r_buf[half:].astype(BF16)

    width = nl_out.shape[1]
    chosen = pick(half * width, width, half)
    for src, out in ((nl_ref, nl_out), (nr_ref, nr_out)):
        rank = src.shape[2]
        rows = dot(chosen, src[...].reshape(count, rank), NN).astype(BF16)
        out[...] = rows.reshape(half, width, rank)


def prepare(lengths, ql, rw, nl, nr, core_of):
    steps, seqs, q_rank = ql.shape
    half = seqs // 2
    rows = rw.shape[1] // ROPE * steps
    turned_rows = jax.ShapeDtypeStruct((half, rows, ROPE), BF16)
    return pl.pallas_call(
        functools.partial(prepare_body, core_of=core_of),
        in_specs=[SMEM] + [VMEM] * 4,
        out_specs=[SMEM] * 2 + [VMEM] * 5,
        out_shape=[jax.ShapeDtypeStruct((seqs,), jnp.int32)] * 2
        + [jax.ShapeDtypeStruct((steps * seqs, q_rank), BF16)]
        + [turned_rows] * 2
        + [jax.ShapeDtypeStruct((half, 128, v.shape[2]), BF16) for v in (nl, nr)],
        scratch_shapes=[pltpu.VMEM((seqs, rows, ROPE), F32)],
        compiler_params=room(12),
        name="prepare",
    )(lengths, ql, rw, nl, nr)


def body(
    grad_parts,
    params,
    moment_one,
    moment_two,
    query_latent,
    rope_weight,
    value_weight,
    out_weight,
    latent_cache,
    rope_cache,
    new_latent,
    new_rope,
    lengths,
):
    send, keep, params, moment_one, moment_two = pack(
        grad_parts[0], params, moment_one, moment_two
    )
    own_sum, *sums = add_columns(keep, other_core(send))
    parts_a = ring_sum(sums[:3], "y")
    parts_b = ring_sum(sums[3:], "y")
    w_a = adam_first(own_sum, parts_a, params, moment_one, moment_two)
    new_params, new_one, new_two, w_b = adam(
        own_sum, parts_a + parts_b, params, moment_one, moment_two, w_a
    )

    w_t = out_weight.T
    w_one, w_two = forth(w_t, "x"), back(w_t, "x")

    lengths, _ = lax.optimization_barrier((lengths, sums[5]))
    steps_n, seq_local, q_rank = query_latent.shape
    order, lengths_in, by_seq, r_own, r_send, nl, nr = prepare(
        lengths, query_latent, rope_weight, new_latent, new_rope, lambda: here()[3]
    )
    r_got = other_core(r_send)

    (w_one, w_two), units = spread(w_a, 1, (w_one, w_two))
    _, more = spread(w_b, -1)
    units += more

    w_rows = SIDE * SIDE * params.shape[0]
    by_seq, r_got, vw_got = lax.optimization_barrier((by_seq, r_got, other_core(value_weight)))
    q_own, q_send = queries(by_seq, units, w_rows, seq_local, q_rank)
    w_one, q_send = lax.optimization_barrier((w_one, q_send))
    w_three = forth(w_one, "x")
    q_got, *early = lax.optimization_barrier((other_core(q_send), w_t, w_one, w_two))
    got_w = [other_core(w) for w in early]
    values = attention(
        order,
        lengths_in,
        q_own,
        q_got,
        r_own,
        r_got,
        nl,
        nr,
        value_weight,
        vw_got,
        latent_cache,
        rope_cache,
    )

    *got_w, w_three, values = lax.optimization_barrier((*got_w, w_three, values))
    own_w = (w_t, w_one, w_two, w_three)
    tokens = ring(values, "z")
    got_w.append(other_core(w_three))
    own, *sums = output_blocks(tokens, own_w, got_w)
    blocks = total_blocks((own,) + ring_sum(sums, "y"))

    arrived = [blocks[0]]
    for d in range(1, SIDE):
        perm = [
            (zz * SIDE + xx, ((zz + d) % SIDE) * SIDE + xx)
            for zz in range(SIDE)
            for xx in range(SIDE)
        ]
        arrived.append(lax.ppermute(blocks[d], "fsdp", perm))
    mine = join_columns(arrived)

    column = list(ring(mine, "y"))
    column += [other_core(b) for b in column]
    decoded = settle(order, column)
    return (new_params, new_one, new_two, decoded)


def solution(mesh):
    return jax.shard_map(
        body,
        mesh=mesh,
        in_specs=(
            P("head", "fsdp", None),
            P("fsdp", "head"),
            P("fsdp", "head"),
            P("fsdp", "head"),
            P(None, "fsdp", None),
            P(None, "head"),
            P(None, "head"),
            P("head", "fsdp"),
            P("fsdp", None, None),
            P("fsdp", None, None),
            P(None, "fsdp", None),
            P(None, "fsdp", None),
            P("fsdp"),
        ),
        out_specs=(P("fsdp", "head"), P("fsdp", "head"), P("fsdp", "head"), P(None, "fsdp", None)),
        check_vma=False,
    )
```

```python
import functools
import itertools
import math

import jax
import jax.numpy as jnp
import numpy as np
from jax import lax
from jax.experimental import pallas as pl
from jax.experimental.pallas import tpu as pltpu
from jax.sharding import PartitionSpec as P

HDIM = 128
ROPE = 64
SIDE = 4
BLOCK = 1024
SLOTS = 12
MIB = 1024 * 1024

first_fix = 1.0 - math.exp(100.0 * math.log(0.9))
second_fix = 1.0 - math.exp(100.0 * math.log(0.999))
NEG = -1e30
LOG2E = math.log2(math.e)

NT = (((1,), (1,)), ((), ()))
NN = (((1,), (0,)), ((), ()))


def dot(a, b, dims):
    return lax.dot_general(a, b, dims, preferred_element_type=jnp.float32)


def moves(step):
    perm = []
    for z in range(SIDE):
        for x in range(SIDE):
            for y in range(SIDE):
                for c in range(2):
                    axis, to_place = step(c)
                    to = {"x": x, "y": y, "z": z}
                    to[axis] = to_place(to[axis]) % SIDE
                    perm.append(
                        (
                            (z * SIDE + x) * 2 * SIDE + y * 2 + c,
                            (to["z"] * SIDE + to["x"]) * 2 * SIDE + to["y"] * 2 + c,
                        )
                    )
    return perm


def shift(v, step):
    return lax.ppermute(v, ("fsdp", "head"), moves(step))


def forth(v, axis):
    return shift(v, lambda c: (axis, lambda i: i + 1 - 2 * c))


def back(v, axis):
    return shift(v, lambda c: (axis, lambda i: i + 2 * c - 1))


def first(v, d):
    return shift(v, lambda c: (("x", "z")[c], lambda i: i + d))


def second(v, d):
    return shift(v, lambda c: (("z", "x")[c], lambda i: i + d))


def other_core(v):
    return lax.ppermute(v, "head", [(i, i ^ 1) for i in range(2 * SIDE)])


def ring(own, axis):
    one = forth(own, axis)
    two = back(own, axis)
    return own, one, two, forth(one, axis)


def ring_sum(blocks, axis):
    far = forth(blocks[2], axis)
    two = back(blocks[1], axis)
    return forth(add_two(blocks[0], far), axis), two


def here():
    f = lax.axis_index("fsdp")
    h = lax.axis_index("head")
    return lax.div(f, SIDE), lax.rem(f, SIDE), lax.div(h, 2), lax.rem(h, 2)


def turned(base, s):
    return [lax.rem(base + d, SIDE) for d in (0, SIDE + s, SIDE - s, 2)]


VMEM = pl.BlockSpec(memory_space=pltpu.VMEM)
SMEM = pl.BlockSpec(memory_space=pltpu.SMEM)
HBM = pl.BlockSpec(memory_space=pltpu.HBM)
F32 = jnp.float32
BF16 = jnp.bfloat16


def in_hbm(v):
    return pltpu.with_memory_space_constraint(v, pltpu.HBM)


def room(mib):
    return pltpu.CompilerParams(vmem_limit_bytes=mib * MIB)


def add_two_body(a, b, o):
    o[...] = (a[...].astype(F32) + b[...].astype(F32)).astype(o.dtype)


def add_two(a, b):
    return pl.pallas_call(
        add_two_body,
        in_specs=[VMEM] * 2,
        out_specs=VMEM,
        out_shape=jax.ShapeDtypeStruct(a.shape, BF16),
        compiler_params=room(8),
        name="add_two",
    )(a, b)


def pack_body(g_ref, p, one, two, send_ref, keep_ref, p_out, one_out, two_out, sem):
    _, _, y, core = here()
    sign = 1 - 2 * core
    cols = send_ref.shape[2]
    copies = []
    for ref, places, c in (
        (send_ref, turned(y, -sign), 1 - core),
        (keep_ref, turned(y, sign), core),
    ):
        for j, place in enumerate(places):
            at = pl.multiple_of((2 * place + c) * cols, 128)
            copies.append(
                pltpu.make_async_copy(
                    g_ref.at[:, pl.ds(at, cols)], ref.at[j], sem.at[len(copies)]
                )
            )
    for src, dst in ((p, p_out), (one, one_out), (two, two_out)):
        copies.append(pltpu.make_async_copy(src, dst, sem.at[len(copies)]))
    for copy in copies:
        copy.start()
    for copy in copies:
        copy.wait()


def pack(g, p, one, two):
    out = jax.ShapeDtypeStruct((SIDE, g.shape[0], g.shape[1] // (2 * SIDE)), g.dtype)
    return pl.pallas_call(
        pack_body,
        in_specs=[HBM] * 4,
        out_specs=[VMEM] * 5,
        out_shape=[out] * 2 + [jax.ShapeDtypeStruct(p.shape, F32)] * 3,
        scratch_shapes=[pltpu.SemaphoreType.DMA((2 * SIDE + 3,))],
        compiler_params=room(8),
        name="pack_columns",
    )(*(in_hbm(v) for v in (g, p, one, two)))


def add_columns_body(keep, got, own, *parts):
    rows, cols = own.shape
    width = cols // 2
    for j in (3, 2, 1, 0):
        for r in range(0, rows, 16):
            part = slice(r, r + 16)
            total = keep[j, part, :].astype(F32) + got[j, part, :].astype(F32)
            if j == 0:
                own[part, :] = total
            else:
                parts[j - 1][part, :] = total[:, :width].astype(BF16)
                parts[j + 2][part, :] = total[:, width:].astype(BF16)


def add_columns(keep, got):
    rows, cols = got.shape[1:]
    half = jax.ShapeDtypeStruct((rows, cols // 2), BF16)
    return pl.pallas_call(
        add_columns_body,
        in_specs=[VMEM] * 2,
        out_specs=[VMEM] * 7,
        out_shape=[jax.ShapeDtypeStruct((rows, cols), F32)] + [half] * 6,
        compiler_params=room(8),
        name="add_columns",
    )(keep, got)


def adam_step(grad, p, one, two):
    step_size = 0.003 / first_fix
    moment = 0.9 * one + 0.1 * grad
    second_moment = 0.999 * two + 0.001 * grad * grad
    denom = jnp.sqrt(second_moment / second_fix) + 1e-08
    return p - step_size * moment / denom, moment, second_moment


def adam_first_body(r0, r1, r2, p, one, two, w):
    width = w.shape[1]
    cols = slice(0, width)
    for r in range(0, p.shape[0], 16):
        part = slice(r, r + 16)
        grad = r0[part, cols] + r1[part].astype(F32) + r2[part].astype(F32)
        w[part] = adam_step(grad, p[part, cols], one[part, cols], two[part, cols])[0].astype(BF16)


def adam_first(own, parts, p, one, two):
    rows, cols = p.shape
    return pl.pallas_call(
        adam_first_body,
        in_specs=[VMEM] * 6,
        out_specs=VMEM,
        out_shape=jax.ShapeDtypeStruct((rows, cols // 2), BF16),
        compiler_params=room(12),
        name="adam_first",
    )(own, *parts, p, one, two)


def adam_body(r0, a1, a2, b1, b2, p, one, two, after, new_p, new_one, new_two, w):
    del after
    width = w.shape[1]
    for r in range(0, p.shape[0], 16):
        part = slice(r, r + 16)
        for k, (r1, r2) in ((1, (b1, b2)), (0, (a1, a2))):
            cols = slice(k * width, (k + 1) * width)
            grad = r0[part, cols] + r1[part].astype(F32) + r2[part].astype(F32)
            params, moment, second_moment = adam_step(
                grad, p[part, cols], one[part, cols], two[part, cols]
            )
            if k:
                w[part] = params.astype(BF16)
            new_p[part, cols] = params
            new_one[part, cols] = moment
            new_two[part, cols] = second_moment


def adam(own, parts, p, one, two, after):
    rows, cols = p.shape
    full = jax.ShapeDtypeStruct(p.shape, F32)
    return pl.pallas_call(
        adam_body,
        in_specs=[VMEM] * 8 + [pl.BlockSpec(memory_space=pl.ANY)],
        out_specs=[VMEM] * 4,
        out_shape=[full] * 3 + [jax.ShapeDtypeStruct((rows, cols // 2), BF16)],
        compiler_params=room(12),
        name="adam",
    )(own, *parts, p, one, two, after)


def stack_body(*refs):
    out = refs[-1]
    rows = refs[0].shape[0]
    for k, ref in enumerate(refs[:-1]):
        out[k * rows : (k + 1) * rows, :] = ref[...]


def stack_rows(*blocks):
    rows, cols = blocks[0].shape
    return pl.pallas_call(
        stack_body,
        in_specs=[VMEM] * len(blocks),
        out_specs=VMEM,
        out_shape=jax.ShapeDtypeStruct((len(blocks) * rows, cols), blocks[0].dtype),
        compiler_params=room(8),
        name="stack_rows",
    )(*blocks)


def spread(w, d, also=()):
    above, below = first(w, 1), first(w, -1)
    unit = stack_rows(w, above, below, first(above if d > 0 else below, d))
    unit, *also = lax.optimization_barrier((unit,) + tuple(also))
    up, down = second(unit, 1), second(unit, -1)
    return also, [unit, up, down, second(up if d > 0 else down, d)]


def query_body(ql_ref, *refs, seqs, steps, heads, q_rank):
    units = refs[:8]
    keep_ref, send_ref, w_buf, lat_buf = refs[8:]
    z, x, _, core = here()
    shard = w_buf.shape[0] // (SIDE * SIDE)
    far = (0, SIDE - 1, 1, 2)
    width = w_buf.shape[1] // 2
    for k in range(SIDE):
        for m in range(SIDE):
            zo = jnp.where(core == 0, far[k], far[m])
            xo = jnp.where(core == 0, far[m], far[k])
            f = lax.rem(z + zo, SIDE) * SIDE + lax.rem(x + xo, SIDE)
            at = pl.multiple_of(f * shard, shard)
            rows = slice(m * shard, (m + 1) * shard)
            for h in range(2):
                cols = slice(h * width, (h + 1) * width)
                w_buf[pl.ds(at, shard), cols] = units[4 * h + k][rows, :]
    nope = dot(ql_ref[...], w_buf[:q_rank, :], NN).astype(BF16)
    for h in range(heads):
        cols = slice(h * HDIM, (h + 1) * HDIM)
        lat = dot(nope[:, cols], w_buf[q_rank:, cols], NT)
        lat_buf[:, h * steps : (h + 1) * steps, :] = lat.reshape(seqs, steps, -1)
    keep_ref[...] = lat_buf[: seqs // 2].astype(BF16)
    send_ref[...] = lat_buf[seqs // 2 :].astype(BF16)


def queries(ql, units, w_rows, seqs, q_rank):
    cols = 2 * units[0].shape[1]
    heads = cols // HDIM
    steps = ql.shape[0] // seqs
    lat_rank = w_rows - q_rank
    out = jax.ShapeDtypeStruct((seqs // 2, heads * steps, lat_rank), BF16)
    return pl.pallas_call(
        functools.partial(query_body, seqs=seqs, steps=steps, heads=heads, q_rank=q_rank),
        in_specs=[VMEM] * 9,
        out_specs=[VMEM] * 2,
        out_shape=[out] * 2,
        scratch_shapes=[
            pltpu.VMEM((w_rows, cols), BF16),
            pltpu.VMEM((seqs, heads * steps, lat_rank), F32),
        ],
        compiler_params=room(16),
        name="queries",
    )(ql, *units)


def attention_body(
    order_ref,
    len_ref,
    q_own,
    q_got,
    r_own,
    r_got,
    nl_ref,
    nr_ref,
    vw_own,
    vw_got,
    lat_hbm,
    rope_hbm,
    out_ref,
    lat_buf,
    rope_buf,
    q_buf,
    qr_buf,
    acc,
    m_ref,
    l_ref,
    flat,
    p0,
    p1,
    a0,
    a1,
    seq_of,
    blk_of,
    lat_sem,
    rope_sem,
    *,
    steps,
):
    seqs, rows, _ = q_buf.shape
    part = rows // 2
    factor = LOG2E / math.sqrt(HDIM + ROPE)

    def listing(s, at):
        blocks = lax.div(len_ref[s] + (BLOCK - 1), BLOCK)

        def put(j, at):
            seq_of[at] = s
            blk_of[at] = j
            return at + 1

        return lax.fori_loop(0, blocks, put, at)

    count = lax.fori_loop(0, seqs, listing, 0)

    def lat_copy(i):
        slot = lax.rem(i, SLOTS)
        start = pl.multiple_of(blk_of[i] * BLOCK, BLOCK)
        return pltpu.make_async_copy(
            lat_hbm.at[order_ref[seq_of[i]], pl.ds(start, BLOCK), :],
            lat_buf.at[slot],
            lat_sem.at[slot],
        )

    def rope_copy(i):
        slot = lax.rem(i, SLOTS)
        start = pl.multiple_of(blk_of[i] * BLOCK, BLOCK)
        return pltpu.make_async_copy(
            rope_hbm.at[order_ref[seq_of[i]], :, pl.ds(start, BLOCK)],
            rope_buf.at[slot],
            rope_sem.at[slot],
        )

    def fetch(i):
        @pl.when(i < count)
        def _():
            lat_copy(i).start()
            rope_copy(i).start()

    for i in range(SLOTS - 2):
        fetch(i)

    q_buf[:, :part, :] = q_own[...]
    q_buf[:, part:, :] = q_got[...]
    qr_buf[:, :part, :] = r_own[...]
    qr_buf[:, part:, :] = r_got[...]

    width = nl_ref.shape[1]
    token = lax.broadcasted_iota(jnp.int32, (rows, width), 1)
    step = lax.rem(lax.broadcasted_iota(jnp.int32, (rows, width), 0), steps)
    seen = token <= step
    for s in range(seqs):
        score = dot(q_buf[s], nl_ref[s], NT) + dot(qr_buf[s], nr_ref[s], NT)
        score = jnp.where(seen, score, NEG)
        top = jnp.max(score, axis=1, keepdims=True)
        prob = jnp.exp2((score - top) * factor)
        m_ref[s] = jnp.broadcast_to(top, (rows, 128))
        l_ref[s] = prob
        acc[s] = dot(prob.astype(BF16), nl_ref[s], NN)

    lane = lax.broadcasted_iota(jnp.int32, (rows, BLOCK), 1)

    def arrive(i):
        lat_copy(i).wait()
        rope_copy(i).wait()

    def scores(i):
        slot = lax.rem(i, SLOTS)
        s = seq_of[i]
        return dot(q_buf[s], lat_buf[slot], NT) + dot(qr_buf[s], rope_buf[slot], NN)

    def weigh(i, score, p_ref, a_ref):
        s = seq_of[i]
        score = jnp.where(lane < len_ref[s] - blk_of[i] * BLOCK, score, NEG)
        before = m_ref[s]
        top = jnp.maximum(before, jnp.max(score, axis=1, keepdims=True))
        prob = jnp.exp2((score - top[:, :1]) * factor)
        alpha = jnp.exp2((before - top) * factor)
        total = l_ref[s] * alpha
        for k in range(BLOCK // 128):
            total += prob[:, k * 128 : (k + 1) * 128]
        m_ref[s] = top
        l_ref[s] = total
        a_ref[...] = alpha
        p_ref[...] = prob.astype(BF16)

    def gather(i, p_ref, a_ref):
        slot = lax.rem(i, SLOTS)
        s = seq_of[i]
        acc[s] = acc[s] * a_ref[:, :1] + dot(p_ref[...], lat_buf[slot], NN)

    arrive(0)
    weigh(0, scores(0), p0, a0)

    def pair(k, carry):
        i = 2 * k
        fetch(i + SLOTS - 2)
        fetch(i + SLOTS - 1)
        arrive(i + 1)
        arrive(i + 2)
        odd = scores(i + 1)
        gather(i, p0, a0)
        even = scores(i + 2)
        weigh(i + 1, odd, p1, a1)
        gather(i + 1, p1, a1)
        weigh(i + 2, even, p0, a0)
        return carry

    pairs = lax.div(count - 1, 2)
    lax.fori_loop(0, pairs, pair, 0)

    @pl.when(2 * pairs + 1 < count)
    def _():
        arrive(2 * pairs + 1)
        odd = scores(2 * pairs + 1)
        gather(2 * pairs, p0, a0)
        weigh(2 * pairs + 1, odd, p1, a1)
        gather(2 * pairs + 1, p1, a1)

    @pl.when(2 * pairs + 1 >= count)
    def _():
        gather(2 * pairs, p0, a0)

    for s in range(seqs):
        acc[s] = acc[s] / jnp.sum(l_ref[s], axis=1, keepdims=True)
    cols = vw_own.shape[1]
    for k, vw in enumerate((vw_own, vw_got)):
        for h in range(cols // HDIM):
            at = k * part + h * steps
            mixed = acc[:, at : at + steps, :].reshape(seqs * steps, -1).astype(BF16)
            value = dot(mixed, vw[:, h * HDIM : (h + 1) * HDIM], NN)
            flat[:, k * cols + h * HDIM : k * cols + (h + 1) * HDIM] = value.astype(BF16)
    _, _, y, core = here()
    count = seqs * steps
    each = steps // SIDE
    row = lax.broadcasted_iota(jnp.int32, (count, count), 0)
    col = lax.broadcasted_iota(jnp.int32, (count, count), 1)
    step = jnp.zeros((count, count), jnp.int32)
    for j, place in enumerate(turned(y, 1 - 2 * core)):
        step = jnp.where(lax.div(row, each * seqs) == j, each * place, step)
    step += lax.rem(lax.div(row, seqs), each)
    same = (step == lax.rem(col, steps)) & (lax.rem(row, seqs) == lax.div(col, steps))
    pick = jnp.where(same, 1.0, 0.0).astype(BF16)
    out_ref[...] = dot(pick, flat[...], NN).astype(BF16)


def attention(order, lengths, q_own, q_got, r_own, r_got, nl, nr, vw_own, vw_got, lat, rope):
    seqs, part, lat_rank = q_own.shape
    rows = 2 * part
    most = seqs * (lat.shape[1] // BLOCK) + 1
    steps = part * HDIM // vw_own.shape[1]
    out = jax.ShapeDtypeStruct((seqs * steps, 2 * vw_own.shape[1]), BF16)
    return pl.pallas_call(
        functools.partial(attention_body, steps=steps),
        in_specs=[SMEM, SMEM] + [VMEM] * 8 + [HBM] * 2,
        out_specs=VMEM,
        out_shape=out,
        scratch_shapes=[
            pltpu.VMEM((SLOTS, BLOCK, lat_rank), BF16),
            pltpu.VMEM((SLOTS, ROPE, BLOCK), BF16),
            pltpu.VMEM((seqs, rows, lat_rank), BF16),
            pltpu.VMEM((seqs, rows, ROPE), BF16),
            pltpu.VMEM((seqs, rows, lat_rank), F32),
            pltpu.VMEM((seqs, rows, 128), F32),
            pltpu.VMEM((seqs, rows, 128), F32),
            pltpu.VMEM(out.shape, BF16),
            pltpu.VMEM((rows, BLOCK), BF16),
            pltpu.VMEM((rows, BLOCK), BF16),
            pltpu.VMEM((rows, 128), F32),
            pltpu.VMEM((rows, 128), F32),
            pltpu.SMEM((most,), jnp.int32),
            pltpu.SMEM((most,), jnp.int32),
            pltpu.SemaphoreType.DMA((SLOTS,)),
            pltpu.SemaphoreType.DMA((SLOTS,)),
        ],
        compiler_params=room(40),
        name="attention",
    )(
        order,
        lengths,
        q_own,
        q_got,
        r_own,
        r_got,
        nl,
        nr,
        vw_own,
        vw_got,
        in_hbm(lat),
        in_hbm(rope),
    )


def join_weights_body(*refs):
    own_w, got_w, out = refs[:4], refs[4:8], refs[8]
    _, x, _, core = here()
    sign = 1 - 2 * core
    part, depth = own_w[0].shape
    for k, (weights, way) in enumerate(((own_w, -sign), (got_w, sign))):
        for place, ref in zip(turned(x, way), weights):
            at = pl.multiple_of(place * part, 64)
            out[pl.ds(at, part), k * depth : (k + 1) * depth] = ref[...]


def join_weights(own_w, got_w):
    part, depth = own_w[0].shape
    return pl.pallas_call(
        join_weights_body,
        in_specs=[VMEM] * 8,
        out_specs=VMEM,
        out_shape=jax.ShapeDtypeStruct((SIDE * part, 2 * depth), BF16),
        compiler_params=room(20),
        name="join_weights",
    )(*own_w, *got_w)


def output_body(t0, t1, t2, t3, w_ref, *refs, rows):
    outs, v_buf = refs[:4], refs[4]
    sign = 1 - 2 * here()[3]
    for place, ref in zip(turned(0, -sign), (t0, t1, t2, t3)):
        v_buf[place] = ref[...]
    tokens_all = v_buf[...].reshape(-1, v_buf.shape[2])
    width = 256
    for n in range(w_ref.shape[0] // width):
        cols = slice(n * width, (n + 1) * width)
        res = dot(tokens_all, w_ref[cols, :], NT).reshape(SIDE, SIDE, rows, width)
        for j in range(SIDE):
            for z in range(SIDE):
                outs[j][z, :, cols] = res[z, j].astype(BF16)


def output_blocks(tokens, weights):
    count, depth = tokens[0].shape
    rows = count // SIDE
    out = jax.ShapeDtypeStruct((SIDE, rows, weights.shape[0]), BF16)
    return pl.pallas_call(
        functools.partial(output_body, rows=rows),
        in_specs=[VMEM] * 5,
        out_specs=[VMEM] * 4,
        out_shape=[out] * 4,
        scratch_shapes=[pltpu.VMEM((SIDE, count, depth), BF16)],
        compiler_params=room(16),
        name="output_blocks",
    )(*tokens, weights)


def total_body(a, b, c, *outs):
    for k in (2, 1, 3, 0):
        outs[k][...] = (a[k].astype(F32) + b[k].astype(F32) + c[k].astype(F32)).astype(BF16)


def total_blocks(parts):
    one = jax.ShapeDtypeStruct(parts[0].shape[1:], BF16)
    return pl.pallas_call(
        total_body,
        in_specs=[VMEM] * 3,
        out_specs=[VMEM] * 4,
        out_shape=[one] * 4,
        compiler_params=room(8),
        name="total_blocks",
    )(*parts)


def columns_body(*refs):
    out = refs[-1]
    width = refs[0].shape[1]
    z = here()[0]
    for d, ref in enumerate(refs[:-1]):
        at = lax.rem(z + SIDE - d, SIDE) * width
        out[:, pl.ds(pl.multiple_of(at, 128), width)] = ref[...]


def join_columns(blocks):
    rows, width = blocks[0].shape
    return pl.pallas_call(
        columns_body,
        in_specs=[VMEM] * SIDE,
        out_specs=VMEM,
        out_shape=jax.ShapeDtypeStruct((rows, SIDE * width), BF16),
        compiler_params=room(8),
        name="join_columns",
    )(*blocks)


def settle_body(order_ref, *refs):
    blocks, out, buf = refs[:8], refs[8], refs[9]
    steps, seqs, cols = out.shape
    half = seqs // 2
    each = steps // SIDE
    count = steps * seqs
    size = each * half
    _, _, y, core = here()
    sign = 1 - 2 * core
    for k, ref in enumerate(blocks):
        buf[k * size : (k + 1) * size, :] = ref[...].astype(F32)
    row = lax.broadcasted_iota(jnp.int32, (count, count), 0)
    col = lax.broadcasted_iota(jnp.int32, (count, count), 1)
    step = jnp.zeros((count, count), jnp.int32)
    for k, place in enumerate(turned(y, -sign) + turned(y, sign)):
        step = jnp.where(lax.div(col, size) == k, each * place, step)
    step += lax.rem(lax.div(col, half), each)
    place = half * lax.div(col, SIDE * size) + lax.rem(col, half)
    seq = jnp.zeros((count, count), jnp.int32)
    for k in range(seqs):
        seq = jnp.where(place == k, order_ref[k], seq)
    same = (step == lax.div(row, seqs)) & (seq == lax.rem(row, seqs))
    pick = jnp.where(same, 1.0, 0.0).astype(BF16)
    width = 1024
    for n in range(cols // width):
        part = slice(n * width, (n + 1) * width)
        res = dot(pick, buf[:, part].astype(BF16), NN)
        out[:, :, part] = res.reshape(steps, seqs, width).astype(BF16)


def settle(order, blocks):
    rows, cols = blocks[0].shape
    return pl.pallas_call(
        settle_body,
        in_specs=[SMEM] + [VMEM] * 8,
        out_specs=VMEM,
        out_shape=jax.ShapeDtypeStruct((rows, 8, cols), BF16),
        scratch_shapes=[pltpu.VMEM((8 * rows, cols), F32)],
        compiler_params=room(12),
        name="settle",
    )(order, *blocks)


def splits(seqs):
    for rest in itertools.combinations(range(1, seqs), seqs // 2 - 1):
        mine = (0,) + rest
        yield mine + tuple(s for s in range(seqs) if s not in mine)


def prepare_body(
    len_ref,
    ql_ref,
    rw_ref,
    nl_ref,
    nr_ref,
    order_ref,
    length_ref,
    by_seq_ref,
    r_own,
    r_send,
    nl_out,
    nr_out,
    r_buf,
    *,
    core_of,
):
    core = core_of()
    steps, seqs, q_rank = ql_ref.shape
    half = seqs // 2
    count = steps * seqs

    blocks = [lax.div(len_ref[s] + (BLOCK - 1), BLOCK) for s in range(seqs)]
    whole = sum(blocks[1:], blocks[0])
    least, code = None, None
    for row in splits(seqs):
        part = blocks[0] + blocks[row[1]] + blocks[row[2]] + blocks[row[3]]
        larger = jnp.maximum(part, whole - part)
        digits = sum(s << (3 * k) for k, s in enumerate(row))
        if least is None:
            least, code = larger, jnp.int32(digits)
        else:
            code = jnp.where(larger < least, digits, code)
            least = jnp.minimum(larger, least)
    order, lengths = [], []
    for k in range(seqs):
        shift_by = jnp.where(core == 0, 3 * k, 3 * ((k + half) % seqs))
        order.append(lax.shift_right_logical(code, shift_by) & 7)
        lengths.append(len_ref[order[k]])
        order_ref[k] = order[k]
        length_ref[k] = lengths[k]

    def by_place(place, values):
        out = jnp.zeros(place.shape, jnp.int32)
        for k, value in enumerate(values):
            out = jnp.where(place == k, value, out)
        return out

    def pick(rows, depth, used):
        row = lax.broadcasted_iota(jnp.int32, (rows, count), 0)
        col = lax.broadcasted_iota(jnp.int32, (rows, count), 1)
        same = (by_place(lax.div(row, depth), order[:used]) == lax.rem(col, seqs)) & (
            lax.rem(row, depth) == lax.div(col, seqs)
        )
        return jnp.where(same, 1.0, 0.0).astype(BF16)

    by_seq = dot(pick(count, steps, seqs), ql_ref[...].reshape(count, q_rank), NN).astype(BF16)
    by_seq_ref[...] = by_seq

    turn = dot(by_seq, rw_ref[...], NN)
    cols = turn.shape[1]
    row = lax.broadcasted_iota(jnp.int32, (count, 128), 0)
    lane = lax.broadcasted_iota(jnp.int32, (count, 128), 1)
    position = (by_place(lax.div(row, steps), lengths) + lax.rem(row, steps)).astype(F32)
    index_f = lax.rem(lane, ROPE // 2).astype(F32)
    angle = position * jnp.exp(-math.log(10000.0) * 2.0 * index_f / ROPE)
    is_first = lax.rem(lane, ROPE) < ROPE // 2
    cosine = jnp.concatenate([jnp.cos(angle)] * (cols // 128), axis=1)
    sine = jnp.sin(angle)
    sine = jnp.concatenate([jnp.where(is_first, -sine, sine)] * (cols // 128), axis=1)
    is_first = lax.rem(lax.broadcasted_iota(jnp.int32, (count, cols), 1), ROPE) < ROPE // 2
    other = jnp.where(
        is_first,
        pltpu.roll(turn, cols - ROPE // 2, 1),
        pltpu.roll(turn, ROPE // 2, 1),
    )
    turn = turn * cosine + other * sine
    for h in range(cols // ROPE):
        piece = turn[:, h * ROPE : (h + 1) * ROPE].reshape(seqs, steps, ROPE)
        r_buf[:, h * steps : (h + 1) * steps, :] = piece
    r_own[...] = r_buf[:half].astype(BF16)
    r_send[...] = r_buf[half:].astype(BF16)

    width = nl_out.shape[1]
    chosen = pick(half * width, width, half)
    for src, out in ((nl_ref, nl_out), (nr_ref, nr_out)):
        rank = src.shape[2]
        rows = dot(chosen, src[...].reshape(count, rank), NN).astype(BF16)
        out[...] = rows.reshape(half, width, rank)


def prepare(lengths, ql, rw, nl, nr, core_of):
    steps, seqs, q_rank = ql.shape
    half = seqs // 2
    rows = rw.shape[1] // ROPE * steps
    turned_rows = jax.ShapeDtypeStruct((half, rows, ROPE), BF16)
    return pl.pallas_call(
        functools.partial(prepare_body, core_of=core_of),
        in_specs=[SMEM] + [VMEM] * 4,
        out_specs=[SMEM] * 2 + [VMEM] * 5,
        out_shape=[jax.ShapeDtypeStruct((seqs,), jnp.int32)] * 2
        + [jax.ShapeDtypeStruct((steps * seqs, q_rank), BF16)]
        + [turned_rows] * 2
        + [jax.ShapeDtypeStruct((half, 128, v.shape[2]), BF16) for v in (nl, nr)],
        scratch_shapes=[pltpu.VMEM((seqs, rows, ROPE), F32)],
        compiler_params=room(12),
        name="prepare",
    )(lengths, ql, rw, nl, nr)


def body(
    grad_parts,
    params,
    moment_one,
    moment_two,
    query_latent,
    rope_weight,
    value_weight,
    out_weight,
    latent_cache,
    rope_cache,
    new_latent,
    new_rope,
    lengths,
):
    send, keep, params, moment_one, moment_two = pack(
        grad_parts[0], params, moment_one, moment_two
    )
    own_sum, *sums = add_columns(keep, other_core(send))
    parts_a = ring_sum(sums[:3], "y")
    parts_b = ring_sum(sums[3:], "y")
    w_a = adam_first(own_sum, parts_a, params, moment_one, moment_two)
    new_params, new_one, new_two, w_b = adam(
        own_sum, parts_a + parts_b, params, moment_one, moment_two, w_a
    )

    w_t = out_weight.T
    w_one, w_two = forth(w_t, "x"), back(w_t, "x")

    lengths, _ = lax.optimization_barrier((lengths, sums[5]))
    steps_n, seq_local, q_rank = query_latent.shape
    order, lengths_in, by_seq, r_own, r_send, nl, nr = prepare(
        lengths, query_latent, rope_weight, new_latent, new_rope, lambda: here()[3]
    )
    r_got = other_core(r_send)

    (w_one, w_two), units = spread(w_a, 1, (w_one, w_two))
    _, more = spread(w_b, -1)
    units += more

    w_rows = SIDE * SIDE * params.shape[0]
    by_seq, r_got, vw_got = lax.optimization_barrier((by_seq, r_got, other_core(value_weight)))
    q_own, q_send = queries(by_seq, units, w_rows, seq_local, q_rank)
    w_one, q_send = lax.optimization_barrier((w_one, q_send))
    w_three = forth(w_one, "x")
    q_got, *early = lax.optimization_barrier((other_core(q_send), w_t, w_one, w_two))
    got_w = [other_core(w) for w in early]
    values = attention(
        order,
        lengths_in,
        q_own,
        q_got,
        r_own,
        r_got,
        nl,
        nr,
        value_weight,
        vw_got,
        latent_cache,
        rope_cache,
    )

    *got_w, w_three, values = lax.optimization_barrier((*got_w, w_three, values))
    own_w = (w_t, w_one, w_two, w_three)
    tokens = ring(values, "z")
    got_w.append(other_core(w_three))
    own, *sums = output_blocks(tokens, join_weights(own_w, got_w))
    blocks = total_blocks((own,) + ring_sum(sums, "y"))

    arrived = [blocks[0]]
    for d in range(1, SIDE):
        perm = [
            (zz * SIDE + xx, ((zz + d) % SIDE) * SIDE + xx)
            for zz in range(SIDE)
            for xx in range(SIDE)
        ]
        arrived.append(lax.ppermute(blocks[d], "fsdp", perm))
    mine = join_columns(arrived)

    column = list(ring(mine, "y"))
    column += [other_core(b) for b in column]
    decoded = settle(order, column)
    return (new_params, new_one, new_two, decoded)


def solution(mesh):
    return jax.shard_map(
        body,
        mesh=mesh,
        in_specs=(
            P("head", "fsdp", None),
            P("fsdp", "head"),
            P("fsdp", "head"),
            P("fsdp", "head"),
            P(None, "fsdp", None),
            P(None, "head"),
            P(None, "head"),
            P("head", "fsdp"),
            P("fsdp", None, None),
            P("fsdp", None, None),
            P(None, "fsdp", None),
            P(None, "fsdp", None),
            P("fsdp"),
        ),
        out_specs=(P("fsdp", "head"), P("fsdp", "head"), P("fsdp", "head"), P(None, "fsdp", None)),
        check_vma=False,
    )
```

```python
import functools
import itertools
import math

import jax
import jax.numpy as jnp
import numpy as np
from jax import lax
from jax.experimental import pallas as pl
from jax.experimental.pallas import tpu as pltpu
from jax.sharding import PartitionSpec as P

HDIM = 128
ROPE = 64
SIDE = 4
BLOCK = 1024
SLOTS = 12
MIB = 1024 * 1024

first_fix = 1.0 - math.exp(100.0 * math.log(0.9))
second_fix = 1.0 - math.exp(100.0 * math.log(0.999))
NEG = -1e30
LOG2E = math.log2(math.e)

NT = (((1,), (1,)), ((), ()))
NN = (((1,), (0,)), ((), ()))


def dot(a, b, dims):
    return lax.dot_general(a, b, dims, preferred_element_type=jnp.float32)


def moves(step):
    perm = []
    for z in range(SIDE):
        for x in range(SIDE):
            for y in range(SIDE):
                for c in range(2):
                    axis, to_place = step(c)
                    to = {"x": x, "y": y, "z": z}
                    to[axis] = to_place(to[axis]) % SIDE
                    perm.append(
                        (
                            (z * SIDE + x) * 2 * SIDE + y * 2 + c,
                            (to["z"] * SIDE + to["x"]) * 2 * SIDE + to["y"] * 2 + c,
                        )
                    )
    return perm


def shift(v, step):
    return lax.ppermute(v, ("fsdp", "head"), moves(step))


def forth(v, axis):
    return shift(v, lambda c: (axis, lambda i: i + 1 - 2 * c))


def back(v, axis):
    return shift(v, lambda c: (axis, lambda i: i + 2 * c - 1))


def first(v, d):
    return shift(v, lambda c: (("x", "z")[c], lambda i: i + d))


def second(v, d):
    return shift(v, lambda c: (("z", "x")[c], lambda i: i + d))


def other_core(v):
    return lax.ppermute(v, "head", [(i, i ^ 1) for i in range(2 * SIDE)])


def ring(own, axis):
    one = forth(own, axis)
    two = back(own, axis)
    return own, one, two, forth(one, axis)


def ring_sum(blocks, axis):
    far = forth(blocks[2], axis)
    two = back(blocks[1], axis)
    return forth(add_two(blocks[0], far), axis), two


def here():
    f = lax.axis_index("fsdp")
    h = lax.axis_index("head")
    return lax.div(f, SIDE), lax.rem(f, SIDE), lax.div(h, 2), lax.rem(h, 2)


def turned(base, s):
    return [lax.rem(base + d, SIDE) for d in (0, SIDE + s, SIDE - s, 2)]


VMEM = pl.BlockSpec(memory_space=pltpu.VMEM)
SMEM = pl.BlockSpec(memory_space=pltpu.SMEM)
HBM = pl.BlockSpec(memory_space=pltpu.HBM)
F32 = jnp.float32
BF16 = jnp.bfloat16


def in_hbm(v):
    return pltpu.with_memory_space_constraint(v, pltpu.HBM)


def room(mib):
    return pltpu.CompilerParams(vmem_limit_bytes=mib * MIB)


def add_two_body(a, b, o):
    o[...] = (a[...].astype(F32) + b[...].astype(F32)).astype(o.dtype)


def add_two(a, b):
    return pl.pallas_call(
        add_two_body,
        in_specs=[VMEM] * 2,
        out_specs=VMEM,
        out_shape=jax.ShapeDtypeStruct(a.shape, BF16),
        compiler_params=room(8),
        name="add_two",
    )(a, b)


def pack_body(g_ref, p, one, two, send_ref, keep_ref, p_out, one_out, two_out, sem):
    _, _, y, core = here()
    sign = 1 - 2 * core
    cols = send_ref.shape[2]
    copies = []
    for ref, places, c in (
        (send_ref, turned(y, -sign), 1 - core),
        (keep_ref, turned(y, sign), core),
    ):
        for j, place in enumerate(places):
            at = pl.multiple_of((2 * place + c) * cols, 128)
            copies.append(
                pltpu.make_async_copy(
                    g_ref.at[:, pl.ds(at, cols)], ref.at[j], sem.at[len(copies)]
                )
            )
    for src, dst in ((p, p_out), (one, one_out), (two, two_out)):
        copies.append(pltpu.make_async_copy(src, dst, sem.at[len(copies)]))
    for copy in copies:
        copy.start()
    for copy in copies:
        copy.wait()


def pack(g, p, one, two):
    out = jax.ShapeDtypeStruct((SIDE, g.shape[0], g.shape[1] // (2 * SIDE)), g.dtype)
    return pl.pallas_call(
        pack_body,
        in_specs=[HBM] * 4,
        out_specs=[VMEM] * 5,
        out_shape=[out] * 2 + [jax.ShapeDtypeStruct(p.shape, F32)] * 3,
        scratch_shapes=[pltpu.SemaphoreType.DMA((2 * SIDE + 3,))],
        compiler_params=room(8),
        name="pack_columns",
    )(*(in_hbm(v) for v in (g, p, one, two)))


def add_columns_body(keep, got, own, *parts):
    rows, cols = own.shape
    width = cols // 2
    for j in (3, 2, 1, 0):
        for r in range(0, rows, 16):
            part = slice(r, r + 16)
            total = keep[j, part, :].astype(F32) + got[j, part, :].astype(F32)
            if j == 0:
                own[part, :] = total
            else:
                parts[j - 1][part, :] = total[:, :width].astype(BF16)
                parts[j + 2][part, :] = total[:, width:].astype(BF16)


def add_columns(keep, got):
    rows, cols = got.shape[1:]
    half = jax.ShapeDtypeStruct((rows, cols // 2), BF16)
    return pl.pallas_call(
        add_columns_body,
        in_specs=[VMEM] * 2,
        out_specs=[VMEM] * 7,
        out_shape=[jax.ShapeDtypeStruct((rows, cols), F32)] + [half] * 6,
        compiler_params=room(8),
        name="add_columns",
    )(keep, got)


def adam_step(grad, p, one, two):
    step_size = 0.003 / first_fix
    moment = 0.9 * one + 0.1 * grad
    second_moment = 0.999 * two + 0.001 * grad * grad
    denom = jnp.sqrt(second_moment / second_fix) + 1e-08
    return p - step_size * moment / denom, moment, second_moment


def adam_first_body(r0, r1, r2, p, one, two, w):
    width = w.shape[1]
    cols = slice(0, width)
    for r in range(0, p.shape[0], 16):
        part = slice(r, r + 16)
        grad = r0[part, cols] + r1[part].astype(F32) + r2[part].astype(F32)
        w[part] = adam_step(grad, p[part, cols], one[part, cols], two[part, cols])[0].astype(BF16)


def adam_first(own, parts, p, one, two):
    rows, cols = p.shape
    return pl.pallas_call(
        adam_first_body,
        in_specs=[VMEM] * 6,
        out_specs=VMEM,
        out_shape=jax.ShapeDtypeStruct((rows, cols // 2), BF16),
        compiler_params=room(12),
        name="adam_first",
    )(own, *parts, p, one, two)


def adam_body(r0, a1, a2, b1, b2, p, one, two, after, new_p, new_one, new_two, w):
    del after
    width = w.shape[1]
    for r in range(0, p.shape[0], 16):
        part = slice(r, r + 16)
        for k, (r1, r2) in ((1, (b1, b2)), (0, (a1, a2))):
            cols = slice(k * width, (k + 1) * width)
            grad = r0[part, cols] + r1[part].astype(F32) + r2[part].astype(F32)
            params, moment, second_moment = adam_step(
                grad, p[part, cols], one[part, cols], two[part, cols]
            )
            if k:
                w[part] = params.astype(BF16)
            new_p[part, cols] = params
            new_one[part, cols] = moment
            new_two[part, cols] = second_moment


def adam(own, parts, p, one, two, after):
    rows, cols = p.shape
    full = jax.ShapeDtypeStruct(p.shape, F32)
    return pl.pallas_call(
        adam_body,
        in_specs=[VMEM] * 8 + [pl.BlockSpec(memory_space=pl.ANY)],
        out_specs=[VMEM] * 4,
        out_shape=[full] * 3 + [jax.ShapeDtypeStruct((rows, cols // 2), BF16)],
        compiler_params=room(12),
        name="adam",
    )(own, *parts, p, one, two, after)


def stack_body(*refs):
    out = refs[-1]
    rows = refs[0].shape[0]
    for k, ref in enumerate(refs[:-1]):
        out[k * rows : (k + 1) * rows, :] = ref[...]


def stack_rows(*blocks):
    rows, cols = blocks[0].shape
    return pl.pallas_call(
        stack_body,
        in_specs=[VMEM] * len(blocks),
        out_specs=VMEM,
        out_shape=jax.ShapeDtypeStruct((len(blocks) * rows, cols), blocks[0].dtype),
        compiler_params=room(8),
        name="stack_rows",
    )(*blocks)


def spread(w, d, also=()):
    above, below = first(w, 1), first(w, -1)
    unit = stack_rows(w, above, below, first(above if d > 0 else below, d))
    unit, *also = lax.optimization_barrier((unit,) + tuple(also))
    up, down = second(unit, 1), second(unit, -1)
    return also, [unit, up, down, second(up if d > 0 else down, d)]


def query_body(ql_ref, *refs, seqs, steps, heads, q_rank):
    units = refs[:8]
    keep_ref, send_ref, w_buf, lat_buf = refs[8:]
    z, x, _, core = here()
    shard = w_buf.shape[0] // (SIDE * SIDE)
    far = (0, SIDE - 1, 1, 2)
    width = w_buf.shape[1] // 2
    for k in range(SIDE):
        for m in range(SIDE):
            zo = jnp.where(core == 0, far[k], far[m])
            xo = jnp.where(core == 0, far[m], far[k])
            f = lax.rem(z + zo, SIDE) * SIDE + lax.rem(x + xo, SIDE)
            at = pl.multiple_of(f * shard, shard)
            rows = slice(m * shard, (m + 1) * shard)
            for h in range(2):
                cols = slice(h * width, (h + 1) * width)
                w_buf[pl.ds(at, shard), cols] = units[4 * h + k][rows, :]
    nope = dot(ql_ref[...], w_buf[:q_rank, :], NN).astype(BF16)
    for h in range(heads):
        cols = slice(h * HDIM, (h + 1) * HDIM)
        lat = dot(nope[:, cols], w_buf[q_rank:, cols], NT)
        lat_buf[:, h * steps : (h + 1) * steps, :] = lat.reshape(seqs, steps, -1)
    keep_ref[...] = lat_buf[: seqs // 2].astype(BF16)
    send_ref[...] = lat_buf[seqs // 2 :].astype(BF16)


def queries(ql, units, w_rows, seqs, q_rank):
    cols = 2 * units[0].shape[1]
    heads = cols // HDIM
    steps = ql.shape[0] // seqs
    lat_rank = w_rows - q_rank
    out = jax.ShapeDtypeStruct((seqs // 2, heads * steps, lat_rank), BF16)
    return pl.pallas_call(
        functools.partial(query_body, seqs=seqs, steps=steps, heads=heads, q_rank=q_rank),
        in_specs=[VMEM] * 9,
        out_specs=[VMEM] * 2,
        out_shape=[out] * 2,
        scratch_shapes=[
            pltpu.VMEM((w_rows, cols), BF16),
            pltpu.VMEM((seqs, heads * steps, lat_rank), F32),
        ],
        compiler_params=room(16),
        name="queries",
    )(ql, *units)


def attention_body(
    order_ref,
    len_ref,
    q_own,
    q_got,
    r_own,
    r_got,
    nl_ref,
    nr_ref,
    vw_own,
    vw_got,
    lat_hbm,
    rope_hbm,
    out_ref,
    lat_buf,
    rope_buf,
    q_buf,
    qr_buf,
    acc,
    m_ref,
    l_ref,
    flat,
    p0,
    p1,
    a0,
    a1,
    seq_of,
    blk_of,
    lat_sem,
    rope_sem,
    *,
    steps,
):
    seqs, rows, _ = q_buf.shape
    part = rows // 2
    factor = LOG2E / math.sqrt(HDIM + ROPE)

    def listing(s, at):
        blocks = lax.div(len_ref[s] + (BLOCK - 1), BLOCK)

        def put(j, at):
            seq_of[at] = s
            blk_of[at] = j
            return at + 1

        return lax.fori_loop(0, blocks, put, at)

    count = lax.fori_loop(0, seqs, listing, 0)

    def lat_copy(i):
        slot = lax.rem(i, SLOTS)
        start = pl.multiple_of(blk_of[i] * BLOCK, BLOCK)
        return pltpu.make_async_copy(
            lat_hbm.at[order_ref[seq_of[i]], pl.ds(start, BLOCK), :],
            lat_buf.at[slot],
            lat_sem.at[slot],
        )

    def rope_copy(i):
        slot = lax.rem(i, SLOTS)
        start = pl.multiple_of(blk_of[i] * BLOCK, BLOCK)
        return pltpu.make_async_copy(
            rope_hbm.at[order_ref[seq_of[i]], :, pl.ds(start, BLOCK)],
            rope_buf.at[slot],
            rope_sem.at[slot],
        )

    def fetch(i):
        @pl.when(i < count)
        def _():
            lat_copy(i).start()
            rope_copy(i).start()

    for i in range(SLOTS - 2):
        fetch(i)

    q_buf[:, :part, :] = q_own[...]
    q_buf[:, part:, :] = q_got[...]
    qr_buf[:, :part, :] = r_own[...]
    qr_buf[:, part:, :] = r_got[...]

    width = nl_ref.shape[1]
    token = lax.broadcasted_iota(jnp.int32, (rows, width), 1)
    step = lax.rem(lax.broadcasted_iota(jnp.int32, (rows, width), 0), steps)
    seen = token <= step
    for s in range(seqs):
        score = dot(q_buf[s], nl_ref[s], NT) + dot(qr_buf[s], nr_ref[s], NT)
        score = jnp.where(seen, score, NEG)
        top = jnp.max(score, axis=1, keepdims=True)
        prob = jnp.exp2((score - top) * factor)
        m_ref[s] = jnp.broadcast_to(top, (rows, 128))
        l_ref[s] = prob
        acc[s] = dot(prob.astype(BF16), nl_ref[s], NN)

    lane = lax.broadcasted_iota(jnp.int32, (rows, BLOCK), 1)

    def arrive(i):
        lat_copy(i).wait()
        rope_copy(i).wait()

    def scores(i):
        slot = lax.rem(i, SLOTS)
        s = seq_of[i]
        return dot(q_buf[s], lat_buf[slot], NT) + dot(qr_buf[s], rope_buf[slot], NN)

    def weigh(i, score, p_ref, a_ref):
        s = seq_of[i]
        score = jnp.where(lane < len_ref[s] - blk_of[i] * BLOCK, score, NEG)
        before = m_ref[s]
        top = jnp.maximum(before, jnp.max(score, axis=1, keepdims=True))
        prob = jnp.exp2((score - top[:, :1]) * factor)
        alpha = jnp.exp2((before - top) * factor)
        total = l_ref[s] * alpha
        for k in range(BLOCK // 128):
            total += prob[:, k * 128 : (k + 1) * 128]
        m_ref[s] = top
        l_ref[s] = total
        a_ref[...] = alpha
        p_ref[...] = prob.astype(BF16)

    def gather(i, p_ref, a_ref):
        slot = lax.rem(i, SLOTS)
        s = seq_of[i]
        acc[s] = acc[s] * a_ref[:, :1] + dot(p_ref[...], lat_buf[slot], NN)

    arrive(0)
    weigh(0, scores(0), p0, a0)

    def pair(k, carry):
        i = 2 * k
        fetch(i + SLOTS - 2)
        fetch(i + SLOTS - 1)
        arrive(i + 1)
        arrive(i + 2)
        odd = scores(i + 1)
        gather(i, p0, a0)
        even = scores(i + 2)
        weigh(i + 1, odd, p1, a1)
        gather(i + 1, p1, a1)
        weigh(i + 2, even, p0, a0)
        return carry

    pairs = lax.div(count - 1, 2)
    lax.fori_loop(0, pairs, pair, 0)

    @pl.when(2 * pairs + 1 < count)
    def _():
        arrive(2 * pairs + 1)
        odd = scores(2 * pairs + 1)
        gather(2 * pairs, p0, a0)
        weigh(2 * pairs + 1, odd, p1, a1)
        gather(2 * pairs + 1, p1, a1)

    @pl.when(2 * pairs + 1 >= count)
    def _():
        gather(2 * pairs, p0, a0)

    for s in range(seqs):
        acc[s] = acc[s] / jnp.sum(l_ref[s], axis=1, keepdims=True)
    cols = vw_own.shape[1]
    for k, vw in enumerate((vw_own, vw_got)):
        for h in range(cols // HDIM):
            at = k * part + h * steps
            mixed = acc[:, at : at + steps, :].reshape(seqs * steps, -1).astype(BF16)
            value = dot(mixed, vw[:, h * HDIM : (h + 1) * HDIM], NN)
            flat[:, k * cols + h * HDIM : k * cols + (h + 1) * HDIM] = value.astype(BF16)
    _, _, y, core = here()
    count = seqs * steps
    each = steps // SIDE
    row = lax.broadcasted_iota(jnp.int32, (count, count), 0)
    col = lax.broadcasted_iota(jnp.int32, (count, count), 1)
    step = jnp.zeros((count, count), jnp.int32)
    for j, place in enumerate(turned(y, 1 - 2 * core)):
        step = jnp.where(lax.div(row, each * seqs) == j, each * place, step)
    step += lax.rem(lax.div(row, seqs), each)
    same = (step == lax.rem(col, steps)) & (lax.rem(row, seqs) == lax.div(col, steps))
    pick = jnp.where(same, 1.0, 0.0).astype(BF16)
    out_ref[...] = dot(pick, flat[...], NN).astype(BF16)


def attention(order, lengths, q_own, q_got, r_own, r_got, nl, nr, vw_own, vw_got, lat, rope):
    seqs, part, lat_rank = q_own.shape
    rows = 2 * part
    most = seqs * (lat.shape[1] // BLOCK) + 1
    steps = part * HDIM // vw_own.shape[1]
    out = jax.ShapeDtypeStruct((seqs * steps, 2 * vw_own.shape[1]), BF16)
    return pl.pallas_call(
        functools.partial(attention_body, steps=steps),
        in_specs=[SMEM, SMEM] + [VMEM] * 8 + [HBM] * 2,
        out_specs=VMEM,
        out_shape=out,
        scratch_shapes=[
            pltpu.VMEM((SLOTS, BLOCK, lat_rank), BF16),
            pltpu.VMEM((SLOTS, ROPE, BLOCK), BF16),
            pltpu.VMEM((seqs, rows, lat_rank), BF16),
            pltpu.VMEM((seqs, rows, ROPE), BF16),
            pltpu.VMEM((seqs, rows, lat_rank), F32),
            pltpu.VMEM((seqs, rows, 128), F32),
            pltpu.VMEM((seqs, rows, 128), F32),
            pltpu.VMEM(out.shape, BF16),
            pltpu.VMEM((rows, BLOCK), BF16),
            pltpu.VMEM((rows, BLOCK), BF16),
            pltpu.VMEM((rows, 128), F32),
            pltpu.VMEM((rows, 128), F32),
            pltpu.SMEM((most,), jnp.int32),
            pltpu.SMEM((most,), jnp.int32),
            pltpu.SemaphoreType.DMA((SLOTS,)),
            pltpu.SemaphoreType.DMA((SLOTS,)),
        ],
        compiler_params=room(40),
        name="attention",
    )(
        order,
        lengths,
        q_own,
        q_got,
        r_own,
        r_got,
        nl,
        nr,
        vw_own,
        vw_got,
        in_hbm(lat),
        in_hbm(rope),
    )


def join_weights_body(*refs):
    own_w, got_w, out = refs[:4], refs[4:8], refs[8]
    _, x, _, core = here()
    sign = 1 - 2 * core
    part, depth = own_w[0].shape
    for k, (weights, way) in enumerate(((own_w, -sign), (got_w, sign))):
        for place, ref in zip(turned(x, way), weights):
            at = pl.multiple_of(place * part, 64)
            out[pl.ds(at, part), k * depth : (k + 1) * depth] = ref[...]


def join_weights(own_w, got_w):
    part, depth = own_w[0].shape
    return pl.pallas_call(
        join_weights_body,
        in_specs=[VMEM] * 8,
        out_specs=VMEM,
        out_shape=jax.ShapeDtypeStruct((SIDE * part, 2 * depth), BF16),
        compiler_params=room(20),
        name="join_weights",
    )(*own_w, *got_w)


def output_body(t0, t1, t2, t3, w_ref, *refs, rows):
    outs, v_buf = refs[:4], refs[4]
    sign = 1 - 2 * here()[3]
    for place, ref in zip(turned(0, -sign), (t0, t1, t2, t3)):
        v_buf[place] = ref[...]
    tokens_all = v_buf[...].reshape(-1, v_buf.shape[2])
    width = 256
    for n in range(w_ref.shape[0] // width):
        cols = slice(n * width, (n + 1) * width)
        res = dot(tokens_all, w_ref[cols, :], NT).reshape(SIDE, SIDE, rows, width)
        for j in range(SIDE):
            for z in range(SIDE):
                outs[j][z, :, cols] = res[z, j].astype(BF16)


def output_blocks(tokens, weights):
    count, depth = tokens[0].shape
    rows = count // SIDE
    out = jax.ShapeDtypeStruct((SIDE, rows, weights.shape[0]), BF16)
    return pl.pallas_call(
        functools.partial(output_body, rows=rows),
        in_specs=[VMEM] * 5,
        out_specs=[VMEM] * 4,
        out_shape=[out] * 4,
        scratch_shapes=[pltpu.VMEM((SIDE, count, depth), BF16)],
        compiler_params=room(16),
        name="output_blocks",
    )(*tokens, weights)


def total_body(a, b, c, *outs):
    for k in (2, 1, 3, 0):
        outs[k][...] = (a[k].astype(F32) + b[k].astype(F32) + c[k].astype(F32)).astype(BF16)


def total_blocks(parts):
    one = jax.ShapeDtypeStruct(parts[0].shape[1:], BF16)
    return pl.pallas_call(
        total_body,
        in_specs=[VMEM] * 3,
        out_specs=[VMEM] * 4,
        out_shape=[one] * 4,
        compiler_params=room(8),
        name="total_blocks",
    )(*parts)


def columns_body(*refs):
    out = refs[-1]
    width = refs[0].shape[1]
    z = here()[0]
    for d, ref in enumerate(refs[:-1]):
        at = lax.rem(z + SIDE - d, SIDE) * width
        out[:, pl.ds(pl.multiple_of(at, 128), width)] = ref[...]


def join_columns(blocks):
    rows, width = blocks[0].shape
    return pl.pallas_call(
        columns_body,
        in_specs=[VMEM] * SIDE,
        out_specs=VMEM,
        out_shape=jax.ShapeDtypeStruct((rows, SIDE * width), BF16),
        compiler_params=room(8),
        name="join_columns",
    )(*blocks)


def settle_body(order_ref, *refs):
    blocks, out = refs[:8], refs[8]
    steps, seqs, cols = out.shape
    half = seqs // 2
    each = steps // SIDE
    count = steps * seqs
    size = each * half
    _, _, y, core = here()
    sign = 1 - 2 * core
    row = lax.broadcasted_iota(jnp.int32, (count, count), 0)
    col = lax.broadcasted_iota(jnp.int32, (count, count), 1)
    step = jnp.zeros((count, count), jnp.int32)
    for k, place in enumerate(turned(y, -sign) + turned(y, sign)):
        step = jnp.where(lax.div(col, size) == k, each * place, step)
    step += lax.rem(lax.div(col, half), each)
    place = half * lax.div(col, SIDE * size) + lax.rem(col, half)
    seq = jnp.zeros((count, count), jnp.int32)
    for k in range(seqs):
        seq = jnp.where(place == k, order_ref[k], seq)
    same = (step == lax.div(row, seqs)) & (seq == lax.rem(row, seqs))
    pick = jnp.where(same, 1.0, 0.0).astype(BF16)
    width = 1024
    for n in range(cols // width):
        part = slice(n * width, (n + 1) * width)
        rows = jnp.concatenate([ref[:, part].astype(F32) for ref in blocks], axis=0)
        res = dot(pick, rows.astype(BF16), NN)
        out[:, :, part] = res.reshape(steps, seqs, width).astype(BF16)


def settle(order, blocks):
    rows, cols = blocks[0].shape
    return pl.pallas_call(
        settle_body,
        in_specs=[SMEM] + [VMEM] * 8,
        out_specs=VMEM,
        out_shape=jax.ShapeDtypeStruct((rows, 8, cols), BF16),
        compiler_params=room(12),
        name="settle",
    )(order, *blocks)


def splits(seqs):
    for rest in itertools.combinations(range(1, seqs), seqs // 2 - 1):
        mine = (0,) + rest
        yield mine + tuple(s for s in range(seqs) if s not in mine)


def prepare_body(
    len_ref,
    ql_ref,
    rw_ref,
    nl_ref,
    nr_ref,
    order_ref,
    length_ref,
    by_seq_ref,
    r_own,
    r_send,
    nl_out,
    nr_out,
    r_buf,
    *,
    core_of,
):
    core = core_of()
    steps, seqs, q_rank = ql_ref.shape
    half = seqs // 2
    count = steps * seqs

    blocks = [lax.div(len_ref[s] + (BLOCK - 1), BLOCK) for s in range(seqs)]
    whole = sum(blocks[1:], blocks[0])
    least, code = None, None
    for row in splits(seqs):
        part = blocks[0] + blocks[row[1]] + blocks[row[2]] + blocks[row[3]]
        larger = jnp.maximum(part, whole - part)
        digits = sum(s << (3 * k) for k, s in enumerate(row))
        if least is None:
            least, code = larger, jnp.int32(digits)
        else:
            code = jnp.where(larger < least, digits, code)
            least = jnp.minimum(larger, least)
    order, lengths = [], []
    for k in range(seqs):
        shift_by = jnp.where(core == 0, 3 * k, 3 * ((k + half) % seqs))
        order.append(lax.shift_right_logical(code, shift_by) & 7)
        lengths.append(len_ref[order[k]])
        order_ref[k] = order[k]
        length_ref[k] = lengths[k]

    def by_place(place, values):
        out = jnp.zeros(place.shape, jnp.int32)
        for k, value in enumerate(values):
            out = jnp.where(place == k, value, out)
        return out

    def pick(rows, depth, used):
        row = lax.broadcasted_iota(jnp.int32, (rows, count), 0)
        col = lax.broadcasted_iota(jnp.int32, (rows, count), 1)
        same = (by_place(lax.div(row, depth), order[:used]) == lax.rem(col, seqs)) & (
            lax.rem(row, depth) == lax.div(col, seqs)
        )
        return jnp.where(same, 1.0, 0.0).astype(BF16)

    by_seq = dot(pick(count, steps, seqs), ql_ref[...].reshape(count, q_rank), NN).astype(BF16)
    by_seq_ref[...] = by_seq

    turn = dot(by_seq, rw_ref[...], NN)
    cols = turn.shape[1]
    row = lax.broadcasted_iota(jnp.int32, (count, 128), 0)
    lane = lax.broadcasted_iota(jnp.int32, (count, 128), 1)
    position = (by_place(lax.div(row, steps), lengths) + lax.rem(row, steps)).astype(F32)
    index_f = lax.rem(lane, ROPE // 2).astype(F32)
    angle = position * jnp.exp(-math.log(10000.0) * 2.0 * index_f / ROPE)
    is_first = lax.rem(lane, ROPE) < ROPE // 2
    cosine = jnp.concatenate([jnp.cos(angle)] * (cols // 128), axis=1)
    sine = jnp.sin(angle)
    sine = jnp.concatenate([jnp.where(is_first, -sine, sine)] * (cols // 128), axis=1)
    is_first = lax.rem(lax.broadcasted_iota(jnp.int32, (count, cols), 1), ROPE) < ROPE // 2
    other = jnp.where(
        is_first,
        pltpu.roll(turn, cols - ROPE // 2, 1),
        pltpu.roll(turn, ROPE // 2, 1),
    )
    turn = turn * cosine + other * sine
    for h in range(cols // ROPE):
        piece = turn[:, h * ROPE : (h + 1) * ROPE].reshape(seqs, steps, ROPE)
        r_buf[:, h * steps : (h + 1) * steps, :] = piece
    r_own[...] = r_buf[:half].astype(BF16)
    r_send[...] = r_buf[half:].astype(BF16)

    width = nl_out.shape[1]
    chosen = pick(half * width, width, half)
    for src, out in ((nl_ref, nl_out), (nr_ref, nr_out)):
        rank = src.shape[2]
        rows = dot(chosen, src[...].reshape(count, rank), NN).astype(BF16)
        out[...] = rows.reshape(half, width, rank)


def prepare(lengths, ql, rw, nl, nr, core_of):
    steps, seqs, q_rank = ql.shape
    half = seqs // 2
    rows = rw.shape[1] // ROPE * steps
    turned_rows = jax.ShapeDtypeStruct((half, rows, ROPE), BF16)
    return pl.pallas_call(
        functools.partial(prepare_body, core_of=core_of),
        in_specs=[SMEM] + [VMEM] * 4,
        out_specs=[SMEM] * 2 + [VMEM] * 5,
        out_shape=[jax.ShapeDtypeStruct((seqs,), jnp.int32)] * 2
        + [jax.ShapeDtypeStruct((steps * seqs, q_rank), BF16)]
        + [turned_rows] * 2
        + [jax.ShapeDtypeStruct((half, 128, v.shape[2]), BF16) for v in (nl, nr)],
        scratch_shapes=[pltpu.VMEM((seqs, rows, ROPE), F32)],
        compiler_params=room(12),
        name="prepare",
    )(lengths, ql, rw, nl, nr)


def body(
    grad_parts,
    params,
    moment_one,
    moment_two,
    query_latent,
    rope_weight,
    value_weight,
    out_weight,
    latent_cache,
    rope_cache,
    new_latent,
    new_rope,
    lengths,
):
    send, keep, params, moment_one, moment_two = pack(
        grad_parts[0], params, moment_one, moment_two
    )
    own_sum, *sums = add_columns(keep, other_core(send))
    parts_a = ring_sum(sums[:3], "y")
    parts_b = ring_sum(sums[3:], "y")
    w_a = adam_first(own_sum, parts_a, params, moment_one, moment_two)
    new_params, new_one, new_two, w_b = adam(
        own_sum, parts_a + parts_b, params, moment_one, moment_two, w_a
    )

    w_t = out_weight.T
    w_one, w_two = forth(w_t, "x"), back(w_t, "x")

    lengths, _ = lax.optimization_barrier((lengths, sums[5]))
    steps_n, seq_local, q_rank = query_latent.shape
    order, lengths_in, by_seq, r_own, r_send, nl, nr = prepare(
        lengths, query_latent, rope_weight, new_latent, new_rope, lambda: here()[3]
    )
    r_got = other_core(r_send)

    (w_one, w_two), units = spread(w_a, 1, (w_one, w_two))
    _, more = spread(w_b, -1)
    units += more

    w_rows = SIDE * SIDE * params.shape[0]
    by_seq, r_got, vw_got = lax.optimization_barrier((by_seq, r_got, other_core(value_weight)))
    q_own, q_send = queries(by_seq, units, w_rows, seq_local, q_rank)
    w_one, q_send = lax.optimization_barrier((w_one, q_send))
    w_three = forth(w_one, "x")
    q_got, *early = lax.optimization_barrier((other_core(q_send), w_t, w_one, w_two))
    got_w = [other_core(w) for w in early]
    values = attention(
        order,
        lengths_in,
        q_own,
        q_got,
        r_own,
        r_got,
        nl,
        nr,
        value_weight,
        vw_got,
        latent_cache,
        rope_cache,
    )

    *got_w, w_three, values = lax.optimization_barrier((*got_w, w_three, values))
    own_w = (w_t, w_one, w_two, w_three)
    tokens = ring(values, "z")
    got_w.append(other_core(w_three))
    own, *sums = output_blocks(tokens, join_weights(own_w, got_w))
    blocks = total_blocks((own,) + ring_sum(sums, "y"))

    arrived = [blocks[0]]
    for d in range(1, SIDE):
        perm = [
            (zz * SIDE + xx, ((zz + d) % SIDE) * SIDE + xx)
            for zz in range(SIDE)
            for xx in range(SIDE)
        ]
        arrived.append(lax.ppermute(blocks[d], "fsdp", perm))
    mine = join_columns(arrived)

    column = list(ring(mine, "y"))
    column += [other_core(b) for b in column]
    decoded = settle(order, column)
    return (new_params, new_one, new_two, decoded)


def solution(mesh):
    return jax.shard_map(
        body,
        mesh=mesh,
        in_specs=(
            P("head", "fsdp", None),
            P("fsdp", "head"),
            P("fsdp", "head"),
            P("fsdp", "head"),
            P(None, "fsdp", None),
            P(None, "head"),
            P(None, "head"),
            P("head", "fsdp"),
            P("fsdp", None, None),
            P("fsdp", None, None),
            P(None, "fsdp", None),
            P(None, "fsdp", None),
            P("fsdp"),
        ),
        out_specs=(P("fsdp", "head"), P("fsdp", "head"), P("fsdp", "head"), P(None, "fsdp", None)),
        check_vma=False,
    )
```
